32 devices in a mesh: wave: 4 (over y, core), tx: 2 (over x), ty: 4 (over z).
Axes of the slice: x: 2, y: 2, z: 4, core: 2. Of those that a mesh axis runs over, the one named last changes fastest.
Arguments:
- initial_fields: float32 [4, 2, 12, 32, 2048], P('wave', None, None, 'tx', 'ty'), may hold values from -6 to 6
- source_profiles: float32 [4, 2, 3, 2048], P('wave'), may hold values from -6 to 6
- source_waveforms: float32 [4, 2, 5], P('wave'), may hold values from -3 to 3
- material_map: int32 [32, 2048], P('tx', 'ty'), may hold values from 0 to 2
- design_density: float32 [32, 2048], P('tx', 'ty'), may hold values from 0 to 1
- material_table: float32 [3, 4], replicated, may hold values from 0.02 to 12, as said below
- plane_indices: int32 [2], replicated, may hold values from 0 to 31
- design_box: int32 [6], replicated, may hold values from 0 to 64, as said below
Outputs:
- density_gradient: float32 [32, 2048], P('tx', 'ty')
- final_electric: float32 [4, 2, 3, 32, 2048], P('wave', None, None, 'tx', 'ty')
The draws below stay inside these ranges and needn't reach their ends.
Inputs may be any that keep to these rules, and one draw needn't show every extreme that they name: `material_map`: material ids are below 3. `material_table`: column 0 lies in [1, 12], column 1 in [0.5, 3], column 2 in [0.3, 1.5], column 3 in [0.02, 0.5]. `plane_indices`: entry 0 is the source plane of the forward run, entry 1 the monitor plane where the adjoint run's source enters. `design_box`: x0 <= 4, y0 <= 4, x1 = 32, y1 = 32, z0 = 0, z1 = 64.
All inputs are finite; a program needn't handle non-finite values.
Results may differ from the reference program's by a relative error of at most 0.0001.
Values sent between devices are 32-bit elements; how exact they have to be, the bound alone decides.
No kernel may reach another device: no remote copies, remote signals or barrier semaphores. Data moves between devices by JAX's collectives and lax.ppermute only.
A program may use at most 64 MiB of HBM per device.

```python
import math
import jax
import jax.numpy as jnp
from jax import lax

NZ = 64
STEPS = 5
NMAT = 3
WAVES = 4
NX = 32
NY = 32


def draw_material_table(key, part):
    keys = jax.random.split(key, 4)
    eps_column = jnp.exp(jax.random.uniform(keys[0], (NMAT,), jnp.float32, 0.0, math.log(12.0)))
    spread_column = jax.random.uniform(keys[1], (NMAT,), jnp.float32, 0.5, 3.0)
    omega_column = jax.random.uniform(keys[2], (NMAT,), jnp.float32, 0.3, 1.5)
    damping_column = jnp.exp(jax.random.uniform(keys[3], (NMAT,), jnp.float32, math.log(0.02), math.log(0.5)))
    return jnp.stack([eps_column, spread_column, omega_column, damping_column], axis=1).astype(jnp.float32)


def draw_design_box(key, part):
    keys = jax.random.split(key, 2)
    rows_low = jax.random.randint(keys[0], (), 0, NX // 8 + 1)
    lines_low = jax.random.randint(keys[1], (), 0, NY // 8 + 1)
    rows_high = jnp.array(NX, jnp.int32)
    lines_high = jnp.array(NY, jnp.int32)
    depth_low = jnp.array(0, jnp.int32)
    depth_high = jnp.array(NZ, jnp.int32)
    return jnp.stack([rows_low, rows_high, lines_low, lines_high, depth_low, depth_high]).astype(jnp.int32)


def plant(values, stream_key, smallest, high):
    place = [jax.random.randint(jax.random.fold_in(stream_key, axis), (), 0, length) for axis, length in enumerate(values.shape)]
    longest = values.shape.index(max(values.shape))
    next_to = place[:longest] + [(place[longest] + 1) % values.shape[longest]] + place[longest + 1:]
    return values.at[tuple(place)].set(smallest).at[tuple(next_to)].set(high)


def block_scale(own_key, extent, shards, smallest, high):
    level, own = 1.0, jax.random.fold_in(own_key, 6)
    for dim, blocks in shards:
        heights = jnp.exp(jax.random.uniform(jax.random.fold_in(own, dim), (blocks,), jnp.float32, smallest / len(shards), high / len(shards)))
        level = level * jnp.repeat(heights, extent[dim] // blocks).reshape([-1 if axis == dim else 1 for axis in range(len(extent))])
    return level


def gaussian(key, dims, deviation, reach, shards=(), held_as=jnp.bfloat16):
    values = deviation * jax.random.normal(key, dims, jnp.float32)
    if shards:
        values = values * block_scale(key, dims, shards, -0.22, 0.18)
    return jnp.clip(values, -reach, reach).astype(held_as)


def setup_inputs(seed: int = 0) -> dict:
    seeds = jax.random.split(jax.random.key(seed), 9)
    initial_fields = gaussian(seeds[0], (WAVES, 2, 12, NX, NY * NZ), 1.0, 6.0, ((0, 4), (3, 2), (4, 4)), jnp.float32)
    source_profiles = gaussian(seeds[1], (WAVES, 2, 3, NY * NZ), 1.0, 6.0, ((0, 4),), jnp.float32)
    source_waveforms = gaussian(seeds[2], (WAVES, 2, STEPS), 1.0, 3.0, ((0, 4),), jnp.float32)
    material_map = plant(jax.random.randint(seeds[3], (NX, NY * NZ), 0, NMAT), jax.random.fold_in(seeds[3], 1), 0, NMAT - 1).astype(jnp.int32)
    design_density = jnp.clip(1.0 * jax.random.uniform(seeds[4], (NX, NY * NZ), jnp.float32) ** block_scale(seeds[4], (NX, NY * NZ), ((0, 2), (1, 4)), -0.2, 0.2), 0.0, 1.0)
    material_table = draw_material_table(jax.random.fold_in(seeds[8], 71), 0)
    plane_indices = jax.random.randint(seeds[6], (2,), 0, NX).astype(jnp.int32)
    design_box = draw_design_box(jax.random.fold_in(seeds[8], 71), 0)
    return {"initial_fields": initial_fields, "source_profiles": source_profiles, "source_waveforms": source_waveforms, "material_map": material_map, "design_density": design_density, "material_table": material_table, "plane_indices": plane_indices, "design_box": design_box}


time_step = 0.5
contrast = 2.0


def ahead_rows(values, border):
    return jnp.concatenate([values[:, 1:], border], axis=1)


def behind_rows(values, border):
    return jnp.concatenate([border, values[:, :-1]], axis=1)


def ahead_lines(values, border):
    width = border.shape[2]
    return jnp.concatenate([values[:, :, width:], border], axis=2)


def behind_lines(values, border):
    width = border.shape[2]
    return jnp.concatenate([border, values[:, :, :-width]], axis=2)


def ahead_depth(values, depth_last):
    shifted = jnp.concatenate([values[:, :, 1:], jnp.zeros_like(values[:, :, :1])], axis=2)
    return jnp.where(depth_last, 0.0, shifted)


def behind_depth(values, depth_first):
    shifted = jnp.concatenate([jnp.zeros_like(values[:, :, :1]), values[:, :, :-1]], axis=2)
    return jnp.where(depth_first, 0.0, shifted)


def curl_electric(field, rows_ahead, lines_ahead, depth_last):
    part_one, part_two, part_three = field[:, 0], field[:, 1], field[:, 2]
    curl_one = (ahead_lines(part_three, lines_ahead[:, 1]) - part_three) - (ahead_depth(part_two, depth_last) - part_two)
    curl_two = (ahead_depth(part_one, depth_last) - part_one) - (ahead_rows(part_three, rows_ahead[:, 1]) - part_three)
    curl_three = (ahead_rows(part_two, rows_ahead[:, 0]) - part_two) - (ahead_lines(part_one, lines_ahead[:, 0]) - part_one)
    return jnp.stack([curl_one, curl_two, curl_three], axis=1)


def curl_magnetic(field, rows_behind, lines_behind, depth_first):
    part_one, part_two, part_three = field[:, 0], field[:, 1], field[:, 2]
    curl_one = (part_three - behind_lines(part_three, lines_behind[:, 1])) - (part_two - behind_depth(part_two, depth_first))
    curl_two = (part_one - behind_depth(part_one, depth_first)) - (part_three - behind_rows(part_three, rows_behind[:, 1]))
    curl_three = (part_two - behind_rows(part_two, rows_behind[:, 0])) - (part_one - behind_lines(part_one, lines_behind[:, 0]))
    return jnp.stack([curl_one, curl_two, curl_three], axis=1)


def zero_borders(field):
    return (jnp.zeros((field.shape[0], 2, 1, field.shape[3]), field.dtype),
            jnp.zeros((field.shape[0], 2, field.shape[2], NZ), field.dtype))


def design_mask(grid_rows, grid_flat, design_box):
    lines = grid_flat // NZ
    depth_ids = grid_flat % NZ
    in_rows = (grid_rows >= design_box[0]) & (grid_rows < design_box[1])
    in_lines = (lines >= design_box[2]) & (lines < design_box[3]) & (depth_ids >= design_box[4]) & (depth_ids < design_box[5])
    return (in_rows[:, None] & in_lines[None, :]).astype(jnp.float32)


def coefficients(material_map, design_density, material_table, inside_design):
    damping = material_table[:, 3]
    denom = 1.0 + 0.25 * damping
    decay = (1.0 - 0.25 * damping) / denom
    drive = material_table[:, 2] * material_table[:, 2] * time_step / denom
    coupled = drive * material_table[:, 1]
    permittivity = jnp.zeros(material_map.shape, jnp.float32)
    decay_map = jnp.zeros(material_map.shape, jnp.float32)
    drive_map = jnp.zeros(material_map.shape, jnp.float32)
    coupled_map = jnp.zeros(material_map.shape, jnp.float32)
    for material_id in range(NMAT):
        chosen = (material_map == material_id).astype(jnp.float32)
        permittivity = permittivity + chosen * material_table[material_id, 0]
        decay_map = decay_map + chosen * decay[material_id]
        drive_map = drive_map + chosen * drive[material_id]
        coupled_map = coupled_map + chosen * coupled[material_id]
    permittivity = permittivity + (inside_design * design_density) * contrast
    return jnp.stack([time_step / permittivity, decay_map, drive_map, coupled_map])


def advance(electric, magnetic, polarization, current, coeffs, inside, depth_last, depth_first, source, electric_borders, magnetic_borders):
    rows_ahead, lines_ahead = electric_borders(electric)
    magnetic = (magnetic - time_step * curl_electric(electric, rows_ahead, lines_ahead, depth_last)) * inside
    current = coeffs[1] * current + coeffs[3] * electric - coeffs[2] * polarization
    polarization = polarization + time_step * current
    rows_behind, lines_behind = magnetic_borders(magnetic)
    electric = electric + coeffs[0] * ((curl_magnetic(magnetic, rows_behind, lines_behind, depth_first) - current) - source)
    return electric, magnetic, polarization, current


def reference(initial_fields, source_profiles, source_waveforms, material_map, design_density, material_table, plane_indices, design_box):
    grid_rows = jnp.arange(NX, dtype=jnp.int32)
    grid_flat = jnp.arange(NY * NZ, dtype=jnp.int32)
    inside_design = design_mask(grid_rows, grid_flat, design_box)
    coeffs = coefficients(material_map, design_density, material_table, inside_design)
    depth_ids = grid_flat % NZ
    depth_last = depth_ids == NZ - 1
    depth_first = depth_ids == 0
    plane_rows = (grid_rows[None, :] == plane_indices[:, None]).astype(jnp.float32)

    def one_channel(inputs):
        fields, profiles, waveforms = inputs
        electric = fields[:, 0:3]
        magnetic = fields[:, 3:6]
        polarization = fields[:, 6:9]
        current = fields[:, 9:12]
        forward_history = [electric[0]]
        adjoint_history = [electric[1]]
        for step_index in range(STEPS):
            source = waveforms[:, step_index][:, None, None, None] * profiles[:, :, None, :] * plane_rows[:, None, :, None]
            electric, magnetic, polarization, current = advance(electric, magnetic, polarization, current, coeffs, 1.0, depth_last, depth_first, source, zero_borders, zero_borders)
            forward_history.append(electric[0])
            adjoint_history.append(electric[1])
        partial_value = jnp.zeros((NX, NY * NZ), jnp.float32)
        for pair_index in range(1, STEPS + 1):
            partial_value = partial_value + jnp.sum(adjoint_history[STEPS + 1 - pair_index] * (forward_history[pair_index] - forward_history[pair_index - 1]), axis=0)
        return electric, partial_value

    finals, partials = lax.map(one_channel, (initial_fields, source_profiles, source_waveforms))
    density_gradient = contrast * inside_design * jnp.sum(partials, axis=0)
    return density_gradient, finals
```

```python
import functools

import jax
import jax.numpy as jnp
from jax import lax
from jax.experimental import pallas as pl
from jax.experimental.pallas import tpu as pltpu
from jax.sharding import PartitionSpec as P

NZ = 64
STEPS = 5
NMAT = 3
LANES = 2 * NZ
ROWS = 16
LINES = 8
PAD = 8
EXT_ROWS = ROWS + 2 * PAD
EXT_LINES = LINES + 2 * STEPS
FIELDS = 13

time_step = 0.5
contrast = 2.0

LINE_DEPTH = (5, 5, 5, 5, 4, 5, 3, 3, 3, 4, 4, 4, 4)
ROW_DEPTH = (5, 5, 5, 4, 5, 5, 3, 3, 3, 4, 4, 4, 4)

Y_ENTRIES = [(f, k) for f in range(FIELDS) for k in range(LINE_DEPTH[f])]


def x_entries():
    start, out = 0, []
    for f in range(FIELDS):
        for line in range(LINES):
            out.append((f, line, ROW_DEPTH[f], start))
            start += ROW_DEPTH[f]
    return out, start


def corner_entries():
    start, out = 0, []
    for f in range(FIELDS):
        for k in range(LINE_DEPTH[f]):
            out.append((f, k, ROW_DEPTH[f], start))
            start += ROW_DEPTH[f]
    return out, start


X_ENTRIES, X_ROWS = x_entries()
C_ENTRIES, C_ROWS = corner_entries()


def round_up(n, m):
    return (n + m - 1) // m * m


def low_lanes(shape):
    return lax.broadcasted_iota(jnp.int32, shape, len(shape) - 1) < NZ


def half_turn(v):
    return pltpu.roll(v, NZ, v.ndim - 1)


def choose(material, table, column):
    values = [column(m) for m in range(NMAT)]
    return jnp.where(material < 0.5, values[0], jnp.where(material < 1.5, values[1], values[2]))


def pole(table):
    def denom(m):
        return 1.0 + 0.25 * table[m, 3]

    def decay(m):
        return (1.0 - 0.25 * table[m, 3]) / denom(m)

    def drive(m):
        return table[m, 2] * table[m, 2] * time_step / denom(m)

    def coupled(m):
        return drive(m) * table[m, 1]

    return decay, drive, coupled


def pack_kernel(parity, table, fields, material, density, tile, y_a, y_b, *rest):
    x_msgs, corner_msgs = rest
    decay, drive, coupled = pole(table)
    low = low_lanes((ROWS, LANES))
    for k in range(LINES // 2):
        at = slice(k * LANES, (k + 1) * LANES)

        def split(one, two):
            return jnp.where(low, one, half_turn(two)), jnp.where(low, half_turn(one), two)

        pairs = [split(fields[0, 0, f, :, at], fields[0, 1, f, :, at]) for f in range(12)]
        mat, dens = material[:, at].astype(jnp.float32), density[:, at]
        turned = half_turn(mat)
        mats = (jnp.where(low, mat, turned), jnp.where(low, turned, mat))
        mixed = split(mat, dens)
        for half in range(2):
            line = 2 * k + half
            dec = choose(mats[half], table, decay)
            dri = choose(mats[half], table, drive)
            cou = choose(mats[half], table, coupled)
            for c in range(3):
                e, p, j = pairs[c][half], pairs[6 + c][half], pairs[9 + c][half]
                j = dec * j + cou * e - dri * p
                tile[c, line] = e
                tile[3 + c, line] = pairs[3 + c][half]
                tile[6 + c, line] = p + time_step * j
                tile[9 + c, line] = j
            tile[12, line] = mixed[half]
    odd_x, odd_y = parity[0], parity[1]
    for i, (f, k) in enumerate(Y_ENTRIES):
        first, last = k, LINES - 1 - k
        y_a[i] = tile[f, jnp.where(odd_y == 1, first, last)]
        y_b[i] = tile[f, jnp.where(odd_y == 1, last, first)]

    def pack_rows(msg, entries, rows_first, line_of):
        for f, k, depth, start in entries:
            line = line_of(k)
            if rows_first:
                msg[start : start + depth, :] = tile[f, line, 0:depth, :]
            else:
                msg[start : start + depth, :] = tile[f, line, ROWS - depth : ROWS, :]

    for x_type in range(len(x_msgs)):
        for first in (False, True):
            sends_last_if = x_type if not first else 1 - x_type

            @pl.when(odd_x == sends_last_if)
            def _(x_type=x_type, first=first):
                pack_rows(x_msgs[x_type], X_ENTRIES, first, lambda k: k)
                for y_type in range(2):
                    pack_rows(
                        corner_msgs[x_type][y_type],
                        C_ENTRIES,
                        first,
                        lambda k, y_type=y_type: jnp.where(odd_y == 1 - y_type, k, LINES - 1 - k),
                    )


def main_kernel(
    place,
    waveforms,
    table,
    plane,
    box,
    profiles,
    tile,
    y_a,
    y_b,
    x_msgs,
    corner_msgs,
    electric_out,
    gradient_out,
    E,
    H,
    Pol,
    J,
    C,
    coef,
):
    odd_x, odd_y = place[0] % 2, place[1] % 2
    rows_base, lines_base = place[0] * ROWS - PAD, place[1] * LINES - STEPS
    rows_all, lines_all = place[2], place[3]

    def put(f, line, rows, value):
        c = f % 3
        if f < 3:
            E[0, c, line, rows, :] = value
        elif f < 6:
            H[c, line, rows, :] = value
        elif f < 9:
            Pol[c, line, rows, :] = value
        elif f < 12:
            J[c, line, rows, :] = value
        else:
            C[line, rows, :] = value

    E[0] = jnp.zeros(E.shape[1:], jnp.float32)
    H[...] = jnp.zeros(H.shape, jnp.float32)
    Pol[...] = jnp.zeros(Pol.shape, jnp.float32)
    J[...] = jnp.zeros(J.shape, jnp.float32)
    C[...] = jnp.zeros(C.shape, jnp.float32)
    middle = slice(PAD, PAD + ROWS)
    for f in range(FIELDS):
        for line in range(LINES):
            put(f, STEPS + line, middle, tile[f, line])

    def line_at(ahead, k):
        return jnp.where(ahead, STEPS + LINES + k, STEPS - 1 - k)

    for i, (f, k) in enumerate(Y_ENTRIES):
        put(f, line_at(odd_y == 0, k), middle, y_a[i])
        put(f, line_at(odd_y == 1, k), middle, y_b[i])
    for x_type in range(len(x_msgs)):
        for ahead in (False, True):
            want = x_type if ahead else 1 - x_type

            @pl.when(odd_x == want)
            def _(x_type=x_type, ahead=ahead):
                def rows_of(depth):
                    return slice(PAD + ROWS, PAD + ROWS + depth) if ahead else slice(PAD - depth, PAD)

                for f, line, depth, start in X_ENTRIES:
                    put(f, STEPS + line, rows_of(depth), x_msgs[x_type][start : start + depth, :])
                for y_type in range(2):
                    for f, k, depth, start in C_ENTRIES:
                        put(
                            f,
                            line_at(odd_y == y_type, k),
                            rows_of(depth),
                            corner_msgs[x_type][y_type][start : start + depth, :],
                        )

    decay, drive, coupled = pole(table)
    shape = (EXT_ROWS, LANES)
    low = low_lanes(shape)
    lane = lax.broadcasted_iota(jnp.int32, shape, 1)
    depth_id = jnp.where(low, lane, lane - NZ)
    row = lax.broadcasted_iota(jnp.int32, shape, 0) + rows_base
    first_z, last_z = depth_id == 0, depth_id == NZ - 1
    row_inside = (row >= 0) & (row < rows_all)
    row_mask = row_inside.astype(jnp.float32)
    design_rows = (
        (row >= box[0]) & (row < box[1]) & (depth_id >= box[4]) & (depth_id < box[5])
    ).astype(jnp.float32)
    source_rows = (row == jnp.where(low, plane[0], plane[1])).astype(jnp.float32)

    def line_flags(line):
        where = lines_base + line
        grid = ((where >= 0) & (where < lines_all)).astype(jnp.float32)
        design = ((where >= box[2]) & (where < box[3])).astype(jnp.float32)
        return grid, design

    def set_coefficients(line, _):
        mixed = C[line]
        turned = half_turn(mixed)
        mat = jnp.where(low, mixed, turned)
        dens = jnp.where(low, turned, mixed)
        grid, design = line_flags(line)
        permittivity = choose(mat, table, lambda m: table[m, 0]) + (design_rows * design) * dens * contrast
        coef[0, line] = time_step / permittivity * (row_mask * grid)
        coef[1, line] = choose(mat, table, decay)
        coef[2, line] = choose(mat, table, drive)
        coef[3, line] = choose(mat, table, coupled)
        return _

    lax.fori_loop(1, EXT_LINES - 1, set_coefficients, 0)

    def ahead_row(v):
        return pltpu.roll(v, EXT_ROWS - 1, 0)

    def behind_row(v):
        return pltpu.roll(v, 1, 0)

    def ahead_depth(v):
        return jnp.where(last_z, 0.0, pltpu.roll(v, LANES - 1, 1))

    def behind_depth(v):
        return jnp.where(first_z, 0.0, pltpu.roll(v, 1, 1))

    def magnetic_line(n, line):
        ex, ey, ez = E[n, 0, line], E[n, 1, line], E[n, 2, line]
        ex_next, ez_next = E[n, 0, line + 1], E[n, 2, line + 1]
        half = time_step * (row_mask * line_flags(line)[0])
        hx = H[0, line] - half * ((ez_next - ez) - (ahead_depth(ey) - ey))
        hy = H[1, line] - half * ((ahead_depth(ex) - ex) - (ahead_row(ez) - ez))
        hz = H[2, line] - half * ((ahead_row(ey) - ey) - (ex_next - ex))
        H[0, line], H[1, line], H[2, line] = hx, hy, hz
        return (hx, hy, hz), (ex, ey, ez)

    for n in range(STEPS):
        magnetic_line(n, n)
        weight = [jnp.where(low[:1], waveforms[0, n], waveforms[1, n])]

        def advance(line, _, n=n, weight=weight[0]):
            (hx, hy, hz), e = magnetic_line(n, line)
            hx_last, hz_last = H[0, line - 1], H[2, line - 1]
            curls = (
                (hz - hz_last) - (hy - behind_depth(hy)),
                (hx - behind_depth(hx)) - (hz - behind_row(hz)),
                (hy - behind_row(hy)) - (hx - hx_last),
            )
            reach = coef[0, line]
            where = jnp.clip(lines_base + line, 0, lines_all - 1)
            for c in range(3):
                if n == 0:
                    j = J[c, line]
                else:
                    p = Pol[c, line]
                    j = coef[1, line] * J[c, line] + coef[3, line] * e[c] - coef[2, line] * p
                    if n < STEPS - 1:
                        J[c, line] = j
                        Pol[c, line] = p + time_step * j
                source = source_rows * (weight * profiles[c, pl.ds(where, 1), :])
                E[n + 1, c, line] = e[c] + reach * ((curls[c] - j) - source)
            return _

        lax.fori_loop(n + 1, EXT_LINES - 1 - n, advance, 0)

    for k in range(LINES // 2):
        at = slice(k * LANES, (k + 1) * LANES)
        low16 = low[:ROWS]
        sums = []
        for half in range(2):
            line = STEPS + 2 * k + half
            total = jnp.zeros((ROWS, LANES), jnp.float32)
            for c in range(3):
                history = [E[n, c, line, middle, :] for n in range(STEPS + 1)]
                for n in range(1, STEPS + 1):
                    total = total + half_turn(history[STEPS + 1 - n]) * (history[n] - history[n - 1])
            design = line_flags(line)[1]
            sums.append(total * (contrast * design_rows[PAD : PAD + ROWS] * design))
        gradient_out[:, at] = jnp.where(low16, sums[0], half_turn(sums[1]))
        for c in range(3):
            one = E[STEPS, c, STEPS + 2 * k, middle, :]
            two = E[STEPS, c, STEPS + 2 * k + 1, middle, :]
            electric_out[0, 0, c, :, at] = jnp.where(low16, one, half_turn(two))
            electric_out[0, 1, c, :, at] = jnp.where(low16, half_turn(one), two)


def pair_of(index, kind, count):
    if kind is None:
        return index
    other = index + 1 if index % 2 == kind else index - 1
    return other if 0 <= other < count else None


def on_device(counts, initial_fields, source_profiles, source_waveforms, material_map, design_density, material_table, plane_indices, design_box):
    tx_count, ty_count = counts
    axes = ("tx", "ty")

    def swap(value, x_kind, y_kind):
        pairs = []
        for x in range(tx_count):
            for y in range(ty_count):
                ox, oy = pair_of(x, x_kind, tx_count), pair_of(y, y_kind, ty_count)
                if ox is not None and oy is not None:
                    pairs.append((x * ty_count + y, ox * ty_count + oy))
        return lax.ppermute(value, axes, pairs)

    x_kinds = (0, 1) if tx_count > 2 else (0,)
    tile_x, tile_y = lax.axis_index("tx"), lax.axis_index("ty")
    parity = jnp.stack([tile_x % 2, tile_y % 2]).astype(jnp.int32)
    place = jnp.stack([tile_x, tile_y, tile_x * 0 + tx_count * ROWS, tile_x * 0 + ty_count * LINES]).astype(jnp.int32)
    smem = pl.BlockSpec(memory_space=pltpu.SMEM)
    vmem = pl.BlockSpec(memory_space=pltpu.VMEM)

    def f32(*shape):
        return jax.ShapeDtypeStruct(shape, jnp.float32)

    x_size, c_size = round_up(X_ROWS, 8), round_up(C_ROWS, 8)
    tile, y_a, y_b, x_msgs, corner_msgs = pl.pallas_call(
        pack_kernel,
        out_shape=(
            f32(FIELDS, LINES, ROWS, LANES),
            f32(len(Y_ENTRIES), ROWS, LANES),
            f32(len(Y_ENTRIES), ROWS, LANES),
            [f32(x_size, LANES) for _ in x_kinds],
            [[f32(c_size, LANES) for _ in range(2)] for _ in x_kinds],
        ),
        in_specs=[smem, smem, vmem, vmem, vmem],
        out_specs=(
            vmem,
            vmem,
            vmem,
            [vmem for _ in x_kinds],
            [[vmem for _ in range(2)] for _ in x_kinds],
        ),
        compiler_params=pltpu.CompilerParams(vmem_limit_bytes=32 * 1024 * 1024),
        name="pack",
    )(parity, material_table, initial_fields, material_map, design_density)
    y_a, y_b = swap(y_a, None, 0), swap(y_b, None, 1)
    x_msgs = [swap(m, kind, None) for m, kind in zip(x_msgs, x_kinds)]
    corner_msgs = [[swap(m[y_kind], kind, y_kind) for y_kind in range(2)] for m, kind in zip(corner_msgs, x_kinds)]

    lines_all = ty_count * LINES
    profiles = source_profiles[0].reshape(2, 3, lines_all, NZ).transpose(1, 2, 0, 3).reshape(3, lines_all, LANES)
    ext = (EXT_LINES, EXT_ROWS, LANES)
    electric, partial = pl.pallas_call(
        main_kernel,
        out_shape=(f32(1, 2, 3, ROWS, LINES * NZ), f32(ROWS, LINES * NZ)),
        in_specs=[smem] * 5
        + [vmem] * 4
        + [[vmem for _ in x_kinds], [[vmem for _ in range(2)] for _ in x_kinds]],
        out_specs=(vmem, vmem),
        scratch_shapes=[
            pltpu.VMEM((STEPS + 1, 3) + ext, jnp.float32),
            pltpu.VMEM((3,) + ext, jnp.float32),
            pltpu.VMEM((3,) + ext, jnp.float32),
            pltpu.VMEM((3,) + ext, jnp.float32),
            pltpu.VMEM(ext, jnp.float32),
            pltpu.VMEM((4,) + ext, jnp.float32),
        ],
        compiler_params=pltpu.CompilerParams(vmem_limit_bytes=48 * 1024 * 1024),
        name="window",
    )(place, source_waveforms[0], material_table, plane_indices, design_box, profiles, tile, y_a, y_b, x_msgs, corner_msgs)

    wave_count = lax.axis_size("wave")
    if wave_count == 4:
        one, two, three = [
            lax.ppermute(partial, "wave", [(i, i ^ k) for i in range(4)]) for k in (1, 2, 3)
        ]
        gradient = (partial + one) + (two + three)
    else:
        gradient = lax.psum(partial, "wave")
    return gradient, electric


def solution(mesh):
    placed = (
        P("wave", None, None, "tx", "ty"),
        P("wave", None, None, None),
        P("wave", None, None),
        P("tx", "ty"),
        P("tx", "ty"),
        P(),
        P(),
        P(),
    )
    return jax.shard_map(
        functools.partial(on_device, (mesh.shape["tx"], mesh.shape["ty"])),
        mesh=mesh,
        in_specs=placed,
        out_specs=(P("tx", "ty"), P("wave", None, None, "tx", "ty")),
        check_vma=False,
    )
```

```python
import functools

import jax
import jax.numpy as jnp
from jax import lax
from jax.experimental import pallas as pl
from jax.experimental.pallas import tpu as pltpu
from jax.sharding import PartitionSpec as P

NZ = 64
STEPS = 5
NMAT = 3
LANES = 2 * NZ
ROWS = 16
LINES = 8
CHUNKS = LINES // 2
PAD = 8
EXT_LINES = LINES + 2 * STEPS
FIELDS = 13

time_step = 0.5
contrast = 2.0

LINE_DEPTH = (5, 5, 5, 5, 4, 5, 3, 3, 3, 4, 4, 4, 4)
ROW_DEPTH = (5, 5, 5, 4, 5, 5, 3, 3, 3, 4, 4, 4, 4)
SAME_DEPTH = (4, 4, 4, 4, 4, 4, 2, 2, 2, 3, 3, 3, 3)
MIXED_DEPTH = (5, 5, 4, 4, 4, 4, 3, 3, 2, 4, 4, 3, 4)

Y_ENTRIES = [(f, k) for f in range(FIELDS) for k in range(LINE_DEPTH[f])]


def listed(entries):
    start, out = 0, []
    for f, k, depth in entries:
        out.append((f, k, depth, start))
        start += depth
    return out, (start + 7) // 8 * 8


X_ENTRIES, X_ROWS = listed([(f, line, ROW_DEPTH[f]) for f in range(FIELDS) for line in range(LINES)])
CORNERS = [
    listed([(f, k, depth[f] - k) for f in range(FIELDS) for k in range(depth[f])])
    for depth in (SAME_DEPTH, MIXED_DEPTH)
]


def low_lanes(shape):
    return lax.broadcasted_iota(jnp.int32, shape, len(shape) - 1) < NZ


def half_turn(v):
    return pltpu.roll(v, NZ, v.ndim - 1)


def choose(material, column):
    values = [column(m) for m in range(NMAT)]
    return jnp.where(material < 0.5, values[0], jnp.where(material < 1.5, values[1], values[2]))


def pole(table):
    out = []
    for m in range(NMAT):
        d, w, g = table[m, 1], table[m, 2], table[m, 3]
        denom = 1.0 + 0.25 * g
        drive = w * w * time_step / denom
        out.append(((1.0 - 0.25 * g) / denom, drive, drive * d))
    return [lambda m, i=i: out[m][i] for i in range(3)]


def pack_kernel(table_hbm, fields_hbm, material_hbm, density_hbm, tile, y_a, y_b, table, fields, material, density, sems):
    copies = [
        pltpu.make_async_copy(table_hbm, table, sems.at[CHUNKS]),
        pltpu.make_async_copy(material_hbm, material, sems.at[CHUNKS + 1]),
        pltpu.make_async_copy(density_hbm, density, sems.at[CHUNKS + 2]),
    ]
    chunks = [
        pltpu.make_async_copy(
            fields_hbm.at[0, :, :, :, pl.ds(k * LANES, LANES)], fields.at[k], sems.at[k]
        )
        for k in range(CHUNKS)
    ]
    for copy in copies + chunks:
        copy.start()
    for copy in copies:
        copy.wait()
    decay, drive, coupled = pole(table)
    low = low_lanes((ROWS, LANES))
    for k in range(CHUNKS):
        at = slice(k * LANES, (k + 1) * LANES)
        chunks[k].wait()

        def split(one, two):
            return jnp.where(low, one, half_turn(two)), jnp.where(low, half_turn(one), two)

        pairs = [split(fields[k, 0, f], fields[k, 1, f]) for f in range(12)]
        mat, dens = material[:, at].astype(jnp.float32), density[:, at]
        turned = half_turn(mat)
        mats = (jnp.where(low, mat, turned), jnp.where(low, turned, mat))
        mixed = split(mat, dens)
        for half in range(2):
            line = 2 * k + half
            dec, dri, cou = [choose(mats[half], column) for column in (decay, drive, coupled)]
            for c in range(3):
                e, p, j = pairs[c][half], pairs[6 + c][half], pairs[9 + c][half]
                j = dec * j + cou * e - dri * p
                tile[c, line] = e
                tile[3 + c, line] = pairs[3 + c][half]
                tile[6 + c, line] = p + time_step * j
                tile[9 + c, line] = j
            tile[12, line] = mixed[half]
    odd = lax.rem(lax.axis_index("ty"), 2) == 1
    for i, (f, k) in enumerate(Y_ENTRIES):
        first, last = k, LINES - 1 - k
        y_a[i] = tile[f, jnp.where(odd, first, last)]
        y_b[i] = tile[f, jnp.where(odd, last, first)]


def edge_kernel(tile, *messages):
    odd = lax.rem(lax.axis_index("tx"), 2)
    for kind in range(len(messages) // 3):
        along, same, mixed = messages[3 * kind : 3 * kind + 3]
        for is_lower in (True, False):

            @pl.when((odd == kind) == is_lower)
            def _(is_lower=is_lower, along=along, same=same, mixed=mixed):
                def pack(message, entries, line_of):
                    for f, k, depth, start in entries:
                        rows = slice(ROWS - depth, ROWS) if is_lower else slice(0, depth)
                        message[start : start + depth, :] = tile[f, line_of(k), rows, :]

                pack(along, X_ENTRIES, lambda k: k)
                pack(same, CORNERS[0][0], lambda k: LINES - 1 - k if is_lower else k)
                pack(mixed, CORNERS[1][0], lambda k: k if is_lower else LINES - 1 - k)


def window_kernel(
    tx_count,
    ty_count,
    waveforms_hbm,
    table_hbm,
    plane_hbm,
    box_hbm,
    profiles,
    tile,
    y_a,
    y_b,
    *rest,
):
    kinds = 1 if tx_count == 2 else 2
    messages, rest = rest[: 3 * kinds], rest[3 * kinds :]
    electric_out, gradient_out, E, H, Pol, J, C, coef, source, waveforms, table, plane, box, sems = rest
    wide = tx_count != 2
    ext_rows = E[0].shape[2]
    copies = [
        pltpu.make_async_copy(src, dst, sems.at[i])
        for i, (src, dst) in enumerate(
            [(waveforms_hbm, waveforms), (table_hbm, table), (plane_hbm, plane), (box_hbm, box)]
        )
    ]
    for copy in copies:
        copy.start()
    tx, ty = lax.axis_index("tx"), lax.axis_index("ty")
    odd_x, odd_y = lax.rem(tx, 2), lax.rem(ty, 2)
    offset = PAD if wide else pl.multiple_of(tx * PAD, PAD)
    rows_base, lines_base = tx * ROWS - offset, ty * LINES - STEPS
    rows_all, lines_all = tx_count * ROWS, ty_count * LINES
    middle = pl.ds(offset, ROWS)

    def put(f, line, rows, value):
        if f < 12:
            (E[0], H[0], Pol[0], J[0])[f // 3][f % 3, line, rows, :] = value
        else:
            C[line, rows, :] = value

    for ref in (E[0], H[0], Pol[0], J[0], C):
        ref[...] = jnp.zeros(ref.shape, jnp.float32)
    for f in range(FIELDS):
        for line in range(LINES):
            put(f, STEPS + line, middle, tile[f, line])

    def line_at(ahead, k):
        return jnp.where(ahead, STEPS + LINES + k, STEPS - 1 - k)

    for i, (f, k) in enumerate(Y_ENTRIES):
        put(f, line_at(odd_y == 0, k), middle, y_a[i])
        put(f, line_at(odd_y == 1, k), middle, y_b[i])
    for kind in range(kinds):
        along, same, mixed = messages[3 * kind : 3 * kind + 3]
        for is_lower in (True, False):

            @pl.when((odd_x == kind) == is_lower)
            def _(is_lower=is_lower, along=along, same=same, mixed=mixed):
                def unpack(message, entries, line_of):
                    for f, k, depth, start in entries:
                        if wide:
                            first = PAD + ROWS if is_lower else PAD - depth
                        else:
                            first = ROWS if is_lower else PAD - depth
                        put(f, line_of(k), slice(first, first + depth), message[start : start + depth, :])

                unpack(along, X_ENTRIES, lambda k: STEPS + k)
                unpack(same, CORNERS[0][0], lambda k: STEPS + LINES + k if is_lower else STEPS - 1 - k)
                unpack(mixed, CORNERS[1][0], lambda k: STEPS - 1 - k if is_lower else STEPS + LINES + k)
    for copy in copies:
        copy.wait()
    decay, drive, coupled = pole(table)
    shape = (ext_rows, LANES)
    low = low_lanes(shape)
    lane = lax.broadcasted_iota(jnp.int32, shape, 1)
    depth_id = jnp.where(low, lane, lane - NZ)
    row = lax.broadcasted_iota(jnp.int32, shape, 0) + rows_base
    first_z, last_z = depth_id == 0, depth_id == NZ - 1
    row_mask = ((row >= 0) & (row < rows_all)).astype(jnp.float32)
    in_z = (depth_id >= box[4]) & (depth_id < box[5])
    design_rows = ((row >= box[0]) & (row < box[1]) & in_z).astype(jnp.float32)
    source_rows = (row == jnp.where(low, plane[0], plane[1])).astype(jnp.float32)

    def line_design(line):
        where = lines_base + line
        return ((where >= box[2]) & (where < box[3])).astype(jnp.float32)

    def line_inside(line):
        where = lines_base + line
        return ((where >= 0) & (where < lines_all)).astype(jnp.float32)

    def is_own(line):
        return STEPS <= line < STEPS + LINES

    for line in range(1, EXT_LINES - 1):
        mixed = C[line]
        turned = half_turn(mixed)
        mat = jnp.where(low, mixed, turned)
        dens = jnp.where(low, turned, mixed)
        design = design_rows * line_design(line)
        permittivity = choose(mat, lambda m: table[m, 0]) + (design * dens) * contrast
        reach = time_step / permittivity
        if wide:
            reach = reach * row_mask
        if not is_own(line):
            reach = reach * line_inside(line)
        coef[0, line] = reach
        for i, column in enumerate((decay, drive, coupled)):
            coef[1 + i, line] = choose(mat, column)

    low_row = low[:1]
    for i in range(EXT_LINES // 2):
        chunk = jnp.clip(ty * CHUNKS + (i - STEPS // 2 - 1) + 1, 0, ty_count * CHUNKS - 1)
        for c in range(3):
            both = profiles[c, :, pl.ds(pl.multiple_of(chunk * LANES, LANES), LANES)]
            one, two = both[0:1], both[1:2]
            source[c, pl.ds(2 * i + 1, 1), :] = jnp.where(low_row, one, half_turn(two))
            source[c, pl.ds(2 * i + 2, 1), :] = jnp.where(low_row, half_turn(one), two)

    edge = jnp.zeros((1, LANES), jnp.float32)

    def ahead_row(v):
        return jnp.concatenate([v[1:], edge], axis=0)

    def behind_row(v):
        return jnp.concatenate([edge, v[:-1]], axis=0)

    def ahead_depth(v):
        return jnp.where(last_z, 0.0, pltpu.roll(v, LANES - 1, 1))

    def behind_depth(v):
        return jnp.where(first_z, 0.0, pltpu.roll(v, 1, 1))

    def magnetic_line(n, line):
        old, new = H[n % 2], H[(n + 1) % 2]
        ex, ey, ez = E[n][0, line], E[n][1, line], E[n][2, line]
        ex_next, ez_next = E[n][0, line + 1], E[n][2, line + 1]
        half = time_step
        if line < STEPS:
            half = half * line_inside(line)
        if wide:
            half = half * row_mask
        new[0, line] = old[0, line] - half * ((ez_next - ez) - (ahead_depth(ey) - ey))
        new[1, line] = old[1, line] - half * ((ahead_depth(ex) - ex) - (ahead_row(ez) - ez))
        new[2, line] = old[2, line] - half * ((ahead_row(ey) - ey) - (ex_next - ex))

    def electric_line(n, line, weight):
        field = H[(n + 1) % 2]
        hx, hy, hz = field[0, line], field[1, line], field[2, line]
        hx_last, hz_last = field[0, line - 1], field[2, line - 1]
        curls = (
            (hz - hz_last) - (hy - behind_depth(hy)),
            (hx - behind_depth(hx)) - (hz - behind_row(hz)),
            (hy - behind_row(hy)) - (hx - hx_last),
        )
        reach = coef[0, line]
        for c in range(3):
            e = E[n][c, line]
            if n == 0:
                j = J[0][c, line]
            else:
                p = Pol[(n + 1) % 2][c, line]
                j = coef[1, line] * J[(n + 1) % 2][c, line] + coef[3, line] * e - coef[2, line] * p
                if n < STEPS - 1:
                    J[n % 2][c, line] = j
                    Pol[n % 2][c, line] = p + time_step * j
            drawn = source_rows * (weight * source[c, line : line + 1, :])
            E[n + 1][c, line] = e + reach * ((curls[c] - j) - drawn)

    for n in range(STEPS):
        weight = jnp.where(low_row, waveforms[0, n], waveforms[1, n])
        for line in range(n, EXT_LINES - 1 - n):
            magnetic_line(n, line)
        for line in range(n + 1, EXT_LINES - 1 - n):
            electric_line(n, line, weight)

    low_tile = low[:ROWS]
    row_tile = lax.broadcasted_iota(jnp.int32, (ROWS, LANES), 0) + tx * ROWS
    design_tile = (
        (row_tile >= box[0]) & (row_tile < box[1]) & in_z[:ROWS]
    ).astype(jnp.float32) * contrast
    for k in range(CHUNKS):
        sums = []
        for half in range(2):
            line = STEPS + 2 * k + half
            total = jnp.zeros((ROWS, LANES), jnp.float32)
            for c in range(3):
                history = [E[n][c, line, middle, :] for n in range(STEPS + 1)]
                for n in range(1, STEPS + 1):
                    total = total + half_turn(history[STEPS + 1 - n]) * (history[n] - history[n - 1])
                electric_out[c, 2 * k + half] = history[STEPS]
            sums.append(total * (design_tile * line_design(line)))
        gradient_out[:, k * LANES : (k + 1) * LANES] = jnp.where(low_tile, sums[0], half_turn(sums[1]))


def emit_kernel(electric, out):
    low = low_lanes((ROWS, LANES))
    for k in range(CHUNKS):
        at = slice(k * LANES, (k + 1) * LANES)
        for c in range(3):
            one, two = electric[c, 2 * k], electric[c, 2 * k + 1]
            out[0, 0, c, :, at] = jnp.where(low, one, half_turn(two))
            out[0, 1, c, :, at] = jnp.where(low, half_turn(one), two)


def pair_of(index, kind, count):
    other = index + 1 if index % 2 == kind else index - 1
    return other if 0 <= other < count else None


def f32(*shape):
    return jax.ShapeDtypeStruct(shape, jnp.float32)


def in_hbm(value):
    return pltpu.with_memory_space_constraint(value, pltpu.HBM)


def on_device(
    tx_count,
    ty_count,
    initial_fields,
    source_profiles,
    source_waveforms,
    material_map,
    design_density,
    material_table,
    plane_indices,
    design_box,
):
    hbm = pl.BlockSpec(memory_space=pltpu.HBM)
    vmem = pl.BlockSpec(memory_space=pltpu.VMEM)
    kinds = (0,) if tx_count == 2 else (0, 1)

    def swap(value, partner):
        pairs = []
        for x in range(tx_count):
            for y in range(ty_count):
                other = partner(x, y)
                if None not in other and 0 <= other[1] < ty_count:
                    pairs.append((x * ty_count + y, other[0] * ty_count + other[1]))
        return lax.ppermute(value, ("tx", "ty"), pairs)

    def corner(kind, mixed):
        def partner(x, y):
            lower = x % 2 == kind
            return pair_of(x, kind, tx_count), y + (1 if lower != mixed else -1)

        return partner

    tile, y_a, y_b = pl.pallas_call(
        pack_kernel,
        out_shape=(
            f32(FIELDS, LINES, ROWS, LANES),
            f32(len(Y_ENTRIES), ROWS, LANES),
            f32(len(Y_ENTRIES), ROWS, LANES),
        ),
        in_specs=[hbm] * 4,
        out_specs=(vmem, vmem, vmem),
        scratch_shapes=[
            pltpu.SMEM((NMAT, 4), jnp.float32),
            pltpu.VMEM((CHUNKS, 2, 12, ROWS, LANES), jnp.float32),
            pltpu.VMEM((ROWS, LINES * NZ), jnp.int32),
            pltpu.VMEM((ROWS, LINES * NZ), jnp.float32),
            pltpu.SemaphoreType.DMA((CHUNKS + 3,)),
        ],
        compiler_params=pltpu.CompilerParams(vmem_limit_bytes=32 * 1024 * 1024),
        name="pack",
    )(*[in_hbm(v) for v in (material_table, initial_fields, material_map, design_density)])
    y_a = swap(y_a, lambda x, y: (x, pair_of(y, 0, ty_count)))
    y_b = swap(y_b, lambda x, y: (x, pair_of(y, 1, ty_count)))

    sizes = (X_ROWS, CORNERS[0][1], CORNERS[1][1]) * len(kinds)
    messages = pl.pallas_call(
        edge_kernel,
        out_shape=[f32(size, LANES) for size in sizes],
        in_specs=[vmem],
        out_specs=[vmem] * len(sizes),
        compiler_params=pltpu.CompilerParams(vmem_limit_bytes=32 * 1024 * 1024),
        name="edges",
    )(tile)
    arrived = []
    for i, message in enumerate(messages):
        kind = i // 3
        if i % 3 == 0:
            arrived.append(swap(message, lambda x, y, kind=kind: (pair_of(x, kind, tx_count), y)))
        else:
            arrived.append(swap(message, corner(kind, i % 3 == 2)))

    ext = (EXT_LINES, ROWS + (PAD if tx_count == 2 else 2 * PAD), LANES)
    electric, partial = pl.pallas_call(
        functools.partial(window_kernel, tx_count, ty_count),
        out_shape=(f32(3, LINES, ROWS, LANES), f32(ROWS, LINES * NZ)),
        in_specs=[hbm] * 4 + [vmem] * (4 + len(arrived)),
        out_specs=(vmem, vmem),
        scratch_shapes=[
            [pltpu.VMEM((3,) + ext, jnp.float32) for _ in range(STEPS + 1)],
            [pltpu.VMEM((3,) + ext, jnp.float32) for _ in range(2)],
            [pltpu.VMEM((3,) + ext, jnp.float32) for _ in range(2)],
            [pltpu.VMEM((3,) + ext, jnp.float32) for _ in range(2)],
            pltpu.VMEM(ext, jnp.float32),
            pltpu.VMEM((4,) + ext, jnp.float32),
            pltpu.VMEM((3, EXT_LINES + 6, LANES), jnp.float32),
            pltpu.SMEM((2, STEPS), jnp.float32),
            pltpu.SMEM((NMAT, 4), jnp.float32),
            pltpu.SMEM((2,), jnp.int32),
            pltpu.SMEM((6,), jnp.int32),
            pltpu.SemaphoreType.DMA((4,)),
        ],
        compiler_params=pltpu.CompilerParams(vmem_limit_bytes=48 * 1024 * 1024),
        name="window",
    )(
        *[in_hbm(v) for v in (source_waveforms[0], material_table, plane_indices, design_box)],
        source_profiles[0].transpose(1, 0, 2),
        tile,
        y_a,
        y_b,
        *arrived,
    )
    final = pl.pallas_call(
        emit_kernel,
        out_shape=f32(1, 2, 3, ROWS, LINES * NZ),
        in_specs=[vmem],
        out_specs=vmem,
        name="emit",
    )(electric)

    if lax.axis_size("wave") == 4:
        one, two, three = [
            lax.ppermute(partial, "wave", [(i, i ^ k) for i in range(4)]) for k in (1, 2, 3)
        ]
        gradient = (partial + one) + (two + three)
    else:
        gradient = lax.psum(partial, "wave")
    return gradient, final


def solution(mesh):
    placed = (
        P("wave", None, None, "tx", "ty"),
        P("wave", None, None, None),
        P("wave", None, None),
        P("tx", "ty"),
        P("tx", "ty"),
        P(),
        P(),
        P(),
    )
    return jax.shard_map(
        functools.partial(on_device, mesh.shape["tx"], mesh.shape["ty"]),
        mesh=mesh,
        in_specs=placed,
        out_specs=(P("tx", "ty"), P("wave", None, None, "tx", "ty")),
        check_vma=False,
    )
```

```python
import functools

import jax
import jax.numpy as jnp
from jax import lax
from jax.experimental import pallas as pl
from jax.experimental.pallas import tpu as pltpu
from jax.sharding import PartitionSpec as P

NZ = 64
STEPS = 5
NMAT = 3
LANES = 2 * NZ
ROWS = 16
LINES = 8
CHUNKS = LINES // 2
PAD = 8
EXT_LINES = LINES + 2 * STEPS
FIELDS = 13

time_step = 0.5
contrast = 2.0

LINE_DEPTH = (5, 5, 5, 5, 4, 5, 3, 3, 3, 4, 4, 4, 4)
ROW_DEPTH = (5, 5, 5, 4, 5, 5, 3, 3, 3, 4, 4, 4, 4)
SAME_DEPTH = (4, 4, 4, 4, 4, 4, 2, 2, 2, 3, 3, 3, 3)
MIXED_DEPTH = (5, 5, 4, 4, 4, 4, 3, 3, 2, 4, 4, 3, 4)

Y_ENTRIES = [(f, k) for f in range(FIELDS) for k in range(LINE_DEPTH[f])]


def listed(entries):
    start, out = 0, []
    for f, k, depth in entries:
        out.append((f, k, depth, start))
        start += depth
    return out, (start + 7) // 8 * 8


X_ENTRIES, X_ROWS = listed([(f, line, ROW_DEPTH[f]) for f in range(FIELDS) for line in range(LINES)])
CORNERS = [
    listed([(f, k, depth[f] - k) for f in range(FIELDS) for k in range(depth[f])])
    for depth in (SAME_DEPTH, MIXED_DEPTH)
]


def low_lanes(shape):
    return lax.broadcasted_iota(jnp.int32, shape, len(shape) - 1) < NZ


def half_turn(v):
    return pltpu.roll(v, NZ, v.ndim - 1)


def choose(material, column):
    values = [column(m) for m in range(NMAT)]
    return jnp.where(material < 0.5, values[0], jnp.where(material < 1.5, values[1], values[2]))


def pole(table):
    out = []
    for m in range(NMAT):
        d, w, g = table[m, 1], table[m, 2], table[m, 3]
        denom = 1.0 + 0.25 * g
        drive = w * w * time_step / denom
        out.append(((1.0 - 0.25 * g) / denom, drive, drive * d))
    return [lambda m, i=i: out[m][i] for i in range(3)]


def is_lower_in_a():
    return lax.rem(lax.axis_index("ty") + lax.axis_index("wave"), 2) == 0


def pack_kernel(table_hbm, fields_hbm, material_hbm, density_hbm, tile, y_a, y_b, table, fields, material, density, sems):
    copies = [
        pltpu.make_async_copy(table_hbm, table, sems.at[CHUNKS]),
        pltpu.make_async_copy(material_hbm, material, sems.at[CHUNKS + 1]),
        pltpu.make_async_copy(density_hbm, density, sems.at[CHUNKS + 2]),
    ]
    chunks = [
        pltpu.make_async_copy(
            fields_hbm.at[0, :, :, :, pl.ds(k * LANES, LANES)], fields.at[k], sems.at[k]
        )
        for k in range(CHUNKS)
    ]
    for copy in copies + chunks:
        copy.start()
    for copy in copies:
        copy.wait()
    decay, drive, coupled = pole(table)
    low = low_lanes((ROWS, LANES))
    for k in range(CHUNKS):
        at = slice(k * LANES, (k + 1) * LANES)
        chunks[k].wait()

        def split(one, two):
            return jnp.where(low, one, half_turn(two)), jnp.where(low, half_turn(one), two)

        pairs = [split(fields[k, 0, f], fields[k, 1, f]) for f in range(12)]
        mat, dens = material[:, at].astype(jnp.float32), density[:, at]
        turned = half_turn(mat)
        mats = (jnp.where(low, mat, turned), jnp.where(low, turned, mat))
        mixed = split(mat, dens)
        for half in range(2):
            line = 2 * k + half
            dec, dri, cou = [choose(mats[half], column) for column in (decay, drive, coupled)]
            for c in range(3):
                e, p, j = pairs[c][half], pairs[6 + c][half], pairs[9 + c][half]
                j = dec * j + cou * e - dri * p
                tile[c, line] = e
                tile[3 + c, line] = pairs[3 + c][half]
                tile[6 + c, line] = p + time_step * j
                tile[9 + c, line] = j
            tile[12, line] = mixed[half]
    lower = is_lower_in_a()
    for i, (f, k) in enumerate(Y_ENTRIES):
        first, last = k, LINES - 1 - k
        y_a[i] = tile[f, jnp.where(lower, last, first)]
        y_b[i] = tile[f, jnp.where(lower, first, last)]


def edge_kernel(tile, *messages):
    odd = lax.rem(lax.axis_index("tx"), 2)
    for kind in range(len(messages) // 3):
        along, same, mixed = messages[3 * kind : 3 * kind + 3]
        for is_lower in (True, False):

            @pl.when((odd == kind) == is_lower)
            def _(is_lower=is_lower, along=along, same=same, mixed=mixed):
                def pack(message, entries, line_of):
                    for f, k, depth, start in entries:
                        rows = slice(ROWS - depth, ROWS) if is_lower else slice(0, depth)
                        message[start : start + depth, :] = tile[f, line_of(k), rows, :]

                pack(along, X_ENTRIES, lambda k: k)
                pack(same, CORNERS[0][0], lambda k: LINES - 1 - k if is_lower else k)
                pack(mixed, CORNERS[1][0], lambda k: k if is_lower else LINES - 1 - k)


def window_kernel(
    tx_count,
    ty_count,
    waveforms_hbm,
    table_hbm,
    plane_hbm,
    box_hbm,
    profiles,
    tile,
    y_a,
    y_b,
    *rest,
):
    kinds = 1 if tx_count == 2 else 2
    messages, rest = rest[: 3 * kinds], rest[3 * kinds :]
    electric_out, gradient_out, E, H, Pol, J, C, coef, source, waveforms, table, plane, box, sems = rest
    wide = tx_count != 2
    ext_rows = E[0].shape[2]
    copies = [
        pltpu.make_async_copy(src, dst, sems.at[i])
        for i, (src, dst) in enumerate(
            [(waveforms_hbm, waveforms), (table_hbm, table), (plane_hbm, plane), (box_hbm, box)]
        )
    ]
    for copy in copies:
        copy.start()
    tx, ty = lax.axis_index("tx"), lax.axis_index("ty")
    odd_x = lax.rem(tx, 2)
    offset = PAD if wide else pl.multiple_of(tx * PAD, PAD)
    rows_base, lines_base = tx * ROWS - offset, ty * LINES - STEPS
    rows_all, lines_all = tx_count * ROWS, ty_count * LINES
    middle = pl.ds(offset, ROWS)

    def put(f, line, rows, value):
        if f < 12:
            (E[0], H[0], Pol[0], J[0])[f // 3][f % 3, line, rows, :] = value
        else:
            C[line, rows, :] = value

    for ref in (E[0], H[0], Pol[0], J[0], C):
        ref[...] = jnp.zeros(ref.shape, jnp.float32)
    for f in range(FIELDS):
        for line in range(LINES):
            put(f, STEPS + line, middle, tile[f, line])

    def line_at(ahead, k):
        return jnp.where(ahead, STEPS + LINES + k, STEPS - 1 - k)

    lower = is_lower_in_a()
    for message, is_lower in ((y_a, lower), (y_b, jnp.logical_not(lower))):

        @pl.when(jnp.where(is_lower, ty + 1 < ty_count, ty > 0))
        def _(message=message, is_lower=is_lower):
            for i, (f, k) in enumerate(Y_ENTRIES):
                put(f, line_at(is_lower, k), middle, message[i])

    for kind in range(kinds):
        along, same, mixed = messages[3 * kind : 3 * kind + 3]
        for is_lower in (True, False):

            in_x = tx + 1 < tx_count if is_lower else tx > 0
            behind, ahead = ty > 0, ty + 1 < ty_count

            @pl.when(jnp.logical_and((odd_x == kind) == is_lower, in_x))
            def _(is_lower=is_lower, along=along, same=same, mixed=mixed, behind=behind, ahead=ahead):
                def unpack(message, entries, line_of):
                    for f, k, depth, start in entries:
                        if wide:
                            first = PAD + ROWS if is_lower else PAD - depth
                        else:
                            first = ROWS if is_lower else PAD - depth
                        put(f, line_of(k), slice(first, first + depth), message[start : start + depth, :])

                unpack(along, X_ENTRIES, lambda k: STEPS + k)

                @pl.when(ahead if is_lower else behind)
                def _():
                    unpack(same, CORNERS[0][0], lambda k: STEPS + LINES + k if is_lower else STEPS - 1 - k)

                @pl.when(behind if is_lower else ahead)
                def _():
                    unpack(mixed, CORNERS[1][0], lambda k: STEPS - 1 - k if is_lower else STEPS + LINES + k)

    for copy in copies:
        copy.wait()
    decay, drive, coupled = pole(table)
    shape = (ext_rows, LANES)
    low = low_lanes(shape)
    lane = lax.broadcasted_iota(jnp.int32, shape, 1)
    depth_id = jnp.where(low, lane, lane - NZ)
    row = lax.broadcasted_iota(jnp.int32, shape, 0) + rows_base
    first_z, last_z = depth_id == 0, depth_id == NZ - 1
    row_mask = ((row >= 0) & (row < rows_all)).astype(jnp.float32)
    in_z = (depth_id >= box[4]) & (depth_id < box[5])
    design_rows = ((row >= box[0]) & (row < box[1]) & in_z).astype(jnp.float32)
    source_rows = (row == jnp.where(low, plane[0], plane[1])).astype(jnp.float32)

    def line_design(line):
        where = lines_base + line
        return ((where >= box[2]) & (where < box[3])).astype(jnp.float32)

    def line_inside(line):
        where = lines_base + line
        return ((where >= 0) & (where < lines_all)).astype(jnp.float32)

    def is_own(line):
        return STEPS <= line < STEPS + LINES

    for line in range(1, EXT_LINES - 1):
        mixed = C[line]
        turned = half_turn(mixed)
        mat = jnp.where(low, mixed, turned)
        dens = jnp.where(low, turned, mixed)
        design = design_rows * line_design(line)
        permittivity = choose(mat, lambda m: table[m, 0]) + (design * dens) * contrast
        reach = time_step / permittivity
        if wide:
            reach = reach * row_mask
        if not is_own(line):
            reach = reach * line_inside(line)
        coef[0, line] = reach
        for i, column in enumerate((decay, drive, coupled)):
            coef[1 + i, line] = choose(mat, column)

    low_row = low[:1]
    for i in range(EXT_LINES // 2):
        chunk = jnp.clip(ty * CHUNKS + (i - STEPS // 2 - 1) + 1, 0, ty_count * CHUNKS - 1)
        for c in range(3):
            both = profiles[c, :, pl.ds(pl.multiple_of(chunk * LANES, LANES), LANES)]
            one, two = both[0:1], both[1:2]
            source[c, pl.ds(2 * i + 1, 1), :] = jnp.where(low_row, one, half_turn(two))
            source[c, pl.ds(2 * i + 2, 1), :] = jnp.where(low_row, half_turn(one), two)

    edge = jnp.zeros((1, LANES), jnp.float32)

    def ahead_row(v):
        return jnp.concatenate([v[1:], edge], axis=0)

    def behind_row(v):
        return jnp.concatenate([edge, v[:-1]], axis=0)

    def ahead_depth(v):
        return jnp.where(last_z, 0.0, pltpu.roll(v, LANES - 1, 1))

    def behind_depth(v):
        return jnp.where(first_z, 0.0, pltpu.roll(v, 1, 1))

    def magnetic_line(n, line):
        old, new = H[n % 2], H[(n + 1) % 2]
        ex, ey, ez = E[n][0, line], E[n][1, line], E[n][2, line]
        ex_next, ez_next = E[n][0, line + 1], E[n][2, line + 1]
        half = time_step
        if line < STEPS:
            half = half * line_inside(line)
        if wide:
            half = half * row_mask
        new[0, line] = old[0, line] - half * ((ez_next - ez) - (ahead_depth(ey) - ey))
        new[1, line] = old[1, line] - half * ((ahead_depth(ex) - ex) - (ahead_row(ez) - ez))
        new[2, line] = old[2, line] - half * ((ahead_row(ey) - ey) - (ex_next - ex))

    def electric_line(n, line, weight):
        field = H[(n + 1) % 2]
        hx, hy, hz = field[0, line], field[1, line], field[2, line]
        hx_last, hz_last = field[0, line - 1], field[2, line - 1]
        curls = (
            (hz - hz_last) - (hy - behind_depth(hy)),
            (hx - behind_depth(hx)) - (hz - behind_row(hz)),
            (hy - behind_row(hy)) - (hx - hx_last),
        )
        reach = coef[0, line]
        for c in range(3):
            e = E[n][c, line]
            if n == 0:
                j = J[0][c, line]
            else:
                p = Pol[(n + 1) % 2][c, line]
                j = coef[1, line] * J[(n + 1) % 2][c, line] + coef[3, line] * e - coef[2, line] * p
                if n < STEPS - 1:
                    J[n % 2][c, line] = j
                    Pol[n % 2][c, line] = p + time_step * j
            drawn = source_rows * (weight * source[c, line : line + 1, :])
            E[n + 1][c, line] = e + reach * ((curls[c] - j) - drawn)

    for n in range(STEPS):
        weight = jnp.where(low_row, waveforms[0, n], waveforms[1, n])
        for line in range(n, EXT_LINES - 1 - n):
            magnetic_line(n, line)
        for line in range(n + 1, EXT_LINES - 1 - n):
            electric_line(n, line, weight)

    low_tile = low[:ROWS]
    row_tile = lax.broadcasted_iota(jnp.int32, (ROWS, LANES), 0) + tx * ROWS
    design_tile = (
        (row_tile >= box[0]) & (row_tile < box[1]) & in_z[:ROWS]
    ).astype(jnp.float32) * contrast
    for k in range(CHUNKS):
        sums = []
        for half in range(2):
            line = STEPS + 2 * k + half
            total = jnp.zeros((ROWS, LANES), jnp.float32)
            for c in range(3):
                history = [E[n][c, line, middle, :] for n in range(STEPS + 1)]
                for n in range(1, STEPS + 1):
                    total = total + half_turn(history[STEPS + 1 - n]) * (history[n] - history[n - 1])
                electric_out[c, 2 * k + half] = history[STEPS]
            sums.append(total * (design_tile * line_design(line)))
        gradient_out[:, k * LANES : (k + 1) * LANES] = jnp.where(low_tile, sums[0], half_turn(sums[1]))


def emit_kernel(electric, out):
    low = low_lanes((ROWS, LANES))
    for k in range(CHUNKS):
        at = slice(k * LANES, (k + 1) * LANES)
        for c in range(3):
            one, two = electric[c, 2 * k], electric[c, 2 * k + 1]
            out[0, 0, c, :, at] = jnp.where(low, one, half_turn(two))
            out[0, 1, c, :, at] = jnp.where(low, half_turn(one), two)


def pair_of(index, kind, count):
    other = index + 1 if index % 2 == kind else index - 1
    return other if 0 <= other < count else None


def f32(*shape):
    return jax.ShapeDtypeStruct(shape, jnp.float32)


def in_hbm(value):
    return pltpu.with_memory_space_constraint(value, pltpu.HBM)


def on_device(
    tx_count,
    ty_count,
    initial_fields,
    source_profiles,
    source_waveforms,
    material_map,
    design_density,
    material_table,
    plane_indices,
    design_box,
):
    hbm = pl.BlockSpec(memory_space=pltpu.HBM)
    vmem = pl.BlockSpec(memory_space=pltpu.VMEM)
    kinds = (0,) if tx_count == 2 else (0, 1)

    waves = lax.axis_size("wave")

    def swap(value, partner):
        def index(w, x, y):
            return (w * tx_count + x) * ty_count + y

        pairs = []
        for w in range(waves):
            for x in range(tx_count):
                for y in range(ty_count):
                    ox, oy = partner(w, x, y)
                    if ox is not None and oy is not None and 0 <= oy < ty_count:
                        pairs.append((index(w, x, y), index(w, ox, oy)))
                    elif waves % 2 == 0:
                        pairs.append((index(w, x, y), index((w + waves // 2) % waves, x, y)))
        return lax.ppermute(value, ("wave", "tx", "ty"), pairs)

    def along_y(b):
        return lambda w, x, y: (x, pair_of(y, (w + b) % 2, ty_count))

    def along_x(kind):
        return lambda w, x, y: (pair_of(x, kind, tx_count), y)

    def corner(kind, mixed):
        return lambda w, x, y: (pair_of(x, kind, tx_count), y + (1 if (x % 2 == kind) != mixed else -1))

    tile, y_a, y_b = pl.pallas_call(
        pack_kernel,
        out_shape=(
            f32(FIELDS, LINES, ROWS, LANES),
            f32(len(Y_ENTRIES), ROWS, LANES),
            f32(len(Y_ENTRIES), ROWS, LANES),
        ),
        in_specs=[hbm] * 4,
        out_specs=(vmem, vmem, vmem),
        scratch_shapes=[
            pltpu.SMEM((NMAT, 4), jnp.float32),
            pltpu.VMEM((CHUNKS, 2, 12, ROWS, LANES), jnp.float32),
            pltpu.VMEM((ROWS, LINES * NZ), jnp.int32),
            pltpu.VMEM((ROWS, LINES * NZ), jnp.float32),
            pltpu.SemaphoreType.DMA((CHUNKS + 3,)),
        ],
        compiler_params=pltpu.CompilerParams(vmem_limit_bytes=32 * 1024 * 1024),
        name="pack",
    )(*[in_hbm(v) for v in (material_table, initial_fields, material_map, design_density)])
    y_a, y_b = swap(y_a, along_y(0)), swap(y_b, along_y(1))

    sizes = (X_ROWS, CORNERS[0][1], CORNERS[1][1]) * len(kinds)
    messages = pl.pallas_call(
        edge_kernel,
        out_shape=[f32(size, LANES) for size in sizes],
        in_specs=[vmem],
        out_specs=[vmem] * len(sizes),
        compiler_params=pltpu.CompilerParams(vmem_limit_bytes=32 * 1024 * 1024),
        name="edges",
    )(tile)
    arrived = []
    for i, message in enumerate(messages):
        kind = i // 3
        arrived.append(swap(message, along_x(kind) if i % 3 == 0 else corner(kind, i % 3 == 2)))

    ext = (EXT_LINES, ROWS + (PAD if tx_count == 2 else 2 * PAD), LANES)
    electric, partial = pl.pallas_call(
        functools.partial(window_kernel, tx_count, ty_count),
        out_shape=(f32(3, LINES, ROWS, LANES), f32(ROWS, LINES * NZ)),
        in_specs=[hbm] * 4 + [vmem] * (4 + len(arrived)),
        out_specs=(vmem, vmem),
        scratch_shapes=[
            [pltpu.VMEM((3,) + ext, jnp.float32) for _ in range(STEPS + 1)],
            [pltpu.VMEM((3,) + ext, jnp.float32) for _ in range(2)],
            [pltpu.VMEM((3,) + ext, jnp.float32) for _ in range(2)],
            [pltpu.VMEM((3,) + ext, jnp.float32) for _ in range(2)],
            pltpu.VMEM(ext, jnp.float32),
            pltpu.VMEM((4,) + ext, jnp.float32),
            pltpu.VMEM((3, EXT_LINES + 6, LANES), jnp.float32),
            pltpu.SMEM((2, STEPS), jnp.float32),
            pltpu.SMEM((NMAT, 4), jnp.float32),
            pltpu.SMEM((2,), jnp.int32),
            pltpu.SMEM((6,), jnp.int32),
            pltpu.SemaphoreType.DMA((4,)),
        ],
        compiler_params=pltpu.CompilerParams(vmem_limit_bytes=48 * 1024 * 1024),
        name="window",
    )(
        *[in_hbm(v) for v in (source_waveforms[0], material_table, plane_indices, design_box)],
        source_profiles[0].transpose(1, 0, 2),
        tile,
        y_a,
        y_b,
        *arrived,
    )
    final = pl.pallas_call(
        emit_kernel,
        out_shape=f32(1, 2, 3, ROWS, LINES * NZ),
        in_specs=[vmem],
        out_specs=vmem,
        compiler_params=pltpu.CompilerParams(vmem_limit_bytes=8 * 1024 * 1024),
        name="emit",
    )(electric)

    if lax.axis_size("wave") == 4:
        one, two, three = [
            lax.ppermute(partial, "wave", [(i, i ^ k) for i in range(4)]) for k in (1, 2, 3)
        ]
        gradient = (partial + one) + (two + three)
    else:
        gradient = lax.psum(partial, "wave")
    return gradient, final


def solution(mesh):
    placed = (
        P("wave", None, None, "tx", "ty"),
        P("wave", None, None, None),
        P("wave", None, None),
        P("tx", "ty"),
        P("tx", "ty"),
        P(),
        P(),
        P(),
    )
    return jax.shard_map(
        functools.partial(on_device, mesh.shape["tx"], mesh.shape["ty"]),
        mesh=mesh,
        in_specs=placed,
        out_specs=(P("tx", "ty"), P("wave", None, None, "tx", "ty")),
        check_vma=False,
    )
```

```python
import functools

import jax
import jax.numpy as jnp
from jax import lax
from jax.experimental import pallas as pl
from jax.experimental.pallas import tpu as pltpu
from jax.sharding import PartitionSpec as P

NZ = 64
STEPS = 5
NMAT = 3
LANES = 2 * NZ
ROWS = 16
LINES = 8
CHUNKS = LINES // 2
PAD = 8
EXT_LINES = LINES + 2 * STEPS
FIELDS = 13

time_step = 0.5
contrast = 2.0

BEHIND_LINES = (4, 4, 4, 5, 4, 5, 2, 2, 2, 3, 3, 3, 4)
AHEAD_LINES = (4, 3, 4, 4, 4, 4, 2, 1, 2, 3, 2, 3, 4)
BEHIND_ROWS = (4, 4, 4, 4, 5, 5, 2, 2, 2, 3, 3, 3, 4)
AHEAD_ROWS = (3, 4, 4, 4, 4, 4, 1, 2, 2, 2, 3, 3, 4)
BEHIND_BOTH = (3, 3, 3, 4, 4, 4, 1, 1, 1, 2, 2, 2, 3)
AHEAD_BOTH = (3, 3, 3, 3, 3, 3, 1, 1, 1, 2, 2, 2, 3)
AHEAD_ROW_BEHIND_LINE = (3, 4, 3, 4, 3, 4, 1, 2, 1, 2, 3, 2, 4)
BEHIND_ROW_AHEAD_LINE = (4, 3, 3, 3, 4, 4, 2, 1, 1, 3, 2, 2, 4)
BORDER = 5


def line_entries(depth):
    return [(f, k) for f in range(FIELDS) for k in range(depth[f])]


def row_entries(entries):
    start, out = 0, []
    for f, k, depth in entries:
        out.append((f, k, depth, start))
        start += depth
    return out, start


def corner_entries(depth):
    return row_entries([(f, k, depth[f] - k) for f in range(FIELDS) for k in range(depth[f])])


Y_ENTRIES = {False: line_entries(BEHIND_LINES), True: line_entries(AHEAD_LINES)}
Y_SIZE = max(len(Y_ENTRIES[False]) + 1, len(Y_ENTRIES[True]) + 3)
X_ENTRIES = {
    ahead: row_entries([(f, line, depth[f]) for f in range(FIELDS) for line in range(LINES)])
    for ahead, depth in ((False, BEHIND_ROWS), (True, AHEAD_ROWS))
}
SAME_ENTRIES = {False: corner_entries(BEHIND_BOTH), True: corner_entries(AHEAD_BOTH)}
MIXED_ENTRIES = {False: corner_entries(BEHIND_ROW_AHEAD_LINE), True: corner_entries(AHEAD_ROW_BEHIND_LINE)}


def round_up(n):
    return (n + 7) // 8 * 8


X_SIZE = round_up(max(X_ENTRIES[False][1] + 2 * BORDER, X_ENTRIES[True][1] + 2 * BORDER + 2 * LINES))
SAME_SIZE = round_up(max(SAME_ENTRIES[False][1], SAME_ENTRIES[True][1] + 16))
MIXED_SIZE = round_up(max(MIXED_ENTRIES[ahead][1] + 2 * BORDER for ahead in (False, True)))


def low_lanes(shape):
    return lax.broadcasted_iota(jnp.int32, shape, len(shape) - 1) < NZ


def half_turn(v):
    return pltpu.roll(v, NZ, v.ndim - 1)


def choose(material, column):
    values = [column(m) for m in range(NMAT)]
    return jnp.where(material < 0.5, values[0], jnp.where(material < 1.5, values[1], values[2]))


def pole(table):
    out = []
    for m in range(NMAT):
        d, w, g = table[m, 1], table[m, 2], table[m, 3]
        denom = 1.0 + 0.25 * g
        drive = w * w * time_step / denom
        out.append(((1.0 - 0.25 * g) / denom, drive, drive * d))
    return [lambda m, i=i: out[m][i] for i in range(3)]


def is_lower_in_a():
    return lax.rem(lax.axis_index("ty") + lax.axis_index("wave"), 2) == 0


def pack_kernel(
    table_hbm,
    box_hbm,
    fields_hbm,
    material_hbm,
    density_hbm,
    tile,
    start,
    y_a,
    y_b,
    table,
    box,
    fields,
    material,
    density,
    sems,
):
    copies = [
        pltpu.make_async_copy(src, dst, sems.at[CHUNKS + i])
        for i, (src, dst) in enumerate(
            [(table_hbm, table), (box_hbm, box), (material_hbm, material), (density_hbm, density)]
        )
    ]
    chunks = [
        pltpu.make_async_copy(
            fields_hbm.at[0, :, :, :, pl.ds(k * LANES, LANES)], fields.at[k], sems.at[k]
        )
        for k in range(CHUNKS)
    ]
    for copy in copies + chunks:
        copy.start()
    for copy in copies:
        copy.wait()
    decay, drive, coupled = pole(table)
    shape = (ROWS, LANES)
    low = low_lanes(shape)
    lane = lax.broadcasted_iota(jnp.int32, shape, 1)
    depth_id = jnp.where(low, lane, lane - NZ)
    last_z = depth_id == NZ - 1
    row = lax.broadcasted_iota(jnp.int32, shape, 0) + lax.axis_index("tx") * ROWS
    in_z = (depth_id >= box[4]) & (depth_id < box[5])
    design_rows = ((row >= box[0]) & (row < box[1]) & in_z).astype(jnp.float32)
    first_line = lax.axis_index("ty") * LINES
    for k in range(CHUNKS):
        at = slice(k * LANES, (k + 1) * LANES)
        chunks[k].wait()

        def split(one, two):
            return jnp.where(low, one, half_turn(two)), jnp.where(low, half_turn(one), two)

        pairs = [split(fields[k, 0, f], fields[k, 1, f]) for f in range(12)]
        mat, dens = material[:, at].astype(jnp.float32), density[:, at]
        turned = half_turn(mat)
        mats = (jnp.where(low, mat, turned), jnp.where(low, turned, mat))
        turned = half_turn(dens)
        denses = (jnp.where(low, dens, turned), jnp.where(low, turned, dens))
        for half in range(2):
            line = 2 * k + half
            mat, dens = mats[half], denses[half]
            where = first_line + line
            design = design_rows * ((where >= box[2]) & (where < box[3])).astype(jnp.float32)
            permittivity = choose(mat, lambda m: table[m, 0]) + design * dens * contrast
            reach = time_step / permittivity
            dec, dri, cou = [choose(mat, column) for column in (decay, drive, coupled)]
            for c in range(3):
                e, p, j = pairs[c][half], pairs[6 + c][half], pairs[9 + c][half]
                j = dec * j + cou * e - dri * p
                p = p + time_step * j
                start[c, line] = e
                tile[c, line] = e - reach * j
                tile[3 + c, line] = pairs[3 + c][half]
                tile[6 + c, line] = p
                tile[9 + c, line] = dec * j - dri * p
            tile[12, line] = jnp.where(low, mat, dens)

    edge = jnp.zeros((1, LANES), jnp.float32)

    def ahead_row(v):
        return jnp.concatenate([v[1:], edge], axis=0)

    def ahead_depth(v):
        return jnp.where(last_z, 0.0, pltpu.roll(v, LANES - 1, 1))

    for line in range(LINES):
        ex, ey, ez = [start[c, line] for c in range(3)]
        if line + 1 < LINES:
            ex_next, ez_next = start[0, line + 1], start[2, line + 1]
        else:
            ex_next = ez_next = jnp.zeros(shape, jnp.float32)
        tile[3, line] = tile[3, line] - time_step * ((ez_next - ez) - (ahead_depth(ey) - ey))
        tile[4, line] = tile[4, line] - time_step * ((ahead_depth(ex) - ex) - (ahead_row(ez) - ez))
        tile[5, line] = tile[5, line] - time_step * ((ahead_row(ey) - ey) - (ex_next - ex))

    lower = is_lower_in_a()
    for message, is_lower in ((y_a, lower), (y_b, jnp.logical_not(lower))):
        for ahead in (False, True):

            @pl.when(is_lower != ahead)
            def _(message=message, ahead=ahead):
                def line_of(k):
                    return k if ahead else LINES - 1 - k

                entries = Y_ENTRIES[ahead]
                for i, (f, k) in enumerate(entries):
                    message[i] = tile[f, line_of(k)]
                last = len(entries)
                for k in range(4 if ahead else 5):
                    message[last, k : k + 1, :] = start[1, line_of(k), 0:1, :]
                    message[last, 5 + k : 6 + k, :] = start[2, line_of(k), 0:1, :]
                if ahead:
                    message[last + 1] = start[0, 0]
                    message[last + 2] = start[2, 0]


def edge_kernel(tile, start, *messages):
    odd = lax.rem(lax.axis_index("tx"), 2)
    for kind in range(len(messages) // 3):
        along, same, mixed = messages[3 * kind : 3 * kind + 3]
        for ahead in (False, True):

            @pl.when((odd == kind) != ahead)
            def _(ahead=ahead, along=along, same=same, mixed=mixed):
                def rows(depth):
                    return slice(0, depth) if ahead else slice(ROWS - depth, ROWS)

                def pack(message, entries, line_of):
                    for f, k, depth, at in entries[0]:
                        message[at : at + depth, :] = tile[f, line_of(k), rows(depth), :]
                    return entries[1]

                def pack_first_line(message, at, depth):
                    for c in (0, 2):
                        message[at : at + depth, :] = start[c, 0, rows(depth), :]
                        at += depth
                    return at

                def pack_first_row(message, at, lines):
                    for c in (1, 2):
                        for line in lines:
                            message[at : at + 1, :] = start[c, line, 0:1, :]
                            at += 1

                at = pack(along, X_ENTRIES[ahead], lambda k: k)
                at = pack_first_line(along, at, BORDER)
                if ahead:
                    pack_first_row(along, at, range(LINES))
                at = pack(same, SAME_ENTRIES[ahead], lambda k: k if ahead else LINES - 1 - k)
                if ahead:
                    at = pack_first_line(same, at, 4)
                    pack_first_row(same, at, range(4))
                at = pack(mixed, MIXED_ENTRIES[ahead], lambda k: LINES - 1 - k if ahead else k)
                if ahead:
                    pack_first_row(mixed, at, [LINES - 1 - k for k in range(BORDER)])
                else:
                    pack_first_line(mixed, at, BORDER)


def window_kernel(
    tx_count,
    ty_count,
    waveforms_hbm,
    table_hbm,
    plane_hbm,
    box_hbm,
    profiles,
    tile,
    start,
    y_a,
    y_b,
    *rest,
):
    kinds = 1 if tx_count == 2 else 2
    messages, rest = rest[: 3 * kinds], rest[3 * kinds :]
    electric_out, gradient_out, E, H, Pol, J, C, coef, source, first_row, waveforms, table, plane, box, sems = rest
    wide = tx_count != 2
    ext_rows = E[0].shape[2]
    copies = [
        pltpu.make_async_copy(src, dst, sems.at[i])
        for i, (src, dst) in enumerate(
            [(waveforms_hbm, waveforms), (table_hbm, table), (plane_hbm, plane), (box_hbm, box)]
        )
    ]
    for copy in copies:
        copy.start()
    tx, ty = lax.axis_index("tx"), lax.axis_index("ty")
    odd_x = lax.rem(tx, 2)
    offset = PAD if wide else pl.multiple_of(tx * PAD, PAD)
    rows_base, lines_base = tx * ROWS - offset, ty * LINES - STEPS
    rows_all, lines_all = tx_count * ROWS, ty_count * LINES
    middle = pl.ds(offset, ROWS)

    def put(f, line, rows, value):
        if f < 12:
            (E[0], H[1], Pol[0], J[0])[f // 3][f % 3, line, rows, :] = value
        else:
            C[line, rows, :] = value

    def clear(lines, rows, count):
        for f in range(FIELDS):
            for line in lines:
                put(f, line, rows, jnp.zeros((count, LANES), jnp.float32))

    every_row, behind_lines, ahead_lines = slice(0, ext_rows), range(STEPS), range(STEPS + LINES, EXT_LINES)
    no_behind, no_ahead = ty == 0, ty + 1 == ty_count
    if wide:

        @pl.when(tx == 0)
        def _():
            clear(range(EXT_LINES), slice(0, PAD), PAD)

        @pl.when(tx + 1 == tx_count)
        def _():
            clear(range(EXT_LINES), slice(PAD + ROWS, ext_rows), PAD)

    @pl.when(no_behind)
    def _():
        clear(behind_lines, every_row, ext_rows)

    @pl.when(no_ahead)
    def _():
        clear(ahead_lines, every_row, ext_rows)

    for f in range(FIELDS):
        for line in range(LINES):
            put(f, STEPS + line, middle, tile[f, line])

    def near(ahead, k):
        return STEPS + LINES + k if ahead else STEPS - 1 - k

    def correct_line(line, rows, ex, ez):
        H[1][0, line, rows, :] = H[1][0, line, rows, :] - time_step * ez
        H[1][2, line, rows, :] = H[1][2, line, rows, :] + time_step * ex

    def correct_row(line, row, ey, ez):
        at = slice(row, row + 1)
        H[1][1, line, at, :] = H[1][1, line, at, :] + time_step * ez
        H[1][2, line, at, :] = H[1][2, line, at, :] - time_step * ey

    lower = is_lower_in_a()
    for message, is_lower in ((y_a, lower), (y_b, jnp.logical_not(lower))):
        for ahead in (False, True):

            @pl.when(jnp.logical_and(is_lower == ahead, jnp.logical_not(no_ahead if ahead else no_behind)))
            def _(message=message, ahead=ahead):
                entries = Y_ENTRIES[ahead]
                for i, (f, k) in enumerate(entries):
                    put(f, near(ahead, k), middle, message[i])
                last = len(entries)
                for k in range(4 if ahead else 5):
                    first_row[0, near(ahead, k) : near(ahead, k) + 1, :] = message[last, k : k + 1, :]
                    first_row[1, near(ahead, k) : near(ahead, k) + 1, :] = message[last, 5 + k : 6 + k, :]
                if ahead:
                    correct_line(STEPS + LINES - 1, middle, message[last + 1], message[last + 2])
                else:
                    correct_line(STEPS - 1, middle, start[0, 0], start[2, 0])

    for kind in range(kinds):
        along, same, mixed = messages[3 * kind : 3 * kind + 3]
        for ahead in (False, True):
            in_x = tx + 1 < tx_count if ahead else tx > 0
            halo = ROWS + (PAD if wide else 0) if ahead else PAD
            last_row = halo - 1

            @pl.when(jnp.logical_and((odd_x == kind) == ahead, in_x))
            def _(ahead=ahead, along=along, same=same, mixed=mixed, halo=halo, last_row=last_row):
                def rows(depth):
                    return slice(halo, halo + depth) if ahead else slice(halo - depth, halo)

                def unpack(message, entries, line_of):
                    for f, k, depth, at in entries[0]:
                        put(f, line_of(k), rows(depth), message[at : at + depth, :])
                    return entries[1]

                def first_line(message, at, depth, line):
                    ex, ez = message[at : at + depth, :], message[at + depth : at + 2 * depth, :]
                    correct_line(line, rows(depth), ex, ez)
                    return at + 2 * depth

                def rows_ahead(message, at, lines):
                    for i, line in enumerate(lines):
                        one, two = at + i, at + len(lines) + i
                        correct_row(line, last_row, message[one : one + 1, :], message[two : two + 1, :])

                def rows_own(lines):
                    for line in lines:
                        correct_row(
                            line,
                            last_row,
                            first_row[0, line : line + 1, :],
                            first_row[1, line : line + 1, :],
                        )

                along_end = unpack(along, X_ENTRIES[ahead], lambda k: STEPS + k)
                if ahead:
                    rows_ahead(along, along_end + 2 * BORDER, range(STEPS, STEPS + LINES))
                else:
                    for line in range(LINES):
                        correct_row(STEPS + line, last_row, start[1, line, 0:1, :], start[2, line, 0:1, :])

                @pl.when(jnp.logical_not(no_behind))
                def _():
                    message, entries = (mixed, MIXED_ENTRIES[True]) if ahead else (same, SAME_ENTRIES[False])
                    at = unpack(message, entries, lambda k: near(False, k))
                    first_line(along, along_end, BORDER, STEPS - 1)
                    if ahead:
                        rows_ahead(message, at, [near(False, k) for k in range(BORDER)])
                    else:
                        rows_own(behind_lines)

                @pl.when(jnp.logical_not(no_ahead))
                def _():
                    message, entries = (same, SAME_ENTRIES[True]) if ahead else (mixed, MIXED_ENTRIES[False])
                    at = unpack(message, entries, lambda k: near(True, k))
                    at = first_line(message, at, 4 if ahead else BORDER, STEPS + LINES - 1)
                    if ahead:
                        rows_ahead(message, at, [near(True, k) for k in range(4)])
                    else:
                        rows_own([near(True, k) for k in range(4)])

    for copy in copies:
        copy.wait()
    decay, drive, coupled = pole(table)
    shape = (ext_rows, LANES)
    low = low_lanes(shape)
    lane = lax.broadcasted_iota(jnp.int32, shape, 1)
    depth_id = jnp.where(low, lane, lane - NZ)
    row = lax.broadcasted_iota(jnp.int32, shape, 0) + rows_base
    first_z, last_z = depth_id == 0, depth_id == NZ - 1
    row_mask = ((row >= 0) & (row < rows_all)).astype(jnp.float32)
    in_z = (depth_id >= box[4]) & (depth_id < box[5])
    design_rows = ((row >= box[0]) & (row < box[1]) & in_z).astype(jnp.float32)
    source_rows = (row == jnp.where(low, plane[0], plane[1])).astype(jnp.float32)

    def line_design(line):
        where = lines_base + line
        return ((where >= box[2]) & (where < box[3])).astype(jnp.float32)

    def line_inside(line):
        where = lines_base + line
        return ((where >= 0) & (where < lines_all)).astype(jnp.float32)

    def is_own(line):
        return STEPS <= line < STEPS + LINES

    for line in range(1, EXT_LINES - 1):
        mixed = C[line]
        turned = half_turn(mixed)
        mat = jnp.where(low, mixed, turned)
        dens = jnp.where(low, turned, mixed)
        design = design_rows * line_design(line)
        permittivity = choose(mat, lambda m: table[m, 0]) + (design * dens) * contrast
        reach = time_step / permittivity
        if wide:
            reach = reach * row_mask
        if not is_own(line):
            reach = reach * line_inside(line)
        coef[0, line] = reach
        for i, column in enumerate((decay, drive, coupled)):
            coef[1 + i, line] = choose(mat, column)

    low_row = low[:1]
    for i in range(EXT_LINES // 2):
        chunk = jnp.clip(ty * CHUNKS + (i - STEPS // 2 - 1) + 1, 0, ty_count * CHUNKS - 1)
        for c in range(3):
            both = profiles[c, :, pl.ds(pl.multiple_of(chunk * LANES, LANES), LANES)]
            one, two = both[0:1], both[1:2]
            source[c, pl.ds(2 * i + 1, 1), :] = jnp.where(low_row, one, half_turn(two))
            source[c, pl.ds(2 * i + 2, 1), :] = jnp.where(low_row, half_turn(one), two)

    edge = jnp.zeros((1, LANES), jnp.float32)

    def ahead_row(v):
        return jnp.concatenate([v[1:], edge], axis=0)

    def behind_row(v):
        return jnp.concatenate([edge, v[:-1]], axis=0)

    def ahead_depth(v):
        return jnp.where(last_z, 0.0, pltpu.roll(v, LANES - 1, 1))

    def behind_depth(v):
        return jnp.where(first_z, 0.0, pltpu.roll(v, 1, 1))

    def magnetic_line(n, line):
        old, new = H[n % 2], H[(n + 1) % 2]
        ex, ey, ez = E[n][0, line], E[n][1, line], E[n][2, line]
        ex_next, ez_next = E[n][0, line + 1], E[n][2, line + 1]
        half = time_step
        if line < STEPS:
            half = half * line_inside(line)
        if wide:
            half = half * row_mask
        new[0, line] = old[0, line] - half * ((ez_next - ez) - (ahead_depth(ey) - ey))
        new[1, line] = old[1, line] - half * ((ahead_depth(ex) - ex) - (ahead_row(ez) - ez))
        new[2, line] = old[2, line] - half * ((ahead_row(ey) - ey) - (ex_next - ex))

    def electric_line(n, line, weight):
        field = H[(n + 1) % 2]
        hx, hy, hz = field[0, line], field[1, line], field[2, line]
        hx_last, hz_last = field[0, line - 1], field[2, line - 1]
        curls = (
            (hz - hz_last) - (hy - behind_depth(hy)),
            (hx - behind_depth(hx)) - (hz - behind_row(hz)),
            (hy - behind_row(hy)) - (hx - hx_last),
        )
        reach = coef[0, line]
        for c in range(3):
            e = E[n][c, line]
            curl = curls[c]
            if n > 0:
                p, j = Pol[(n + 1) % 2][c, line], J[(n + 1) % 2][c, line]
                if n == 1:
                    j = j + coef[3, line] * e
                else:
                    j = coef[1, line] * j + coef[3, line] * e - coef[2, line] * p
                if n < STEPS - 1:
                    J[n % 2][c, line] = j
                    Pol[n % 2][c, line] = p + time_step * j
                curl = curl - j
            drawn = source_rows * (weight * source[c, line : line + 1, :])
            E[n + 1][c, line] = e + reach * (curl - drawn)

    for n in range(STEPS):
        weight = jnp.where(low_row, waveforms[0, n], waveforms[1, n])
        for line in range(n, EXT_LINES - 1 - n) if n > 0 else ():
            magnetic_line(n, line)
        for line in range(n + 1, EXT_LINES - 1 - n):
            electric_line(n, line, weight)

    low_tile = low[:ROWS]
    row_tile = lax.broadcasted_iota(jnp.int32, (ROWS, LANES), 0) + tx * ROWS
    design_tile = (
        (row_tile >= box[0]) & (row_tile < box[1]) & in_z[:ROWS]
    ).astype(jnp.float32) * contrast
    for k in range(CHUNKS):
        sums = []
        for half in range(2):
            line = STEPS + 2 * k + half
            total = jnp.zeros((ROWS, LANES), jnp.float32)
            for c in range(3):
                history = [start[c, 2 * k + half]]
                history += [E[n][c, line, middle, :] for n in range(1, STEPS + 1)]
                for n in range(1, STEPS + 1):
                    total = total + half_turn(history[STEPS + 1 - n]) * (history[n] - history[n - 1])
                electric_out[c, 2 * k + half] = history[STEPS]
            sums.append(total * (design_tile * line_design(line)))
        gradient_out[:, k * LANES : (k + 1) * LANES] = jnp.where(low_tile, sums[0], half_turn(sums[1]))


def emit_kernel(electric, out):
    low = low_lanes((ROWS, LANES))
    for k in range(CHUNKS):
        at = slice(k * LANES, (k + 1) * LANES)
        for c in range(3):
            one, two = electric[c, 2 * k], electric[c, 2 * k + 1]
            out[0, 0, c, :, at] = jnp.where(low, one, half_turn(two))
            out[0, 1, c, :, at] = jnp.where(low, half_turn(one), two)


def pair_of(index, kind, count):
    other = index + 1 if index % 2 == kind else index - 1
    return other if 0 <= other < count else None


def f32(*shape):
    return jax.ShapeDtypeStruct(shape, jnp.float32)


def in_hbm(value):
    return pltpu.with_memory_space_constraint(value, pltpu.HBM)


def on_device(
    tx_count,
    ty_count,
    initial_fields,
    source_profiles,
    source_waveforms,
    material_map,
    design_density,
    material_table,
    plane_indices,
    design_box,
):
    hbm = pl.BlockSpec(memory_space=pltpu.HBM)
    vmem = pl.BlockSpec(memory_space=pltpu.VMEM)
    kinds = (0,) if tx_count == 2 else (0, 1)

    waves = lax.axis_size("wave")

    def swap(value, partner):
        def index(w, x, y):
            return (w * tx_count + x) * ty_count + y

        pairs = []
        for w in range(waves):
            for x in range(tx_count):
                for y in range(ty_count):
                    ox, oy = partner(w, x, y)
                    if ox is not None and oy is not None and 0 <= oy < ty_count:
                        pairs.append((index(w, x, y), index(w, ox, oy)))
                    elif waves % 2 == 0:
                        pairs.append((index(w, x, y), index((w + waves // 2) % waves, x, y)))
        return lax.ppermute(value, ("wave", "tx", "ty"), pairs)

    def along_y(b):
        return lambda w, x, y: (x, pair_of(y, (w + b) % 2, ty_count))

    def along_x(kind):
        return lambda w, x, y: (pair_of(x, kind, tx_count), y)

    def corner(kind, mixed):
        return lambda w, x, y: (pair_of(x, kind, tx_count), y + (1 if (x % 2 == kind) != mixed else -1))

    tile, start, y_a, y_b = pl.pallas_call(
        pack_kernel,
        out_shape=(
            f32(FIELDS, LINES, ROWS, LANES),
            f32(3, LINES, ROWS, LANES),
            f32(Y_SIZE, ROWS, LANES),
            f32(Y_SIZE, ROWS, LANES),
        ),
        in_specs=[hbm] * 5,
        out_specs=(vmem,) * 4,
        scratch_shapes=[
            pltpu.SMEM((NMAT, 4), jnp.float32),
            pltpu.SMEM((6,), jnp.int32),
            pltpu.VMEM((CHUNKS, 2, 12, ROWS, LANES), jnp.float32),
            pltpu.VMEM((ROWS, LINES * NZ), jnp.int32),
            pltpu.VMEM((ROWS, LINES * NZ), jnp.float32),
            pltpu.SemaphoreType.DMA((CHUNKS + 4,)),
        ],
        compiler_params=pltpu.CompilerParams(vmem_limit_bytes=32 * 1024 * 1024),
        name="pack",
    )(*[in_hbm(v) for v in (material_table, design_box, initial_fields, material_map, design_density)])
    y_a, y_b = swap(y_a, along_y(0)), swap(y_b, along_y(1))

    sizes = (X_SIZE, SAME_SIZE, MIXED_SIZE) * len(kinds)
    messages = pl.pallas_call(
        edge_kernel,
        out_shape=[f32(size, LANES) for size in sizes],
        in_specs=[vmem, vmem],
        out_specs=[vmem] * len(sizes),
        compiler_params=pltpu.CompilerParams(vmem_limit_bytes=32 * 1024 * 1024),
        name="edges",
    )(tile, start)
    arrived = []
    for i, message in enumerate(messages):
        kind = i // 3
        arrived.append(swap(message, along_x(kind) if i % 3 == 0 else corner(kind, i % 3 == 2)))

    ext = (EXT_LINES, ROWS + (PAD if tx_count == 2 else 2 * PAD), LANES)
    electric, partial = pl.pallas_call(
        functools.partial(window_kernel, tx_count, ty_count),
        out_shape=(f32(3, LINES, ROWS, LANES), f32(ROWS, LINES * NZ)),
        in_specs=[hbm] * 4 + [vmem] * (5 + len(arrived)),
        out_specs=(vmem, vmem),
        scratch_shapes=[
            [pltpu.VMEM((3,) + ext, jnp.float32) for _ in range(STEPS + 1)],
            [pltpu.VMEM((3,) + ext, jnp.float32) for _ in range(2)],
            [pltpu.VMEM((3,) + ext, jnp.float32) for _ in range(2)],
            [pltpu.VMEM((3,) + ext, jnp.float32) for _ in range(2)],
            pltpu.VMEM(ext, jnp.float32),
            pltpu.VMEM((4,) + ext, jnp.float32),
            pltpu.VMEM((3, EXT_LINES + 6, LANES), jnp.float32),
            pltpu.VMEM((2, EXT_LINES + 6, LANES), jnp.float32),
            pltpu.SMEM((2, STEPS), jnp.float32),
            pltpu.SMEM((NMAT, 4), jnp.float32),
            pltpu.SMEM((2,), jnp.int32),
            pltpu.SMEM((6,), jnp.int32),
            pltpu.SemaphoreType.DMA((4,)),
        ],
        compiler_params=pltpu.CompilerParams(vmem_limit_bytes=48 * 1024 * 1024),
        name="window",
    )(
        *[in_hbm(v) for v in (source_waveforms[0], material_table, plane_indices, design_box)],
        source_profiles[0].transpose(1, 0, 2),
        tile,
        start,
        y_a,
        y_b,
        *arrived,
    )
    final = pl.pallas_call(
        emit_kernel,
        out_shape=f32(1, 2, 3, ROWS, LINES * NZ),
        in_specs=[vmem],
        out_specs=vmem,
        compiler_params=pltpu.CompilerParams(vmem_limit_bytes=8 * 1024 * 1024),
        name="emit",
    )(electric)

    if lax.axis_size("wave") == 4:
        one, two, three = [
            lax.ppermute(partial, "wave", [(i, i ^ k) for i in range(4)]) for k in (1, 2, 3)
        ]
        gradient = (partial + one) + (two + three)
    else:
        gradient = lax.psum(partial, "wave")
    return gradient, final


def solution(mesh):
    placed = (
        P("wave", None, None, "tx", "ty"),
        P("wave", None, None, None),
        P("wave", None, None),
        P("tx", "ty"),
        P("tx", "ty"),
        P(),
        P(),
        P(),
    )
    return jax.shard_map(
        functools.partial(on_device, mesh.shape["tx"], mesh.shape["ty"]),
        mesh=mesh,
        in_specs=placed,
        out_specs=(P("tx", "ty"), P("wave", None, None, "tx", "ty")),
        check_vma=False,
    )
```

```python
import functools

import jax
import jax.numpy as jnp
from jax import lax
from jax.experimental import pallas as pl
from jax.experimental.pallas import tpu as pltpu
from jax.sharding import PartitionSpec as P

NZ = 64
STEPS = 5
NMAT = 3
LANES = 2 * NZ
ROWS = 16
LINES = 8
CHUNKS = LINES // 2
PAD = 8
EXT_LINES = LINES + 2 * STEPS
FIELDS = 13

time_step = 0.5
contrast = 2.0

BEHIND_LINES = (4, 4, 4, 5, 4, 5, 2, 2, 2, 3, 3, 3, 4)
AHEAD_LINES = (4, 3, 4, 4, 4, 4, 2, 1, 2, 3, 2, 3, 4)
BEHIND_ROWS = (4, 4, 4, 4, 5, 5, 2, 2, 2, 3, 3, 3, 4)
AHEAD_ROWS = (3, 4, 4, 4, 4, 4, 1, 2, 2, 2, 3, 3, 4)
BEHIND_BOTH = (3, 3, 3, 4, 4, 4, 1, 1, 1, 2, 2, 2, 3)
AHEAD_BOTH = (3, 3, 3, 3, 3, 3, 1, 1, 1, 2, 2, 2, 3)
AHEAD_ROW_BEHIND_LINE = (3, 4, 3, 4, 3, 4, 1, 2, 1, 2, 3, 2, 4)
BEHIND_ROW_AHEAD_LINE = (4, 3, 3, 3, 4, 4, 2, 1, 1, 3, 2, 2, 4)
BORDER = 5


def line_entries(depth):
    return [(f, k) for f in range(FIELDS) for k in range(depth[f])]


def row_entries(entries):
    start, out = 0, []
    for f, k, depth in entries:
        out.append((f, k, depth, start))
        start += depth
    return out, start


def corner_entries(depth):
    return row_entries([(f, k, depth[f] - k) for f in range(FIELDS) for k in range(depth[f])])


Y_ENTRIES = {False: line_entries(BEHIND_LINES), True: line_entries(AHEAD_LINES)}
Y_SIZE = max(len(Y_ENTRIES[False]) + 1, len(Y_ENTRIES[True]) + 3)
X_ENTRIES = {
    ahead: row_entries([(f, line, depth[f]) for f in range(FIELDS) for line in range(LINES)])
    for ahead, depth in ((False, BEHIND_ROWS), (True, AHEAD_ROWS))
}
SAME_ENTRIES = {False: corner_entries(BEHIND_BOTH), True: corner_entries(AHEAD_BOTH)}
MIXED_ENTRIES = {False: corner_entries(BEHIND_ROW_AHEAD_LINE), True: corner_entries(AHEAD_ROW_BEHIND_LINE)}


def round_up(n):
    return (n + 7) // 8 * 8


X_SIZE = round_up(max(X_ENTRIES[False][1] + 2 * BORDER, X_ENTRIES[True][1] + 2 * BORDER + 2 * LINES))
SAME_SIZE = round_up(max(SAME_ENTRIES[False][1], SAME_ENTRIES[True][1] + 16))
MIXED_SIZE = round_up(max(MIXED_ENTRIES[ahead][1] + 2 * BORDER for ahead in (False, True)))


def low_lanes(shape):
    return lax.broadcasted_iota(jnp.int32, shape, len(shape) - 1) < NZ


def half_turn(v):
    return pltpu.roll(v, NZ, v.ndim - 1)


def choose(material, column):
    values = [column(m) for m in range(NMAT)]
    return jnp.where(material < 0.5, values[0], jnp.where(material < 1.5, values[1], values[2]))


def pole(table):
    out = []
    for m in range(NMAT):
        d, w, g = table[m, 1], table[m, 2], table[m, 3]
        denom = 1.0 + 0.25 * g
        drive = w * w * time_step / denom
        out.append(((1.0 - 0.25 * g) / denom, drive, drive * d))
    return [lambda m, i=i: out[m][i] for i in range(3)]


def is_lower_in_a():
    return lax.rem(lax.axis_index("ty"), 2) == 0


def pack_kernel(
    table_hbm,
    box_hbm,
    fields_hbm,
    material_hbm,
    density_hbm,
    tile,
    start,
    y_a,
    y_b,
    table,
    box,
    fields,
    material,
    density,
    sems,
):
    copies = [
        pltpu.make_async_copy(src, dst, sems.at[CHUNKS + i])
        for i, (src, dst) in enumerate(
            [(table_hbm, table), (box_hbm, box), (material_hbm, material), (density_hbm, density)]
        )
    ]
    chunks = [
        pltpu.make_async_copy(
            fields_hbm.at[0, :, :, :, pl.ds(k * LANES, LANES)], fields.at[k], sems.at[k]
        )
        for k in range(CHUNKS)
    ]
    for copy in copies + chunks:
        copy.start()
    for copy in copies:
        copy.wait()
    decay, drive, coupled = pole(table)
    shape = (ROWS, LANES)
    low = low_lanes(shape)
    lane = lax.broadcasted_iota(jnp.int32, shape, 1)
    depth_id = jnp.where(low, lane, lane - NZ)
    last_z = depth_id == NZ - 1
    row = lax.broadcasted_iota(jnp.int32, shape, 0) + lax.axis_index("tx") * ROWS
    in_z = (depth_id >= box[4]) & (depth_id < box[5])
    design_rows = ((row >= box[0]) & (row < box[1]) & in_z).astype(jnp.float32)
    first_line = lax.axis_index("ty") * LINES
    for k in range(CHUNKS):
        at = slice(k * LANES, (k + 1) * LANES)
        chunks[k].wait()

        def split(one, two):
            return jnp.where(low, one, half_turn(two)), jnp.where(low, half_turn(one), two)

        pairs = [split(fields[k, 0, f], fields[k, 1, f]) for f in range(12)]
        mat, dens = material[:, at].astype(jnp.float32), density[:, at]
        turned = half_turn(mat)
        mats = (jnp.where(low, mat, turned), jnp.where(low, turned, mat))
        turned = half_turn(dens)
        denses = (jnp.where(low, dens, turned), jnp.where(low, turned, dens))
        for half in range(2):
            line = 2 * k + half
            mat, dens = mats[half], denses[half]
            where = first_line + line
            design = design_rows * ((where >= box[2]) & (where < box[3])).astype(jnp.float32)
            permittivity = choose(mat, lambda m: table[m, 0]) + design * dens * contrast
            reach = time_step / permittivity
            dec, dri, cou = [choose(mat, column) for column in (decay, drive, coupled)]
            for c in range(3):
                e, p, j = pairs[c][half], pairs[6 + c][half], pairs[9 + c][half]
                j = dec * j + cou * e - dri * p
                p = p + time_step * j
                start[c, line] = e
                tile[c, line] = e - reach * j
                tile[3 + c, line] = pairs[3 + c][half]
                tile[6 + c, line] = p
                tile[9 + c, line] = dec * j - dri * p
            tile[12, line] = jnp.where(low, mat, dens)

    edge = jnp.zeros((1, LANES), jnp.float32)

    def ahead_row(v):
        return jnp.concatenate([v[1:], edge], axis=0)

    def ahead_depth(v):
        return jnp.where(last_z, 0.0, pltpu.roll(v, LANES - 1, 1))

    for line in range(LINES):
        ex, ey, ez = [start[c, line] for c in range(3)]
        if line + 1 < LINES:
            ex_next, ez_next = start[0, line + 1], start[2, line + 1]
        else:
            ex_next = ez_next = jnp.zeros(shape, jnp.float32)
        tile[3, line] = tile[3, line] - time_step * ((ez_next - ez) - (ahead_depth(ey) - ey))
        tile[4, line] = tile[4, line] - time_step * ((ahead_depth(ex) - ex) - (ahead_row(ez) - ez))
        tile[5, line] = tile[5, line] - time_step * ((ahead_row(ey) - ey) - (ex_next - ex))

    lower = is_lower_in_a()
    for message, is_lower in ((y_a, lower), (y_b, jnp.logical_not(lower))):
        for ahead in (False, True):

            @pl.when(is_lower != ahead)
            def _(message=message, ahead=ahead):
                def line_of(k):
                    return k if ahead else LINES - 1 - k

                entries = Y_ENTRIES[ahead]
                for i, (f, k) in enumerate(entries):
                    message[i] = tile[f, line_of(k)]
                last = len(entries)
                for k in range(4 if ahead else 5):
                    message[last, k : k + 1, :] = start[1, line_of(k), 0:1, :]
                    message[last, 5 + k : 6 + k, :] = start[2, line_of(k), 0:1, :]
                if ahead:
                    message[last + 1] = start[0, 0]
                    message[last + 2] = start[2, 0]


def edge_kernel(tile, start, *messages):
    odd = lax.rem(lax.axis_index("tx"), 2)
    for kind in range(len(messages) // 3):
        along, same, mixed = messages[3 * kind : 3 * kind + 3]
        for ahead in (False, True):

            @pl.when((odd == kind) != ahead)
            def _(ahead=ahead, along=along, same=same, mixed=mixed):
                def rows(depth):
                    return slice(0, depth) if ahead else slice(ROWS - depth, ROWS)

                def pack(message, entries, line_of):
                    for f, k, depth, at in entries[0]:
                        message[at : at + depth, :] = tile[f, line_of(k), rows(depth), :]
                    return entries[1]

                def pack_first_line(message, at, depth):
                    for c in (0, 2):
                        message[at : at + depth, :] = start[c, 0, rows(depth), :]
                        at += depth
                    return at

                def pack_first_row(message, at, lines):
                    for c in (1, 2):
                        for line in lines:
                            message[at : at + 1, :] = start[c, line, 0:1, :]
                            at += 1

                at = pack(along, X_ENTRIES[ahead], lambda k: k)
                at = pack_first_line(along, at, BORDER)
                if ahead:
                    pack_first_row(along, at, range(LINES))
                at = pack(same, SAME_ENTRIES[ahead], lambda k: k if ahead else LINES - 1 - k)
                if ahead:
                    at = pack_first_line(same, at, 4)
                    pack_first_row(same, at, range(4))
                at = pack(mixed, MIXED_ENTRIES[ahead], lambda k: LINES - 1 - k if ahead else k)
                if ahead:
                    pack_first_row(mixed, at, [LINES - 1 - k for k in range(BORDER)])
                else:
                    pack_first_line(mixed, at, BORDER)


def window_kernel(
    tx_count,
    ty_count,
    waveforms_hbm,
    table_hbm,
    plane_hbm,
    box_hbm,
    profiles,
    tile,
    start,
    y_a,
    y_b,
    *rest,
):
    kinds = 1 if tx_count == 2 else 2
    messages, rest = rest[: 3 * kinds], rest[3 * kinds :]
    electric_out, gradient_out, E, H, Pol, J, C, coef, source, first_row, waveforms, table, plane, box, sems = rest
    wide = tx_count != 2
    ext_rows = E[0].shape[2]
    copies = [
        pltpu.make_async_copy(src, dst, sems.at[i])
        for i, (src, dst) in enumerate(
            [(waveforms_hbm, waveforms), (table_hbm, table), (plane_hbm, plane), (box_hbm, box)]
        )
    ]
    for copy in copies:
        copy.start()
    tx, ty = lax.axis_index("tx"), lax.axis_index("ty")
    odd_x = lax.rem(tx, 2)
    offset = PAD if wide else pl.multiple_of(tx * PAD, PAD)
    rows_base, lines_base = tx * ROWS - offset, ty * LINES - STEPS
    rows_all, lines_all = tx_count * ROWS, ty_count * LINES
    middle = pl.ds(offset, ROWS)

    def put(f, line, rows, value):
        if f < 12:
            (E[0], H[1], Pol[0], J[0])[f // 3][f % 3, line, rows, :] = value
        else:
            C[line, rows, :] = value

    def clear(lines, rows, count):
        for f in range(FIELDS):
            for line in lines:
                put(f, line, rows, jnp.zeros((count, LANES), jnp.float32))

    every_row, behind_lines, ahead_lines = slice(0, ext_rows), range(STEPS), range(STEPS + LINES, EXT_LINES)
    no_behind, no_ahead = ty == 0, ty + 1 == ty_count
    if wide:

        @pl.when(tx == 0)
        def _():
            clear(range(EXT_LINES), slice(0, PAD), PAD)

        @pl.when(tx + 1 == tx_count)
        def _():
            clear(range(EXT_LINES), slice(PAD + ROWS, ext_rows), PAD)

    @pl.when(no_behind)
    def _():
        clear(behind_lines, every_row, ext_rows)

    @pl.when(no_ahead)
    def _():
        clear(ahead_lines, every_row, ext_rows)

    for f in range(FIELDS):
        for line in range(LINES):
            put(f, STEPS + line, middle, tile[f, line])

    def near(ahead, k):
        return STEPS + LINES + k if ahead else STEPS - 1 - k

    def correct_line(line, rows, ex, ez):
        H[1][0, line, rows, :] = H[1][0, line, rows, :] - time_step * ez
        H[1][2, line, rows, :] = H[1][2, line, rows, :] + time_step * ex

    def correct_row(line, row, ey, ez):
        at = slice(row, row + 1)
        H[1][1, line, at, :] = H[1][1, line, at, :] + time_step * ez
        H[1][2, line, at, :] = H[1][2, line, at, :] - time_step * ey

    lower = is_lower_in_a()
    for message, is_lower in ((y_a, lower), (y_b, jnp.logical_not(lower))):
        for ahead in (False, True):

            @pl.when(jnp.logical_and(is_lower == ahead, jnp.logical_not(no_ahead if ahead else no_behind)))
            def _(message=message, ahead=ahead):
                entries = Y_ENTRIES[ahead]
                for i, (f, k) in enumerate(entries):
                    put(f, near(ahead, k), middle, message[i])
                last = len(entries)
                for k in range(4 if ahead else 5):
                    first_row[0, near(ahead, k) : near(ahead, k) + 1, :] = message[last, k : k + 1, :]
                    first_row[1, near(ahead, k) : near(ahead, k) + 1, :] = message[last, 5 + k : 6 + k, :]
                if ahead:
                    correct_line(STEPS + LINES - 1, middle, message[last + 1], message[last + 2])
                else:
                    correct_line(STEPS - 1, middle, start[0, 0], start[2, 0])

    for kind in range(kinds):
        along, same, mixed = messages[3 * kind : 3 * kind + 3]
        for ahead in (False, True):
            in_x = tx + 1 < tx_count if ahead else tx > 0
            halo = ROWS + (PAD if wide else 0) if ahead else PAD
            last_row = halo - 1

            @pl.when(jnp.logical_and((odd_x == kind) == ahead, in_x))
            def _(ahead=ahead, along=along, same=same, mixed=mixed, halo=halo, last_row=last_row):
                def rows(depth):
                    return slice(halo, halo + depth) if ahead else slice(halo - depth, halo)

                def unpack(message, entries, line_of):
                    for f, k, depth, at in entries[0]:
                        put(f, line_of(k), rows(depth), message[at : at + depth, :])
                    return entries[1]

                def first_line(message, at, depth, line):
                    ex, ez = message[at : at + depth, :], message[at + depth : at + 2 * depth, :]
                    correct_line(line, rows(depth), ex, ez)
                    return at + 2 * depth

                def rows_ahead(message, at, lines):
                    for i, line in enumerate(lines):
                        one, two = at + i, at + len(lines) + i
                        correct_row(line, last_row, message[one : one + 1, :], message[two : two + 1, :])

                def rows_own(lines):
                    for line in lines:
                        correct_row(
                            line,
                            last_row,
                            first_row[0, line : line + 1, :],
                            first_row[1, line : line + 1, :],
                        )

                along_end = unpack(along, X_ENTRIES[ahead], lambda k: STEPS + k)
                if ahead:
                    rows_ahead(along, along_end + 2 * BORDER, range(STEPS, STEPS + LINES))
                else:
                    for line in range(LINES):
                        correct_row(STEPS + line, last_row, start[1, line, 0:1, :], start[2, line, 0:1, :])

                @pl.when(jnp.logical_not(no_behind))
                def _():
                    message, entries = (mixed, MIXED_ENTRIES[True]) if ahead else (same, SAME_ENTRIES[False])
                    at = unpack(message, entries, lambda k: near(False, k))
                    first_line(along, along_end, BORDER, STEPS - 1)
                    if ahead:
                        rows_ahead(message, at, [near(False, k) for k in range(BORDER)])
                    else:
                        rows_own(behind_lines)

                @pl.when(jnp.logical_not(no_ahead))
                def _():
                    message, entries = (same, SAME_ENTRIES[True]) if ahead else (mixed, MIXED_ENTRIES[False])
                    at = unpack(message, entries, lambda k: near(True, k))
                    at = first_line(message, at, 4 if ahead else BORDER, STEPS + LINES - 1)
                    if ahead:
                        rows_ahead(message, at, [near(True, k) for k in range(4)])
                    else:
                        rows_own([near(True, k) for k in range(4)])

    for copy in copies:
        copy.wait()
    decay, drive, coupled = pole(table)
    shape = (ext_rows, LANES)
    low = low_lanes(shape)
    lane = lax.broadcasted_iota(jnp.int32, shape, 1)
    depth_id = jnp.where(low, lane, lane - NZ)
    row = lax.broadcasted_iota(jnp.int32, shape, 0) + rows_base
    first_z, last_z = depth_id == 0, depth_id == NZ - 1
    row_mask = ((row >= 0) & (row < rows_all)).astype(jnp.float32)
    in_z = (depth_id >= box[4]) & (depth_id < box[5])
    design_rows = ((row >= box[0]) & (row < box[1]) & in_z).astype(jnp.float32)
    source_rows = (row == jnp.where(low, plane[0], plane[1])).astype(jnp.float32)

    def line_design(line):
        where = lines_base + line
        return ((where >= box[2]) & (where < box[3])).astype(jnp.float32)

    def line_inside(line):
        where = lines_base + line
        return ((where >= 0) & (where < lines_all)).astype(jnp.float32)

    def is_own(line):
        return STEPS <= line < STEPS + LINES

    for line in range(1, EXT_LINES - 1):
        mixed = C[line]
        turned = half_turn(mixed)
        mat = jnp.where(low, mixed, turned)
        dens = jnp.where(low, turned, mixed)
        design = design_rows * line_design(line)
        permittivity = choose(mat, lambda m: table[m, 0]) + (design * dens) * contrast
        reach = time_step / permittivity
        if wide:
            reach = reach * row_mask
        if not is_own(line):
            reach = reach * line_inside(line)
        coef[0, line] = reach
        for i, column in enumerate((decay, drive, coupled)):
            coef[1 + i, line] = choose(mat, column)

    low_row = low[:1]
    for i in range(EXT_LINES // 2):
        chunk = jnp.clip(ty * CHUNKS + (i - STEPS // 2 - 1) + 1, 0, ty_count * CHUNKS - 1)
        for c in range(3):
            both = profiles[c, :, pl.ds(pl.multiple_of(chunk * LANES, LANES), LANES)]
            one, two = both[0:1], both[1:2]
            source[c, pl.ds(2 * i + 1, 1), :] = jnp.where(low_row, one, half_turn(two))
            source[c, pl.ds(2 * i + 2, 1), :] = jnp.where(low_row, half_turn(one), two)

    edge = jnp.zeros((1, LANES), jnp.float32)

    def ahead_row(v):
        return jnp.concatenate([v[1:], edge], axis=0)

    def behind_row(v):
        return jnp.concatenate([edge, v[:-1]], axis=0)

    def ahead_depth(v):
        return jnp.where(last_z, 0.0, pltpu.roll(v, LANES - 1, 1))

    def behind_depth(v):
        return jnp.where(first_z, 0.0, pltpu.roll(v, 1, 1))

    def magnetic_line(n, line):
        old, new = H[n % 2], H[(n + 1) % 2]
        ex, ey, ez = E[n][0, line], E[n][1, line], E[n][2, line]
        ex_next, ez_next = E[n][0, line + 1], E[n][2, line + 1]
        half = time_step
        if line < STEPS:
            half = half * line_inside(line)
        if wide:
            half = half * row_mask
        new[0, line] = old[0, line] - half * ((ez_next - ez) - (ahead_depth(ey) - ey))
        new[1, line] = old[1, line] - half * ((ahead_depth(ex) - ex) - (ahead_row(ez) - ez))
        new[2, line] = old[2, line] - half * ((ahead_row(ey) - ey) - (ex_next - ex))

    def electric_line(n, line, weight):
        field = H[(n + 1) % 2]
        hx, hy, hz = field[0, line], field[1, line], field[2, line]
        hx_last, hz_last = field[0, line - 1], field[2, line - 1]
        curls = (
            (hz - hz_last) - (hy - behind_depth(hy)),
            (hx - behind_depth(hx)) - (hz - behind_row(hz)),
            (hy - behind_row(hy)) - (hx - hx_last),
        )
        reach = coef[0, line]
        for c in range(3):
            e = E[n][c, line]
            curl = curls[c]
            if n > 0:
                p, j = Pol[(n + 1) % 2][c, line], J[(n + 1) % 2][c, line]
                if n == 1:
                    j = j + coef[3, line] * e
                else:
                    j = coef[1, line] * j + coef[3, line] * e - coef[2, line] * p
                if n < STEPS - 1:
                    J[n % 2][c, line] = j
                    Pol[n % 2][c, line] = p + time_step * j
                curl = curl - j
            drawn = source_rows * (weight * source[c, line : line + 1, :])
            E[n + 1][c, line] = e + reach * (curl - drawn)

    for n in range(STEPS):
        weight = jnp.where(low_row, waveforms[0, n], waveforms[1, n])
        for line in range(n, EXT_LINES - 1 - n) if n > 0 else ():
            magnetic_line(n, line)
        for line in range(n + 1, EXT_LINES - 1 - n):
            electric_line(n, line, weight)

    low_tile = low[:ROWS]
    row_tile = lax.broadcasted_iota(jnp.int32, (ROWS, LANES), 0) + tx * ROWS
    design_tile = (
        (row_tile >= box[0]) & (row_tile < box[1]) & in_z[:ROWS]
    ).astype(jnp.float32) * contrast
    for k in range(CHUNKS):
        sums = []
        for half in range(2):
            line = STEPS + 2 * k + half
            total = jnp.zeros((ROWS, LANES), jnp.float32)
            for c in range(3):
                history = [start[c, 2 * k + half]]
                history += [E[n][c, line, middle, :] for n in range(1, STEPS + 1)]
                for n in range(1, STEPS + 1):
                    total = total + half_turn(history[STEPS + 1 - n]) * (history[n] - history[n - 1])
                electric_out[c, 2 * k + half] = history[STEPS]
            sums.append(total * (design_tile * line_design(line)))
        gradient_out[:, k * LANES : (k + 1) * LANES] = jnp.where(low_tile, sums[0], half_turn(sums[1]))


def emit_kernel(electric, out):
    low = low_lanes((ROWS, LANES))
    for k in range(CHUNKS):
        at = slice(k * LANES, (k + 1) * LANES)
        for c in range(3):
            one, two = electric[c, 2 * k], electric[c, 2 * k + 1]
            out[0, 0, c, :, at] = jnp.where(low, one, half_turn(two))
            out[0, 1, c, :, at] = jnp.where(low, half_turn(one), two)


def pair_of(index, kind, count):
    other = index + 1 if index % 2 == kind else index - 1
    return other if 0 <= other < count else None


def f32(*shape):
    return jax.ShapeDtypeStruct(shape, jnp.float32)


def in_hbm(value):
    return pltpu.with_memory_space_constraint(value, pltpu.HBM)


def on_device(
    tx_count,
    ty_count,
    initial_fields,
    source_profiles,
    source_waveforms,
    material_map,
    design_density,
    material_table,
    plane_indices,
    design_box,
):
    hbm = pl.BlockSpec(memory_space=pltpu.HBM)
    vmem = pl.BlockSpec(memory_space=pltpu.VMEM)
    kinds = (0,) if tx_count == 2 else (0, 1)

    waves = lax.axis_size("wave")

    def swap(value, partner):
        def index(w, x, y):
            return (w * tx_count + x) * ty_count + y

        pairs = []
        for w in range(waves):
            for x in range(tx_count):
                for y in range(ty_count):
                    ox, oy = partner(w, x, y)
                    if ox is not None and oy is not None and 0 <= oy < ty_count:
                        pairs.append((index(w, x, y), index(w, ox, oy)))
                    elif waves % 2 == 0:
                        pairs.append((index(w, x, y), index(w ^ 1, x, y)))
        return lax.ppermute(value, ("wave", "tx", "ty"), pairs)

    def along_y(b):
        return lambda w, x, y: (x, pair_of(y, b, ty_count))

    def along_x(kind):
        return lambda w, x, y: (pair_of(x, kind, tx_count), y)

    def corner(kind, mixed):
        return lambda w, x, y: (pair_of(x, kind, tx_count), y + (1 if (x % 2 == kind) != mixed else -1))

    tile, start, y_a, y_b = pl.pallas_call(
        pack_kernel,
        out_shape=(
            f32(FIELDS, LINES, ROWS, LANES),
            f32(3, LINES, ROWS, LANES),
            f32(Y_SIZE, ROWS, LANES),
            f32(Y_SIZE, ROWS, LANES),
        ),
        in_specs=[hbm] * 5,
        out_specs=(vmem,) * 4,
        scratch_shapes=[
            pltpu.SMEM((NMAT, 4), jnp.float32),
            pltpu.SMEM((6,), jnp.int32),
            pltpu.VMEM((CHUNKS, 2, 12, ROWS, LANES), jnp.float32),
            pltpu.VMEM((ROWS, LINES * NZ), jnp.int32),
            pltpu.VMEM((ROWS, LINES * NZ), jnp.float32),
            pltpu.SemaphoreType.DMA((CHUNKS + 4,)),
        ],
        compiler_params=pltpu.CompilerParams(vmem_limit_bytes=32 * 1024 * 1024),
        name="pack",
    )(*[in_hbm(v) for v in (material_table, design_box, initial_fields, material_map, design_density)])
    y_a, y_b = swap(y_a, along_y(0)), swap(y_b, along_y(1))

    sizes = (X_SIZE, SAME_SIZE, MIXED_SIZE) * len(kinds)
    messages = pl.pallas_call(
        edge_kernel,
        out_shape=[f32(size, LANES) for size in sizes],
        in_specs=[vmem, vmem],
        out_specs=[vmem] * len(sizes),
        compiler_params=pltpu.CompilerParams(vmem_limit_bytes=32 * 1024 * 1024),
        name="edges",
    )(tile, start)
    arrived = []
    for i, message in enumerate(messages):
        kind = i // 3
        arrived.append(swap(message, along_x(kind) if i % 3 == 0 else corner(kind, i % 3 == 2)))

    ext = (EXT_LINES, ROWS + (PAD if tx_count == 2 else 2 * PAD), LANES)
    electric, partial = pl.pallas_call(
        functools.partial(window_kernel, tx_count, ty_count),
        out_shape=(f32(3, LINES, ROWS, LANES), f32(ROWS, LINES * NZ)),
        in_specs=[hbm] * 4 + [vmem] * (5 + len(arrived)),
        out_specs=(vmem, vmem),
        scratch_shapes=[
            [pltpu.VMEM((3,) + ext, jnp.float32) for _ in range(STEPS + 1)],
            [pltpu.VMEM((3,) + ext, jnp.float32) for _ in range(2)],
            [pltpu.VMEM((3,) + ext, jnp.float32) for _ in range(2)],
            [pltpu.VMEM((3,) + ext, jnp.float32) for _ in range(2)],
            pltpu.VMEM(ext, jnp.float32),
            pltpu.VMEM((4,) + ext, jnp.float32),
            pltpu.VMEM((3, EXT_LINES + 6, LANES), jnp.float32),
            pltpu.VMEM((2, EXT_LINES + 6, LANES), jnp.float32),
            pltpu.SMEM((2, STEPS), jnp.float32),
            pltpu.SMEM((NMAT, 4), jnp.float32),
            pltpu.SMEM((2,), jnp.int32),
            pltpu.SMEM((6,), jnp.int32),
            pltpu.SemaphoreType.DMA((4,)),
        ],
        compiler_params=pltpu.CompilerParams(vmem_limit_bytes=48 * 1024 * 1024),
        name="window",
    )(
        *[in_hbm(v) for v in (source_waveforms[0], material_table, plane_indices, design_box)],
        source_profiles[0].transpose(1, 0, 2),
        tile,
        start,
        y_a,
        y_b,
        *arrived,
    )
    final = pl.pallas_call(
        emit_kernel,
        out_shape=f32(1, 2, 3, ROWS, LINES * NZ),
        in_specs=[vmem],
        out_specs=vmem,
        compiler_params=pltpu.CompilerParams(vmem_limit_bytes=8 * 1024 * 1024),
        name="emit",
    )(electric)

    if lax.axis_size("wave") == 4:
        one, two, three = [
            lax.ppermute(partial, "wave", [(i, i ^ k) for i in range(4)]) for k in (1, 2, 3)
        ]
        gradient = (partial + one) + (two + three)
    else:
        gradient = lax.psum(partial, "wave")
    return gradient, final


def solution(mesh):
    placed = (
        P("wave", None, None, "tx", "ty"),
        P("wave", None, None, None),
        P("wave", None, None),
        P("tx", "ty"),
        P("tx", "ty"),
        P(),
        P(),
        P(),
    )
    return jax.shard_map(
        functools.partial(on_device, mesh.shape["tx"], mesh.shape["ty"]),
        mesh=mesh,
        in_specs=placed,
        out_specs=(P("tx", "ty"), P("wave", None, None, "tx", "ty")),
        check_vma=False,
    )
```

```python
import functools

import jax
import jax.numpy as jnp
from jax import lax
from jax.experimental import pallas as pl
from jax.experimental.pallas import tpu as pltpu
from jax.sharding import PartitionSpec as P

NZ = 64
STEPS = 5
NMAT = 3
LANES = 2 * NZ
ROWS = 16
LINES = 8
CHUNKS = LINES // 2
PAD = 8
EXT_LINES = LINES + 2 * STEPS
FIELDS = 13

time_step = 0.5
contrast = 2.0

BEHIND_LINES = (4, 4, 4, 5, 4, 5, 2, 2, 2, 3, 3, 3, 4)
AHEAD_LINES = (4, 3, 4, 4, 4, 4, 2, 1, 2, 3, 2, 3, 4)
BEHIND_ROWS = (4, 4, 4, 4, 5, 5, 2, 2, 2, 3, 3, 3, 4)
AHEAD_ROWS = (3, 4, 4, 4, 4, 4, 1, 2, 2, 2, 3, 3, 4)
BEHIND_BOTH = (3, 3, 3, 4, 4, 4, 1, 1, 1, 2, 2, 2, 3)
AHEAD_BOTH = (3, 3, 3, 3, 3, 3, 1, 1, 1, 2, 2, 2, 3)
AHEAD_ROW_BEHIND_LINE = (3, 4, 3, 4, 3, 4, 1, 2, 1, 2, 3, 2, 4)
BEHIND_ROW_AHEAD_LINE = (4, 3, 3, 3, 4, 4, 2, 1, 1, 3, 2, 2, 4)
BORDER = 5


def line_entries(depth):
    return [(f, k) for f in range(FIELDS) for k in range(depth[f])]


def row_entries(entries):
    start, out = 0, []
    for f, k, depth in entries:
        out.append((f, k, depth, start))
        start += depth
    return out, start


def corner_entries(depth):
    return row_entries([(f, k, depth[f] - k) for f in range(FIELDS) for k in range(depth[f])])


Y_ENTRIES = {False: line_entries(BEHIND_LINES), True: line_entries(AHEAD_LINES)}
Y_SIZE = max(len(Y_ENTRIES[False]) + 1, len(Y_ENTRIES[True]) + 3)
X_ENTRIES = {
    ahead: row_entries([(f, line, depth[f]) for f in range(FIELDS) for line in range(LINES)])
    for ahead, depth in ((False, BEHIND_ROWS), (True, AHEAD_ROWS))
}
SAME_ENTRIES = {False: corner_entries(BEHIND_BOTH), True: corner_entries(AHEAD_BOTH)}
MIXED_ENTRIES = {False: corner_entries(BEHIND_ROW_AHEAD_LINE), True: corner_entries(AHEAD_ROW_BEHIND_LINE)}


def round_up(n):
    return (n + 7) // 8 * 8


X_SIZE = round_up(max(X_ENTRIES[False][1] + 2 * BORDER, X_ENTRIES[True][1] + 2 * BORDER + 2 * LINES))
SAME_SIZE = round_up(max(SAME_ENTRIES[False][1], SAME_ENTRIES[True][1] + 16))
MIXED_SIZE = round_up(max(MIXED_ENTRIES[ahead][1] + 2 * BORDER for ahead in (False, True)))


def low_lanes(shape):
    return lax.broadcasted_iota(jnp.int32, shape, len(shape) - 1) < NZ


def half_turn(v):
    return pltpu.roll(v, NZ, v.ndim - 1)


def choose(material, column):
    values = [column(m) for m in range(NMAT)]
    return jnp.where(material < 0.5, values[0], jnp.where(material < 1.5, values[1], values[2]))


def pole(table):
    out = []
    for m in range(NMAT):
        d, w, g = table[m, 1], table[m, 2], table[m, 3]
        denom = 1.0 + 0.25 * g
        drive = w * w * time_step / denom
        out.append(((1.0 - 0.25 * g) / denom, drive * 0.5, drive * d * 2.0))
    return [lambda m, i=i: out[m][i] for i in range(3)]


def is_lower_in_a():
    return lax.rem(lax.axis_index("ty"), 2) == 0


def pack_kernel(
    table_hbm,
    box_hbm,
    fields_hbm,
    material_hbm,
    density_hbm,
    tile,
    start,
    y_a,
    y_b,
    table,
    box,
    fields,
    material,
    density,
    sems,
):
    copies = [
        pltpu.make_async_copy(src, dst, sems.at[CHUNKS + i])
        for i, (src, dst) in enumerate(
            [(table_hbm, table), (box_hbm, box), (material_hbm, material), (density_hbm, density)]
        )
    ]
    chunks = [
        pltpu.make_async_copy(
            fields_hbm.at[0, :, :, :, pl.ds(k * LANES, LANES)], fields.at[k], sems.at[k]
        )
        for k in range(CHUNKS)
    ]
    for copy in copies + chunks:
        copy.start()
    for copy in copies:
        copy.wait()
    decay, drive, coupled = pole(table)
    shape = (ROWS, LANES)
    low = low_lanes(shape)
    lane = lax.broadcasted_iota(jnp.int32, shape, 1)
    depth_id = jnp.where(low, lane, lane - NZ)
    last_z = depth_id == NZ - 1
    row = lax.broadcasted_iota(jnp.int32, shape, 0) + lax.axis_index("tx") * ROWS
    in_z = (depth_id >= box[4]) & (depth_id < box[5])
    design_rows = ((row >= box[0]) & (row < box[1]) & in_z).astype(jnp.float32)
    first_line = lax.axis_index("ty") * LINES
    for k in range(CHUNKS):
        at = slice(k * LANES, (k + 1) * LANES)
        chunks[k].wait()

        def split(one, two):
            return jnp.where(low, one, half_turn(two)), jnp.where(low, half_turn(one), two)

        pairs = [split(fields[k, 0, f], fields[k, 1, f]) for f in range(12)]
        mat, dens = material[:, at].astype(jnp.float32), density[:, at]
        turned = half_turn(mat)
        mats = (jnp.where(low, mat, turned), jnp.where(low, turned, mat))
        turned = half_turn(dens)
        denses = (jnp.where(low, dens, turned), jnp.where(low, turned, dens))
        for half in range(2):
            line = 2 * k + half
            mat, dens = mats[half], denses[half]
            where = first_line + line
            design = design_rows * ((where >= box[2]) & (where < box[3])).astype(jnp.float32)
            permittivity = choose(mat, lambda m: table[m, 0]) + design * dens * contrast
            reach = time_step * 0.5 / permittivity
            dec, dri, cou = [choose(mat, column) for column in (decay, drive, coupled)]
            for c in range(3):
                e, p, j = pairs[c][half], 4.0 * pairs[6 + c][half], 2.0 * pairs[9 + c][half]
                j = dec * j + cou * e - dri * p
                p = p + j
                start[c, line] = e
                tile[c, line] = e - reach * j
                tile[3 + c, line] = 2.0 * pairs[3 + c][half]
                tile[6 + c, line] = p
                tile[9 + c, line] = dec * j - dri * p
            tile[12, line] = jnp.where(low, mat, dens)

    edge = jnp.zeros((1, LANES), jnp.float32)

    def ahead_row(v):
        return jnp.concatenate([v[1:], edge], axis=0)

    def ahead_depth(v):
        return jnp.where(last_z, 0.0, pltpu.roll(v, LANES - 1, 1))

    for line in range(LINES):
        ex, ey, ez = [start[c, line] for c in range(3)]
        if line + 1 < LINES:
            ex_next, ez_next = start[0, line + 1], start[2, line + 1]
        else:
            ex_next = ez_next = jnp.zeros(shape, jnp.float32)
        tile[3, line] = tile[3, line] - ((ez_next - ez) - (ahead_depth(ey) - ey))
        tile[4, line] = tile[4, line] - ((ahead_depth(ex) - ex) - (ahead_row(ez) - ez))
        tile[5, line] = tile[5, line] - ((ahead_row(ey) - ey) - (ex_next - ex))

    lower = is_lower_in_a()
    for message, is_lower in ((y_a, lower), (y_b, jnp.logical_not(lower))):
        for ahead in (False, True):

            @pl.when(is_lower != ahead)
            def _(message=message, ahead=ahead):
                def line_of(k):
                    return k if ahead else LINES - 1 - k

                entries = Y_ENTRIES[ahead]
                for i, (f, k) in enumerate(entries):
                    message[i] = tile[f, line_of(k)]
                last = len(entries)
                for k in range(4 if ahead else 5):
                    message[last, k : k + 1, :] = start[1, line_of(k), 0:1, :]
                    message[last, 5 + k : 6 + k, :] = start[2, line_of(k), 0:1, :]
                if ahead:
                    message[last + 1] = start[0, 0]
                    message[last + 2] = start[2, 0]


def edge_kernel(tile, start, *messages):
    odd = lax.rem(lax.axis_index("tx"), 2)
    for kind in range(len(messages) // 3):
        along, same, mixed = messages[3 * kind : 3 * kind + 3]
        for ahead in (False, True):

            @pl.when((odd == kind) != ahead)
            def _(ahead=ahead, along=along, same=same, mixed=mixed):
                def rows(depth):
                    return slice(0, depth) if ahead else slice(ROWS - depth, ROWS)

                def pack(message, entries, line_of):
                    for f, k, depth, at in entries[0]:
                        message[at : at + depth, :] = tile[f, line_of(k), rows(depth), :]
                    return entries[1]

                def pack_first_line(message, at, depth):
                    for c in (0, 2):
                        message[at : at + depth, :] = start[c, 0, rows(depth), :]
                        at += depth
                    return at

                def pack_first_row(message, at, lines):
                    for c in (1, 2):
                        for line in lines:
                            message[at : at + 1, :] = start[c, line, 0:1, :]
                            at += 1

                at = pack(along, X_ENTRIES[ahead], lambda k: k)
                at = pack_first_line(along, at, BORDER)
                if ahead:
                    pack_first_row(along, at, range(LINES))
                at = pack(same, SAME_ENTRIES[ahead], lambda k: k if ahead else LINES - 1 - k)
                if ahead:
                    at = pack_first_line(same, at, 4)
                    pack_first_row(same, at, range(4))
                at = pack(mixed, MIXED_ENTRIES[ahead], lambda k: LINES - 1 - k if ahead else k)
                if ahead:
                    pack_first_row(mixed, at, [LINES - 1 - k for k in range(BORDER)])
                else:
                    pack_first_line(mixed, at, BORDER)


def prepare_kernel(
    tx_count,
    ty_count,
    waveforms_hbm,
    table_hbm,
    plane_hbm,
    box_hbm,
    profiles,
    sources,
    source_rows,
    design,
    poles,
    waveforms,
    table,
    plane,
    box,
    sems,
):
    copies = [
        pltpu.make_async_copy(src, dst, sems.at[i])
        for i, (src, dst) in enumerate(
            [(waveforms_hbm, waveforms), (table_hbm, table), (plane_hbm, plane), (box_hbm, box)]
        )
    ]
    for copy in copies:
        copy.start()
    for copy in copies:
        copy.wait()
    tx, ty = lax.axis_index("tx"), lax.axis_index("ty")
    shape = source_rows.shape
    low = low_lanes(shape)
    lane = lax.broadcasted_iota(jnp.int32, shape, 1)
    depth_id = jnp.where(low, lane, lane - NZ)
    row = window_rows(tx_count, shape)
    source_rows[...] = (row == jnp.where(low, plane[0], plane[1])).astype(jnp.float32)
    in_z = (depth_id >= box[4]) & (depth_id < box[5])
    design_rows = ((row >= box[0]) & (row < box[1]) & in_z).astype(jnp.float32) * contrast
    for line in range(1, EXT_LINES - 1):
        where = ty * LINES - STEPS + line
        design[line] = design_rows * ((where >= box[2]) & (where < box[3])).astype(jnp.float32)
    for i, column in enumerate((lambda m: table[m, 0], *pole(table))):
        for m in range(NMAT):
            at = NMAT * i + m
            poles[at : at + 1, :] = jnp.full((1, LANES), column(m), jnp.float32)
    low_row = low[:1]
    weights = [2.0 * jnp.where(low_row, waveforms[0, n], waveforms[1, n]) for n in range(STEPS)]
    for i in range(EXT_LINES // 2 - 1):
        chunk = jnp.clip(ty * CHUNKS + i - STEPS // 2, 0, ty_count * CHUNKS - 1)
        for c in range(3):
            both = profiles[c, :, pl.ds(pl.multiple_of(chunk * LANES, LANES), LANES)]
            one, two = both[0:1], both[1:2]
            first = jnp.where(low_row, one, half_turn(two))
            second = jnp.where(low_row, half_turn(one), two)
            for n in range(STEPS):
                sources[n, c, 2 * i + 1 : 2 * i + 2, :] = weights[n] * first
                sources[n, c, 2 * i + 2 : 2 * i + 3, :] = weights[n] * second


def window_rows(tx_count, shape):
    tx = lax.axis_index("tx")
    at = lax.broadcasted_iota(jnp.int32, shape, 0)
    if tx_count == 2:
        return at + tx * ROWS - jnp.where(at >= ROWS, tx * (ROWS + PAD), 0)
    return at + tx * ROWS - PAD


def window_kernel(
    tx_count,
    ty_count,
    sources,
    source_rows,
    design,
    poles,
    tile,
    start,
    y_a,
    y_b,
    *rest,
):
    kinds = 1 if tx_count == 2 else 2
    messages, rest = rest[: 3 * kinds], rest[3 * kinds :]
    electric_out, gradient_out, E, H, Pol, J, C, coef, first_row = rest
    wide = tx_count != 2
    ext_rows = E[0].shape[2]
    tx, ty = lax.axis_index("tx"), lax.axis_index("ty")
    odd_x = lax.rem(tx, 2)
    tile_row = PAD if wide else 0
    lines_base = ty * LINES - STEPS
    rows_all, lines_all = tx_count * ROWS, ty_count * LINES
    middle = slice(tile_row, tile_row + ROWS)

    def put(f, line, rows, value):
        if f < 12:
            (E[0], H[1], Pol[0], J[0])[f // 3][f % 3, line, rows, :] = value
        else:
            C[line, rows, :] = value

    def clear(lines, rows, count):
        for f in range(FIELDS):
            for line in lines:
                put(f, line, rows, jnp.zeros((count, LANES), jnp.float32))

    every_row, behind_lines, ahead_lines = slice(0, ext_rows), range(STEPS), range(STEPS + LINES, EXT_LINES)
    no_behind, no_ahead = ty == 0, ty + 1 == ty_count
    if wide:

        @pl.when(tx == 0)
        def _():
            clear(range(EXT_LINES), slice(0, PAD), PAD)

        @pl.when(tx + 1 == tx_count)
        def _():
            clear(range(EXT_LINES), slice(PAD + ROWS, ext_rows), PAD)

    @pl.when(no_behind)
    def _():
        clear(behind_lines, every_row, ext_rows)

    @pl.when(no_ahead)
    def _():
        clear(ahead_lines, every_row, ext_rows)

    for f in range(FIELDS):
        for line in range(LINES):
            put(f, STEPS + line, middle, tile[f, line])
    if not wide:
        H[1][1:3, :, ROWS:ext_rows, :] = jnp.zeros((2, EXT_LINES, PAD, LANES), jnp.float32)

    def near(ahead, k):
        return STEPS + LINES + k if ahead else STEPS - 1 - k

    def correct_line(line, rows, ex, ez):
        H[1][0, line, rows, :] = H[1][0, line, rows, :] - ez
        H[1][2, line, rows, :] = H[1][2, line, rows, :] + ex

    def correct_row(line, row, ey, ez):
        at = slice(row, row + 1)
        H[1][1, line, at, :] = H[1][1, line, at, :] + ez
        H[1][2, line, at, :] = H[1][2, line, at, :] - ey

    lower = is_lower_in_a()
    for message, is_lower in ((y_a, lower), (y_b, jnp.logical_not(lower))):
        for ahead in (False, True):

            @pl.when(jnp.logical_and(is_lower == ahead, jnp.logical_not(no_ahead if ahead else no_behind)))
            def _(message=message, ahead=ahead):
                entries = Y_ENTRIES[ahead]
                for i, (f, k) in enumerate(entries):
                    put(f, near(ahead, k), middle, message[i])
                last = len(entries)
                for k in range(4 if ahead else 5):
                    first_row[0, near(ahead, k) : near(ahead, k) + 1, :] = message[last, k : k + 1, :]
                    first_row[1, near(ahead, k) : near(ahead, k) + 1, :] = message[last, 5 + k : 6 + k, :]
                if ahead:
                    correct_line(STEPS + LINES - 1, middle, message[last + 1], message[last + 2])
                else:
                    correct_line(STEPS - 1, middle, start[0, 0], start[2, 0])

    for kind in range(kinds):
        along, same, mixed = messages[3 * kind : 3 * kind + 3]
        for ahead in (False, True):
            in_x = tx + 1 < tx_count if ahead else tx > 0
            halo = tile_row + ROWS if ahead else (PAD if wide else ext_rows)
            last_row = halo - 1

            @pl.when(jnp.logical_and((odd_x == kind) == ahead, in_x))
            def _(ahead=ahead, along=along, same=same, mixed=mixed, halo=halo, last_row=last_row):
                def rows(depth):
                    return slice(halo, halo + depth) if ahead else slice(halo - depth, halo)

                def unpack(message, entries, line_of):
                    for f, k, depth, at in entries[0]:
                        put(f, line_of(k), rows(depth), message[at : at + depth, :])
                    return entries[1]

                def first_line(message, at, depth, line):
                    ex, ez = message[at : at + depth, :], message[at + depth : at + 2 * depth, :]
                    correct_line(line, rows(depth), ex, ez)
                    return at + 2 * depth

                def rows_ahead(message, at, lines):
                    for i, line in enumerate(lines):
                        one, two = at + i, at + len(lines) + i
                        correct_row(line, last_row, message[one : one + 1, :], message[two : two + 1, :])

                def rows_own(lines):
                    for line in lines:
                        correct_row(
                            line,
                            last_row,
                            first_row[0, line : line + 1, :],
                            first_row[1, line : line + 1, :],
                        )

                along_end = unpack(along, X_ENTRIES[ahead], lambda k: STEPS + k)
                if ahead:
                    rows_ahead(along, along_end + 2 * BORDER, range(STEPS, STEPS + LINES))
                else:
                    for line in range(LINES):
                        correct_row(STEPS + line, last_row, start[1, line, 0:1, :], start[2, line, 0:1, :])

                @pl.when(jnp.logical_not(no_behind))
                def _():
                    message, entries = (mixed, MIXED_ENTRIES[True]) if ahead else (same, SAME_ENTRIES[False])
                    at = unpack(message, entries, lambda k: near(False, k))
                    first_line(along, along_end, BORDER, STEPS - 1)
                    if ahead:
                        rows_ahead(message, at, [near(False, k) for k in range(BORDER)])
                    else:
                        rows_own(behind_lines)

                @pl.when(jnp.logical_not(no_ahead))
                def _():
                    message, entries = (same, SAME_ENTRIES[True]) if ahead else (mixed, MIXED_ENTRIES[False])
                    at = unpack(message, entries, lambda k: near(True, k))
                    at = first_line(message, at, 4 if ahead else BORDER, STEPS + LINES - 1)
                    if ahead:
                        rows_ahead(message, at, [near(True, k) for k in range(4)])
                    else:
                        rows_own([near(True, k) for k in range(4)])

    shape = (ext_rows, LANES)
    low = low_lanes(shape)
    row = window_rows(tx_count, shape)
    row_mask = ((row >= 0) & (row < rows_all)).astype(jnp.float32)

    def line_inside(line):
        where = lines_base + line
        return ((where >= 0) & (where < lines_all)).astype(jnp.float32)

    def is_own(line):
        return STEPS <= line < STEPS + LINES

    for line in range(1, EXT_LINES - 1):
        mixed = C[line]
        turned = half_turn(mixed)
        mat = jnp.where(low, mixed, turned)
        dens = jnp.where(low, turned, mixed)
        eps, *others = [
            choose(mat, lambda m, i=i: poles[NMAT * i + m : NMAT * i + m + 1, :]) for i in range(4)
        ]
        reach = time_step * 0.5 / (eps + design[line] * dens)
        if wide:
            reach = reach * row_mask
        if not is_own(line):
            reach = reach * line_inside(line)
        coef[0, line] = reach
        for i, value in enumerate(others):
            coef[1 + i, line] = value

    count = ext_rows // 8
    block = (8, LANES)
    lane = lax.broadcasted_iota(jnp.int32, block, 1)
    depth_id = jnp.where(low[:8], lane, lane - NZ)
    first_z, last_z = depth_id == 0, depth_id == NZ - 1
    sub = lax.broadcasted_iota(jnp.int32, block, 0)
    first_sub, last_sub = sub == 0, sub == 7
    sent = sub + tx * (7 - 2 * sub) < STEPS
    every, own = range(count), range(tile_row // 8, (tile_row + ROWS) // 8)

    def blocks(ref, c, line):
        return [ref[c, line, 8 * b : 8 * b + 8, :] for b in every]

    def ahead_row(v):
        turned = [pltpu.roll(x, 7, 0) for x in v]
        return [jnp.where(last_sub, turned[(b + 1) % count], turned[b]) for b in every]

    def behind_row(v):
        turned = [pltpu.roll(x, 1, 0) for x in v]
        return [jnp.where(first_sub, turned[b - 1], turned[b]) for b in every]

    def ahead_depth(v):
        return jnp.where(last_z, 0.0, pltpu.roll(v, LANES - 1, 1))

    def behind_depth(v):
        return jnp.where(first_z, 0.0, pltpu.roll(v, 1, 1))

    def settle(ref, c, line, b, value):
        if not wide and b not in own:
            value = jnp.where(sent, value, 0.0)
        ref[c, line, 8 * b : 8 * b + 8, :] = value

    def magnetic_line(n, line):
        old, new = H[n % 2], H[(n + 1) % 2]
        ex, ey, ez = [blocks(E[n], c, line) for c in range(3)]
        ex_next, ez_next = blocks(E[n], 0, line + 1), blocks(E[n], 2, line + 1)
        hx, hy, hz = [blocks(old, c, line) for c in range(3)]
        ey_ahead, ez_ahead = ahead_row(ey), ahead_row(ez)
        for b in every:
            curls = (
                (ez_next[b] - ez[b]) - (ahead_depth(ey[b]) - ey[b]),
                (ahead_depth(ex[b]) - ex[b]) - (ez_ahead[b] - ez[b]),
                (ey_ahead[b] - ey[b]) - (ex_next[b] - ex[b]),
            )
            if line < STEPS:
                curls = [curl * line_inside(line) for curl in curls]
            if wide:
                curls = [curl * row_mask[8 * b : 8 * b + 8] for curl in curls]
            for c, h in enumerate((hx, hy, hz)):
                settle(new, c, line, b, h[b] - curls[c])

    def electric_line(n, line):
        field = H[(n + 1) % 2]
        hx, hy, hz = [blocks(field, c, line) for c in range(3)]
        hx_last, hz_last = blocks(field, 0, line - 1), blocks(field, 2, line - 1)
        hy_behind, hz_behind = behind_row(hy), behind_row(hz)
        for b in every if n + 1 < STEPS else own:
            rows = slice(8 * b, 8 * b + 8)
            curls = (
                (hz[b] - hz_last[b]) - (hy[b] - behind_depth(hy[b])),
                (hx[b] - behind_depth(hx[b])) - (hz[b] - hz_behind[b]),
                (hy[b] - hy_behind[b]) - (hx[b] - hx_last[b]),
            )
            reach = coef[0, line, rows, :]
            for c in range(3):
                e = E[n][c, line, rows, :]
                curl = curls[c]
                if n > 0:
                    p, j = Pol[(n + 1) % 2][c, line, rows, :], J[(n + 1) % 2][c, line, rows, :]
                    if n == 1:
                        j = j + coef[3, line, rows, :] * e
                    else:
                        j = coef[1, line, rows, :] * j + coef[3, line, rows, :] * e - coef[2, line, rows, :] * p
                    if n < STEPS - 1:
                        J[n % 2][c, line, rows, :] = j
                        Pol[n % 2][c, line, rows, :] = p + j
                    curl = curl - j
                drawn = source_rows[rows, :] * sources[n, c, line : line + 1, :]
                settle(E[n + 1], c, line, b, e + reach * (curl - drawn))

    for n in range(STEPS):
        for line in range(n, EXT_LINES - 1 - n) if n > 0 else ():
            magnetic_line(n, line)
        for line in range(n + 1, EXT_LINES - 1 - n):
            electric_line(n, line)

    low_tile = low[:ROWS]

    def turned(line):
        return [[half_turn(E[n][c, line, middle, :]) for n in (5, 4, 3)] for c in range(3)]

    totals, following = [], turned(STEPS)
    for own_line in range(LINES):
        line, (x, y, z) = STEPS + own_line, following
        if own_line + 1 < LINES:
            following = turned(line + 1)
        terms = []
        for c, (five, four, three) in enumerate((x, y, z)):
            one, two = E[1][c, line, middle, :], E[2][c, line, middle, :]
            zero_low = jnp.where(low_tile, start[c, own_line], 0.0)
            three_low = jnp.where(low_tile, E[3][c, line, middle, :], 0.0)
            terms.append(five * (one - zero_low) + four * (two - one) + three * (three_low - two))
            electric_out[c, own_line] = E[STEPS][c, line, middle, :]
        totals.append((terms[0] + terms[1] + terms[2]) * design[line, middle, :])
    folded = [total + half_turn(total) for total in totals]
    for k in range(CHUNKS):
        gradient_out[:, k * LANES : (k + 1) * LANES] = jnp.where(low_tile, folded[2 * k], folded[2 * k + 1])


def emit_kernel(electric, out):
    low = low_lanes((ROWS, LANES))
    for k in range(CHUNKS):
        at = slice(k * LANES, (k + 1) * LANES)
        for c in range(3):
            one, two = electric[c, 2 * k], electric[c, 2 * k + 1]
            out[0, 0, c, :, at] = jnp.where(low, one, half_turn(two))
            out[0, 1, c, :, at] = jnp.where(low, half_turn(one), two)


def pair_of(index, kind, count):
    other = index + 1 if index % 2 == kind else index - 1
    return other if 0 <= other < count else None


def f32(*shape):
    return jax.ShapeDtypeStruct(shape, jnp.float32)


def in_hbm(value):
    return pltpu.with_memory_space_constraint(value, pltpu.HBM)


def on_device(
    tx_count,
    ty_count,
    initial_fields,
    source_profiles,
    source_waveforms,
    material_map,
    design_density,
    material_table,
    plane_indices,
    design_box,
):
    hbm = pl.BlockSpec(memory_space=pltpu.HBM)
    vmem = pl.BlockSpec(memory_space=pltpu.VMEM)
    kinds = (0,) if tx_count == 2 else (0, 1)

    waves = lax.axis_size("wave")

    def swap(value, partner):
        def index(w, x, y):
            return (w * tx_count + x) * ty_count + y

        pairs = []
        for w in range(waves):
            for x in range(tx_count):
                for y in range(ty_count):
                    ox, oy = partner(w, x, y)
                    if ox is not None and oy is not None and 0 <= oy < ty_count:
                        pairs.append((index(w, x, y), index(w, ox, oy)))
                    elif waves % 2 == 0:
                        pairs.append((index(w, x, y), index(w ^ 1, x, y)))
        return lax.ppermute(value, ("wave", "tx", "ty"), pairs)

    def along_y(b):
        return lambda w, x, y: (x, pair_of(y, b, ty_count))

    def along_x(kind):
        return lambda w, x, y: (pair_of(x, kind, tx_count), y)

    def corner(kind, mixed):
        return lambda w, x, y: (pair_of(x, kind, tx_count), y + (1 if (x % 2 == kind) != mixed else -1))

    tile, start, y_a, y_b = pl.pallas_call(
        pack_kernel,
        out_shape=(
            f32(FIELDS, LINES, ROWS, LANES),
            f32(3, LINES, ROWS, LANES),
            f32(Y_SIZE, ROWS, LANES),
            f32(Y_SIZE, ROWS, LANES),
        ),
        in_specs=[hbm] * 5,
        out_specs=(vmem,) * 4,
        scratch_shapes=[
            pltpu.SMEM((NMAT, 4), jnp.float32),
            pltpu.SMEM((6,), jnp.int32),
            pltpu.VMEM((CHUNKS, 2, 12, ROWS, LANES), jnp.float32),
            pltpu.VMEM((ROWS, LINES * NZ), jnp.int32),
            pltpu.VMEM((ROWS, LINES * NZ), jnp.float32),
            pltpu.SemaphoreType.DMA((CHUNKS + 4,)),
        ],
        compiler_params=pltpu.CompilerParams(vmem_limit_bytes=32 * 1024 * 1024),
        name="pack",
    )(*[in_hbm(v) for v in (material_table, design_box, initial_fields, material_map, design_density)])
    y_a, y_b = swap(y_a, along_y(0)), swap(y_b, along_y(1))

    sizes = (X_SIZE, SAME_SIZE, MIXED_SIZE) * len(kinds)
    messages = pl.pallas_call(
        edge_kernel,
        out_shape=[f32(size, LANES) for size in sizes],
        in_specs=[vmem, vmem],
        out_specs=[vmem] * len(sizes),
        compiler_params=pltpu.CompilerParams(vmem_limit_bytes=32 * 1024 * 1024),
        name="edges",
    )(tile, start)
    arrived = []
    for i, message in enumerate(messages):
        kind = i // 3
        arrived.append(swap(message, along_x(kind) if i % 3 == 0 else corner(kind, i % 3 == 2)))

    ext = (EXT_LINES, ROWS + (PAD if tx_count == 2 else 2 * PAD), LANES)
    prepared = pl.pallas_call(
        functools.partial(prepare_kernel, tx_count, ty_count),
        out_shape=(f32(STEPS, 3, EXT_LINES + 6, LANES), f32(*ext[1:]), f32(*ext), f32(16, LANES)),
        in_specs=[hbm] * 4 + [vmem],
        out_specs=(vmem,) * 4,
        scratch_shapes=[
            pltpu.SMEM((2, STEPS), jnp.float32),
            pltpu.SMEM((NMAT, 4), jnp.float32),
            pltpu.SMEM((2,), jnp.int32),
            pltpu.SMEM((6,), jnp.int32),
            pltpu.SemaphoreType.DMA((4,)),
        ],
        compiler_params=pltpu.CompilerParams(vmem_limit_bytes=16 * 1024 * 1024),
        name="prepare",
    )(
        *[in_hbm(v) for v in (source_waveforms[0], material_table, plane_indices, design_box)],
        source_profiles[0].transpose(1, 0, 2),
    )
    electric, partial = pl.pallas_call(
        functools.partial(window_kernel, tx_count, ty_count),
        out_shape=(f32(3, LINES, ROWS, LANES), f32(ROWS, LINES * NZ)),
        in_specs=[vmem] * (8 + len(arrived)),
        out_specs=(vmem, vmem),
        scratch_shapes=[
            [pltpu.VMEM((3,) + ext, jnp.float32) for _ in range(STEPS + 1)],
            [pltpu.VMEM((3,) + ext, jnp.float32) for _ in range(2)],
            [pltpu.VMEM((3,) + ext, jnp.float32) for _ in range(2)],
            [pltpu.VMEM((3,) + ext, jnp.float32) for _ in range(2)],
            pltpu.VMEM(ext, jnp.float32),
            pltpu.VMEM((4,) + ext, jnp.float32),
            pltpu.VMEM((2, EXT_LINES + 6, LANES), jnp.float32),
        ],
        compiler_params=pltpu.CompilerParams(vmem_limit_bytes=48 * 1024 * 1024),
        name="window",
    )(
        *prepared,
        tile,
        start,
        y_a,
        y_b,
        *arrived,
    )
    final = pl.pallas_call(
        emit_kernel,
        out_shape=f32(1, 2, 3, ROWS, LINES * NZ),
        in_specs=[vmem],
        out_specs=vmem,
        compiler_params=pltpu.CompilerParams(vmem_limit_bytes=8 * 1024 * 1024),
        name="emit",
    )(electric)

    if lax.axis_size("wave") == 4:
        one, two, three = [
            lax.ppermute(partial, "wave", [(i, i ^ k) for i in range(4)]) for k in (1, 2, 3)
        ]
        gradient = (partial + one) + (two + three)
    else:
        gradient = lax.psum(partial, "wave")
    return gradient, final


def solution(mesh):
    placed = (
        P("wave", None, None, "tx", "ty"),
        P("wave", None, None, None),
        P("wave", None, None),
        P("tx", "ty"),
        P("tx", "ty"),
        P(),
        P(),
        P(),
    )
    return jax.shard_map(
        functools.partial(on_device, mesh.shape["tx"], mesh.shape["ty"]),
        mesh=mesh,
        in_specs=placed,
        out_specs=(P("tx", "ty"), P("wave", None, None, "tx", "ty")),
        check_vma=False,
    )
```

```python
import functools

import jax
import jax.numpy as jnp
from jax import lax
from jax.experimental import pallas as pl
from jax.experimental.pallas import tpu as pltpu
from jax.sharding import PartitionSpec as P

NZ = 64
STEPS = 5
NMAT = 3
LANES = 2 * NZ
ROWS = 16
LINES = 8
CHUNKS = LINES // 2
PAD = 8
EXT_LINES = LINES + 2 * STEPS
FIELDS = 13

time_step = 0.5
contrast = 2.0

BEHIND_LINES = (4, 4, 4, 5, 4, 5, 2, 2, 2, 3, 3, 3, 4)
AHEAD_LINES = (4, 3, 4, 4, 4, 4, 2, 1, 2, 3, 2, 3, 4)
BEHIND_ROWS = (4, 4, 4, 4, 5, 5, 2, 2, 2, 3, 3, 3, 4)
AHEAD_ROWS = (3, 4, 4, 4, 4, 4, 1, 2, 2, 2, 3, 3, 4)
BEHIND_BOTH = (3, 3, 3, 4, 4, 4, 1, 1, 1, 2, 2, 2, 3)
AHEAD_BOTH = (3, 3, 3, 3, 3, 3, 1, 1, 1, 2, 2, 2, 3)
AHEAD_ROW_BEHIND_LINE = (3, 4, 3, 4, 3, 4, 1, 2, 1, 2, 3, 2, 4)
BEHIND_ROW_AHEAD_LINE = (4, 3, 3, 3, 4, 4, 2, 1, 1, 3, 2, 2, 4)
BORDER = 5


def line_entries(depth):
    return [(f, k) for f in range(FIELDS) for k in range(depth[f])]


def row_entries(entries):
    start, out = 0, []
    for f, k, depth in entries:
        out.append((f, k, depth, start))
        start += depth
    return out, start


def corner_entries(depth):
    return row_entries([(f, k, depth[f] - k) for f in range(FIELDS) for k in range(depth[f])])


Y_ENTRIES = {False: line_entries(BEHIND_LINES), True: line_entries(AHEAD_LINES)}
Y_SIZE = max(len(Y_ENTRIES[False]) + 1, len(Y_ENTRIES[True]) + 3)
X_ENTRIES = {
    ahead: row_entries([(f, line, depth[f]) for f in range(FIELDS) for line in range(LINES)])
    for ahead, depth in ((False, BEHIND_ROWS), (True, AHEAD_ROWS))
}
SAME_ENTRIES = {False: corner_entries(BEHIND_BOTH), True: corner_entries(AHEAD_BOTH)}
MIXED_ENTRIES = {False: corner_entries(BEHIND_ROW_AHEAD_LINE), True: corner_entries(AHEAD_ROW_BEHIND_LINE)}


def round_up(n):
    return (n + 7) // 8 * 8


X_SIZE = round_up(max(X_ENTRIES[False][1] + 2 * BORDER, X_ENTRIES[True][1] + 2 * BORDER + 2 * LINES))
SAME_SIZE = round_up(max(SAME_ENTRIES[False][1], SAME_ENTRIES[True][1] + 16))
MIXED_SIZE = round_up(max(MIXED_ENTRIES[ahead][1] + 2 * BORDER for ahead in (False, True)))


def low_lanes(shape):
    return lax.broadcasted_iota(jnp.int32, shape, len(shape) - 1) < NZ


def half_turn(v):
    return pltpu.roll(v, NZ, v.ndim - 1)


def choose(material, column):
    values = [column(m) for m in range(NMAT)]
    return jnp.where(material < 0.5, values[0], jnp.where(material < 1.5, values[1], values[2]))


def pole(table):
    out = []
    for m in range(NMAT):
        d, w, g = table[m, 1], table[m, 2], table[m, 3]
        denom = 1.0 + 0.25 * g
        drive = w * w * time_step / denom
        out.append(((1.0 - 0.25 * g) / denom, drive * 0.5, drive * d * 2.0))
    return [lambda m, i=i: out[m][i] for i in range(3)]


def is_lower_in_a():
    return lax.rem(lax.axis_index("ty"), 2) == 0


def pack_kernel(
    table_hbm,
    box_hbm,
    fields_hbm,
    material_hbm,
    density_hbm,
    tile,
    start,
    y_a,
    y_b,
    table,
    box,
    fields,
    material,
    density,
    sems,
):
    copies = [
        pltpu.make_async_copy(src, dst, sems.at[CHUNKS + i])
        for i, (src, dst) in enumerate(
            [(table_hbm, table), (box_hbm, box), (material_hbm, material), (density_hbm, density)]
        )
    ]
    chunks = [
        pltpu.make_async_copy(fields_hbm.at[0, :, :, pl.ds(8 * b, 8), :], fields.at[b], sems.at[b])
        for b in range(ROWS // 8)
    ]
    for copy in copies + chunks:
        copy.start()
    for copy in copies:
        copy.wait()
    decay, drive, coupled = pole(table)
    block = (8, LANES)
    low = low_lanes(block)
    lane = lax.broadcasted_iota(jnp.int32, block, 1)
    depth_id = jnp.where(low, lane, lane - NZ)
    last_z = (jnp.concatenate([depth_id, depth_id], axis=0) == NZ - 1)
    in_z = (depth_id >= box[4]) & (depth_id < box[5])
    first_line = lax.axis_index("ty") * LINES

    def split(one, two):
        return jnp.where(low, one, half_turn(two)), jnp.where(low, half_turn(one), two)

    for b in range(ROWS // 8):
        rows = slice(8 * b, 8 * b + 8)
        row = lax.broadcasted_iota(jnp.int32, block, 0) + (lax.axis_index("tx") * ROWS + 8 * b)
        design_rows = ((row >= box[0]) & (row < box[1]) & in_z).astype(jnp.float32)
        chunks[b].wait()
        for k in range(CHUNKS):
            at = slice(k * LANES, (k + 1) * LANES)
            pairs = [split(fields[b, 0, f, :, at], fields[b, 1, f, :, at]) for f in range(12)]
            mat, dens = material[rows, at].astype(jnp.float32), density[rows, at]
            turned = half_turn(mat)
            mats = (jnp.where(low, mat, turned), jnp.where(low, turned, mat))
            turned = half_turn(dens)
            denses = (jnp.where(low, dens, turned), jnp.where(low, turned, dens))
            for half in range(2):
                line = 2 * k + half
                mat, dens = mats[half], denses[half]
                where = first_line + line
                design = design_rows * ((where >= box[2]) & (where < box[3])).astype(jnp.float32)
                permittivity = choose(mat, lambda m: table[m, 0]) + design * dens * contrast
                reach = time_step * 0.5 / permittivity
                dec, dri, cou = [choose(mat, column) for column in (decay, drive, coupled)]
                for c in range(3):
                    e, p, j = pairs[c][half], 4.0 * pairs[6 + c][half], 2.0 * pairs[9 + c][half]
                    j = dec * j + cou * e - dri * p
                    p = p + j
                    start[c, line, rows, :] = e
                    tile[c, line, rows, :] = e - reach * j
                    tile[3 + c, line, rows, :] = 2.0 * pairs[3 + c][half]
                    tile[6 + c, line, rows, :] = p
                    tile[9 + c, line, rows, :] = dec * j - dri * p
                tile[12, line, rows, :] = jnp.where(low, mat, dens)

    edge = jnp.zeros((1, LANES), jnp.float32)

    def ahead_row(v):
        return jnp.concatenate([v[1:], edge], axis=0)

    def ahead_depth(v):
        return jnp.where(last_z, 0.0, pltpu.roll(v, LANES - 1, 1))

    for line in range(LINES):
        ex, ey, ez = [start[c, line] for c in range(3)]
        if line + 1 < LINES:
            ex_next, ez_next = start[0, line + 1], start[2, line + 1]
        else:
            ex_next = ez_next = jnp.zeros((ROWS, LANES), jnp.float32)
        tile[3, line] = tile[3, line] - ((ez_next - ez) - (ahead_depth(ey) - ey))
        tile[4, line] = tile[4, line] - ((ahead_depth(ex) - ex) - (ahead_row(ez) - ez))
        tile[5, line] = tile[5, line] - ((ahead_row(ey) - ey) - (ex_next - ex))

    lower = is_lower_in_a()
    for message, is_lower in ((y_a, lower), (y_b, jnp.logical_not(lower))):
        for ahead in (False, True):

            @pl.when(is_lower != ahead)
            def _(message=message, ahead=ahead):
                def line_of(k):
                    return k if ahead else LINES - 1 - k

                entries = Y_ENTRIES[ahead]
                for i, (f, k) in enumerate(entries):
                    message[i] = tile[f, line_of(k)]
                last = len(entries)
                for k in range(4 if ahead else 5):
                    message[last, k : k + 1, :] = start[1, line_of(k), 0:1, :]
                    message[last, 5 + k : 6 + k, :] = start[2, line_of(k), 0:1, :]
                if ahead:
                    message[last + 1] = start[0, 0]
                    message[last + 2] = start[2, 0]


def edge_kernel(tile, start, *messages):
    odd = lax.rem(lax.axis_index("tx"), 2)
    for kind in range(len(messages) // 3):
        along, same, mixed = messages[3 * kind : 3 * kind + 3]
        for ahead in (False, True):

            @pl.when((odd == kind) != ahead)
            def _(ahead=ahead, along=along, same=same, mixed=mixed):
                def rows(depth):
                    return slice(0, depth) if ahead else slice(ROWS - depth, ROWS)

                def pack(message, entries, line_of):
                    for f, k, depth, at in entries[0]:
                        message[at : at + depth, :] = tile[f, line_of(k), rows(depth), :]
                    return entries[1]

                def pack_first_line(message, at, depth):
                    for c in (0, 2):
                        message[at : at + depth, :] = start[c, 0, rows(depth), :]
                        at += depth
                    return at

                def pack_first_row(message, at, lines):
                    for c in (1, 2):
                        for line in lines:
                            message[at : at + 1, :] = start[c, line, 0:1, :]
                            at += 1

                at = pack(along, X_ENTRIES[ahead], lambda k: k)
                at = pack_first_line(along, at, BORDER)
                if ahead:
                    pack_first_row(along, at, range(LINES))
                at = pack(same, SAME_ENTRIES[ahead], lambda k: k if ahead else LINES - 1 - k)
                if ahead:
                    at = pack_first_line(same, at, 4)
                    pack_first_row(same, at, range(4))
                at = pack(mixed, MIXED_ENTRIES[ahead], lambda k: LINES - 1 - k if ahead else k)
                if ahead:
                    pack_first_row(mixed, at, [LINES - 1 - k for k in range(BORDER)])
                else:
                    pack_first_line(mixed, at, BORDER)


def prepare_kernel(
    tx_count,
    ty_count,
    waveforms_hbm,
    table_hbm,
    plane_hbm,
    box_hbm,
    profiles,
    sources,
    source_rows,
    design,
    poles,
    waveforms,
    table,
    plane,
    box,
    sems,
):
    copies = [
        pltpu.make_async_copy(src, dst, sems.at[i])
        for i, (src, dst) in enumerate(
            [(waveforms_hbm, waveforms), (table_hbm, table), (plane_hbm, plane), (box_hbm, box)]
        )
    ]
    for copy in copies:
        copy.start()
    for copy in copies:
        copy.wait()
    tx, ty = lax.axis_index("tx"), lax.axis_index("ty")
    shape = source_rows.shape
    low = low_lanes(shape)
    lane = lax.broadcasted_iota(jnp.int32, shape, 1)
    depth_id = jnp.where(low, lane, lane - NZ)
    row = window_rows(tx_count, shape)
    source_rows[...] = (row == jnp.where(low, plane[0], plane[1])).astype(jnp.float32)
    in_z = (depth_id >= box[4]) & (depth_id < box[5])
    design_rows = ((row >= box[0]) & (row < box[1]) & in_z).astype(jnp.float32) * contrast
    for line in range(1, EXT_LINES - 1):
        where = ty * LINES - STEPS + line
        design[line] = design_rows * ((where >= box[2]) & (where < box[3])).astype(jnp.float32)
    for i, column in enumerate((lambda m: table[m, 0], *pole(table))):
        for m in range(NMAT):
            at = NMAT * i + m
            poles[at : at + 1, :] = jnp.full((1, LANES), column(m), jnp.float32)
    low_row = low[:1]
    weights = [2.0 * jnp.where(low_row, waveforms[0, n], waveforms[1, n]) for n in range(STEPS)]
    for i in range(EXT_LINES // 2 - 1):
        chunk = jnp.clip(ty * CHUNKS + i - STEPS // 2, 0, ty_count * CHUNKS - 1)
        for c in range(3):
            both = profiles[c, :, pl.ds(pl.multiple_of(chunk * LANES, LANES), LANES)]
            one, two = both[0:1], both[1:2]
            first = jnp.where(low_row, one, half_turn(two))
            second = jnp.where(low_row, half_turn(one), two)
            for n in range(STEPS):
                sources[n, c, 2 * i + 1 : 2 * i + 2, :] = weights[n] * first
                sources[n, c, 2 * i + 2 : 2 * i + 3, :] = weights[n] * second


def window_rows(tx_count, shape):
    tx = lax.axis_index("tx")
    at = lax.broadcasted_iota(jnp.int32, shape, 0)
    if tx_count == 2:
        return at + tx * ROWS - jnp.where(at >= ROWS, tx * (ROWS + PAD), 0)
    return at + tx * ROWS - PAD


def window_part(early, late, tx_count, ty_count, *refs):
    *most, one, two = refs
    window_kernel(early, late, tx_count, ty_count, *most, (one, two))


def window_kernel(early, late, tx_count, ty_count, *refs):
    kinds = 1 if tx_count == 2 else 2
    refs = list(refs)
    sources, source_rows, design, poles, start = [refs.pop(0) for _ in range(5)]
    tile, y_a, y_b = [refs.pop(0) for _ in range(3)] if early else (None,) * 3
    messages = [refs.pop(0) for _ in range(3 * kinds)] if late else []
    if late and not early:
        refs.pop(0)
    electric_out, gradient_out = [refs.pop(0) for _ in range(2)] if late else (None, None)
    (E, H, Pol, J, C, coef, first_row), (Pol_next, J_next) = refs if len(refs) == 2 else (refs[:-1], refs[-1])
    H = [None] + list(H)
    Pol, J = (Pol, Pol_next), (J, J_next)
    wide = tx_count != 2
    ext_rows = E[0].shape[2]
    tx, ty = lax.axis_index("tx"), lax.axis_index("ty")
    odd_x = lax.rem(tx, 2)
    tile_row = PAD if wide else 0
    lines_base = ty * LINES - STEPS
    rows_all, lines_all = tx_count * ROWS, ty_count * LINES
    middle = slice(tile_row, tile_row + ROWS)

    def put(f, line, rows, value):
        if f < 12:
            (E[0], H[1], Pol[0], J[0])[f // 3][f % 3, line, rows, :] = value
        else:
            C[line, rows, :] = value

    def clear(lines, rows, count):
        for f in range(FIELDS):
            for line in lines:
                put(f, line, rows, jnp.zeros((count, LANES), jnp.float32))

    every_row = slice(0 if early else ROWS, ext_rows if late else ROWS)
    row_count = every_row.stop - every_row.start
    behind_lines, ahead_lines = range(STEPS), range(STEPS + LINES, EXT_LINES)
    no_behind, no_ahead = ty == 0, ty + 1 == ty_count
    if wide:

        @pl.when(tx == 0)
        def _():
            clear(range(EXT_LINES), slice(0, PAD), PAD)

        @pl.when(tx + 1 == tx_count)
        def _():
            clear(range(EXT_LINES), slice(PAD + ROWS, ext_rows), PAD)

    @pl.when(no_behind)
    def _():
        clear(behind_lines, every_row, row_count)

    @pl.when(no_ahead)
    def _():
        clear(ahead_lines, every_row, row_count)

    if early:
        for f in range(FIELDS):
            for line in range(LINES):
                put(f, STEPS + line, middle, tile[f, line])
    if late and not wide:
        H[1][1:3, :, ROWS:ext_rows, :] = jnp.zeros((2, EXT_LINES, PAD, LANES), jnp.float32)

    def near(ahead, k):
        return STEPS + LINES + k if ahead else STEPS - 1 - k

    def correct_line(line, rows, ex, ez):
        H[1][0, line, rows, :] = H[1][0, line, rows, :] - ez
        H[1][2, line, rows, :] = H[1][2, line, rows, :] + ex

    def correct_row(line, row, ey, ez):
        at = slice(row, row + 1)
        H[1][1, line, at, :] = H[1][1, line, at, :] + ez
        H[1][2, line, at, :] = H[1][2, line, at, :] - ey

    lower = is_lower_in_a()
    for message, is_lower in ((y_a, lower), (y_b, jnp.logical_not(lower))) if early else ():
        for ahead in (False, True):

            @pl.when(jnp.logical_and(is_lower == ahead, jnp.logical_not(no_ahead if ahead else no_behind)))
            def _(message=message, ahead=ahead):
                entries = Y_ENTRIES[ahead]
                for i, (f, k) in enumerate(entries):
                    put(f, near(ahead, k), middle, message[i])
                last = len(entries)
                for k in range(4 if ahead else 5):
                    first_row[0, near(ahead, k) : near(ahead, k) + 1, :] = message[last, k : k + 1, :]
                    first_row[1, near(ahead, k) : near(ahead, k) + 1, :] = message[last, 5 + k : 6 + k, :]
                if ahead:
                    correct_line(STEPS + LINES - 1, middle, message[last + 1], message[last + 2])
                else:
                    correct_line(STEPS - 1, middle, start[0, 0], start[2, 0])

    for kind in range(kinds if late else 0):
        along, same, mixed = messages[3 * kind : 3 * kind + 3]
        for ahead in (False, True):
            in_x = tx + 1 < tx_count if ahead else tx > 0
            halo = tile_row + ROWS if ahead else (PAD if wide else ext_rows)
            last_row = halo - 1

            @pl.when(jnp.logical_and((odd_x == kind) == ahead, in_x))
            def _(ahead=ahead, along=along, same=same, mixed=mixed, halo=halo, last_row=last_row):
                def rows(depth):
                    return slice(halo, halo + depth) if ahead else slice(halo - depth, halo)

                def unpack(message, entries, line_of):
                    for f, k, depth, at in entries[0]:
                        put(f, line_of(k), rows(depth), message[at : at + depth, :])
                    return entries[1]

                def first_line(message, at, depth, line):
                    ex, ez = message[at : at + depth, :], message[at + depth : at + 2 * depth, :]
                    correct_line(line, rows(depth), ex, ez)
                    return at + 2 * depth

                def rows_ahead(message, at, lines):
                    for i, line in enumerate(lines):
                        one, two = at + i, at + len(lines) + i
                        correct_row(line, last_row, message[one : one + 1, :], message[two : two + 1, :])

                def rows_own(lines):
                    for line in lines:
                        correct_row(
                            line,
                            last_row,
                            first_row[0, line : line + 1, :],
                            first_row[1, line : line + 1, :],
                        )

                along_end = unpack(along, X_ENTRIES[ahead], lambda k: STEPS + k)
                if ahead:
                    rows_ahead(along, along_end + 2 * BORDER, range(STEPS, STEPS + LINES))
                else:
                    for line in range(LINES):
                        correct_row(STEPS + line, last_row, start[1, line, 0:1, :], start[2, line, 0:1, :])

                @pl.when(jnp.logical_not(no_behind))
                def _():
                    message, entries = (mixed, MIXED_ENTRIES[True]) if ahead else (same, SAME_ENTRIES[False])
                    at = unpack(message, entries, lambda k: near(False, k))
                    first_line(along, along_end, BORDER, STEPS - 1)
                    if ahead:
                        rows_ahead(message, at, [near(False, k) for k in range(BORDER)])
                    else:
                        rows_own(behind_lines)

                @pl.when(jnp.logical_not(no_ahead))
                def _():
                    message, entries = (same, SAME_ENTRIES[True]) if ahead else (mixed, MIXED_ENTRIES[False])
                    at = unpack(message, entries, lambda k: near(True, k))
                    at = first_line(message, at, 4 if ahead else BORDER, STEPS + LINES - 1)
                    if ahead:
                        rows_ahead(message, at, [near(True, k) for k in range(4)])
                    else:
                        rows_own([near(True, k) for k in range(4)])

    shape = (row_count, LANES)
    low = low_lanes(shape)
    row = window_rows(tx_count, (ext_rows, LANES))
    row_mask = ((row >= 0) & (row < rows_all)).astype(jnp.float32)

    def line_inside(line):
        where = lines_base + line
        return ((where >= 0) & (where < lines_all)).astype(jnp.float32)

    def is_own(line):
        return STEPS <= line < STEPS + LINES

    for line in range(1, EXT_LINES - 1):
        mixed = C[line, every_row, :]
        turned = half_turn(mixed)
        mat = jnp.where(low, mixed, turned)
        dens = jnp.where(low, turned, mixed)
        eps, *others = [
            choose(mat, lambda m, i=i: poles[NMAT * i + m : NMAT * i + m + 1, :]) for i in range(4)
        ]
        reach = time_step * 0.5 / (eps + design[line, every_row, :] * dens)
        if wide:
            reach = reach * row_mask
        if not is_own(line):
            reach = reach * line_inside(line)
        coef[0, line, every_row, :] = reach
        for i, value in enumerate(others):
            coef[1 + i, line, every_row, :] = value

    count = ext_rows // 8
    block = (8, LANES)
    lane = lax.broadcasted_iota(jnp.int32, block, 1)
    depth_id = jnp.where(low_lanes(block), lane, lane - NZ)
    first_z, last_z = depth_id == 0, depth_id == NZ - 1
    sub = lax.broadcasted_iota(jnp.int32, block, 0)
    first_sub, last_sub = sub == 0, sub == 7
    sent = sub + tx * (7 - 2 * sub) < STEPS
    own = range(tile_row // 8, (tile_row + ROWS) // 8)
    if early:
        made = {b: ((b - 1) % count, (b + 1) % count) for b in (range(count) if late else own)}
        own_made = list(own)
    else:
        beside = 1 - tx
        made = {2: (1, 0), "beside": (lax.rem(beside + 2, 3), beside + 1)}
        own_made = ["beside"]

    def rows_of(b):
        if isinstance(b, int):
            return slice(8 * b, 8 * b + 8)
        return pl.ds(pl.multiple_of(8 * (beside if isinstance(b, str) else b), 8), 8)

    def block_of(ref, c, line, b):
        if isinstance(b, int) and not late and b not in own:
            return jnp.zeros(block, jnp.float32)
        return ref[c, line, rows_of(b), :]

    def blocks(ref, c, line):
        return {b: block_of(ref, c, line, b) for b in made}

    def ahead_row(ref, c, line, v):
        return {
            b: jnp.where(last_sub, pltpu.roll(block_of(ref, c, line, made[b][1]), 7, 0), pltpu.roll(v[b], 7, 0))
            for b in made
        }

    def behind_row(ref, c, line, v):
        return {
            b: jnp.where(first_sub, pltpu.roll(block_of(ref, c, line, made[b][0]), 1, 0), pltpu.roll(v[b], 1, 0))
            for b in made
        }

    def ahead_depth(v):
        return jnp.where(last_z, 0.0, pltpu.roll(v, LANES - 1, 1))

    def behind_depth(v):
        return jnp.where(first_z, 0.0, pltpu.roll(v, 1, 1))

    def settle(ref, c, line, b, value):
        if not wide and isinstance(b, int) and b not in own:
            value = jnp.where(sent, value, 0.0)
        ref[c, line, rows_of(b), :] = value

    def magnetic_line(n, line):
        ex, ey, ez = [blocks(E[n], c, line) for c in range(3)]
        ex_next, ez_next = blocks(E[n], 0, line + 1), blocks(E[n], 2, line + 1)
        hx, hy, hz = [blocks(H[n], c, line) for c in range(3)]
        ey_ahead, ez_ahead = ahead_row(E[n], 1, line, ey), ahead_row(E[n], 2, line, ez)
        for b in made:
            curls = (
                (ez_next[b] - ez[b]) - (ahead_depth(ey[b]) - ey[b]),
                (ahead_depth(ex[b]) - ex[b]) - (ez_ahead[b] - ez[b]),
                (ey_ahead[b] - ey[b]) - (ex_next[b] - ex[b]),
            )
            if line < STEPS:
                curls = [curl * line_inside(line) for curl in curls]
            if wide:
                curls = [curl * row_mask[8 * b : 8 * b + 8] for curl in curls]
            for c, h in enumerate((hx, hy, hz)):
                settle(H[n + 1], c, line, b, h[b] - curls[c])

    def electric_line(n, line):
        field = H[n + 1]
        hx, hy, hz = [blocks(field, c, line) for c in range(3)]
        hx_last, hz_last = blocks(field, 0, line - 1), blocks(field, 2, line - 1)
        hy_behind, hz_behind = behind_row(field, 1, line, hy), behind_row(field, 2, line, hz)
        for b in made if n + 1 < STEPS else own_made:
            rows = rows_of(b)
            curls = (
                (hz[b] - hz_last[b]) - (hy[b] - behind_depth(hy[b])),
                (hx[b] - behind_depth(hx[b])) - (hz[b] - hz_behind[b]),
                (hy[b] - hy_behind[b]) - (hx[b] - hx_last[b]),
            )
            reach = coef[0, line, rows, :]
            for c in range(3):
                e = E[n][c, line, rows, :]
                curl = curls[c]
                if n > 0:
                    held = 0 if n == 1 else 1
                    p, j = Pol[held][c, line, rows, :], J[held][c, line, rows, :]
                    if n == 1:
                        j = j + coef[3, line, rows, :] * e
                    else:
                        j = coef[1, line, rows, :] * j + coef[3, line, rows, :] * e - coef[2, line, rows, :] * p
                    if n < STEPS - 1:
                        J[1][c, line, rows, :] = j
                        Pol[1][c, line, rows, :] = p + j
                    curl = curl - j
                drawn = source_rows[rows, :] * sources[n, c, line : line + 1, :]
                settle(E[n + 1], c, line, b, e + reach * (curl - drawn))

    for n in range(STEPS):
        for line in range(n, EXT_LINES - 1 - n) if n > 0 else ():
            magnetic_line(n, line)
        for line in range(n + 1, EXT_LINES - 1 - n):
            electric_line(n, line)

    if not late:
        return

    low_tile = low_lanes((ROWS, LANES))

    def turned(line):
        return [[half_turn(E[n][c, line, middle, :]) for n in (5, 4, 3)] for c in range(3)]

    totals, following = [], turned(STEPS)
    for own_line in range(LINES):
        line, (x, y, z) = STEPS + own_line, following
        if own_line + 1 < LINES:
            following = turned(line + 1)
        terms = []
        for c, (five, four, three) in enumerate((x, y, z)):
            one, two = E[1][c, line, middle, :], E[2][c, line, middle, :]
            zero_low = jnp.where(low_tile, start[c, own_line], 0.0)
            three_low = jnp.where(low_tile, E[3][c, line, middle, :], 0.0)
            terms.append(five * (one - zero_low) + four * (two - one) + three * (three_low - two))
            electric_out[c, own_line] = E[STEPS][c, line, middle, :]
        totals.append((terms[0] + terms[1] + terms[2]) * design[line, middle, :])
    folded = [total + half_turn(total) for total in totals]
    for k in range(CHUNKS):
        gradient_out[:, k * LANES : (k + 1) * LANES] = jnp.where(low_tile, folded[2 * k], folded[2 * k + 1])


def emit_kernel(electric, out):
    low = low_lanes((ROWS, LANES))
    for k in range(CHUNKS):
        at = slice(k * LANES, (k + 1) * LANES)
        for c in range(3):
            one, two = electric[c, 2 * k], electric[c, 2 * k + 1]
            out[0, 0, c, :, at] = jnp.where(low, one, half_turn(two))
            out[0, 1, c, :, at] = jnp.where(low, half_turn(one), two)


def pair_of(index, kind, count):
    other = index + 1 if index % 2 == kind else index - 1
    return other if 0 <= other < count else None


def f32(*shape):
    return jax.ShapeDtypeStruct(shape, jnp.float32)


def in_hbm(value):
    return pltpu.with_memory_space_constraint(value, pltpu.HBM)


def on_device(
    tx_count,
    ty_count,
    initial_fields,
    source_profiles,
    source_waveforms,
    material_map,
    design_density,
    material_table,
    plane_indices,
    design_box,
):
    hbm = pl.BlockSpec(memory_space=pltpu.HBM)
    vmem = pl.BlockSpec(memory_space=pltpu.VMEM)
    kinds = (0,) if tx_count == 2 else (0, 1)

    waves = lax.axis_size("wave")

    def swap(value, partner):
        def index(w, x, y):
            return (w * tx_count + x) * ty_count + y

        pairs = []
        for w in range(waves):
            for x in range(tx_count):
                for y in range(ty_count):
                    ox, oy = partner(w, x, y)
                    if ox is not None and oy is not None and 0 <= oy < ty_count:
                        pairs.append((index(w, x, y), index(w, ox, oy)))
                    elif waves % 2 == 0:
                        pairs.append((index(w, x, y), index(w ^ 1, x, y)))
        return lax.ppermute(value, ("wave", "tx", "ty"), pairs)

    def along_y(b):
        return lambda w, x, y: (x, pair_of(y, b, ty_count))

    def along_x(kind):
        return lambda w, x, y: (pair_of(x, kind, tx_count), y)

    def corner(kind, mixed):
        return lambda w, x, y: (pair_of(x, kind, tx_count), y + (1 if (x % 2 == kind) != mixed else -1))

    tile, start, y_a, y_b = pl.pallas_call(
        pack_kernel,
        out_shape=(
            f32(FIELDS, LINES, ROWS, LANES),
            f32(3, LINES, ROWS, LANES),
            f32(Y_SIZE, ROWS, LANES),
            f32(Y_SIZE, ROWS, LANES),
        ),
        in_specs=[hbm] * 5,
        out_specs=(vmem,) * 4,
        scratch_shapes=[
            pltpu.SMEM((NMAT, 4), jnp.float32),
            pltpu.SMEM((6,), jnp.int32),
            pltpu.VMEM((ROWS // 8, 2, 12, 8, LINES * NZ), jnp.float32),
            pltpu.VMEM((ROWS, LINES * NZ), jnp.int32),
            pltpu.VMEM((ROWS, LINES * NZ), jnp.float32),
            pltpu.SemaphoreType.DMA((CHUNKS + 4,)),
        ],
        compiler_params=pltpu.CompilerParams(vmem_limit_bytes=32 * 1024 * 1024),
        name="pack",
    )(*[in_hbm(v) for v in (material_table, design_box, initial_fields, material_map, design_density)])
    y_a, y_b = swap(y_a, along_y(0)), swap(y_b, along_y(1))

    sizes = (X_SIZE, SAME_SIZE, MIXED_SIZE) * len(kinds)
    messages = pl.pallas_call(
        edge_kernel,
        out_shape=[f32(size, LANES) for size in sizes],
        in_specs=[vmem, vmem],
        out_specs=[vmem] * len(sizes),
        compiler_params=pltpu.CompilerParams(vmem_limit_bytes=32 * 1024 * 1024),
        name="edges",
    )(tile, start)
    arrived = []
    for i, message in enumerate(messages):
        kind = i // 3
        arrived.append(swap(message, along_x(kind) if i % 3 == 0 else corner(kind, i % 3 == 2)))

    ext = (EXT_LINES, ROWS + (PAD if tx_count == 2 else 2 * PAD), LANES)
    prepared = pl.pallas_call(
        functools.partial(prepare_kernel, tx_count, ty_count),
        out_shape=(f32(STEPS, 3, EXT_LINES + 6, LANES), f32(*ext[1:]), f32(*ext), f32(16, LANES)),
        in_specs=[hbm] * 4 + [vmem],
        out_specs=(vmem,) * 4,
        scratch_shapes=[
            pltpu.SMEM((2, STEPS), jnp.float32),
            pltpu.SMEM((NMAT, 4), jnp.float32),
            pltpu.SMEM((2,), jnp.int32),
            pltpu.SMEM((6,), jnp.int32),
            pltpu.SemaphoreType.DMA((4,)),
        ],
        compiler_params=pltpu.CompilerParams(vmem_limit_bytes=16 * 1024 * 1024),
        name="prepare",
    )(
        *[in_hbm(v) for v in (source_waveforms[0], material_table, plane_indices, design_box)],
        source_profiles[0].transpose(1, 0, 2),
    )
    fields = f32(3, *ext)
    state = ([fields] * (STEPS + 1), [fields] * STEPS, fields, fields, f32(*ext), f32(4, *ext), f32(2, EXT_LINES + 6, LANES))
    scratch = [pltpu.VMEM(fields.shape, jnp.float32)] * 2
    results = (f32(3, LINES, ROWS, LANES), f32(ROWS, LINES * NZ))
    params = pltpu.CompilerParams(vmem_limit_bytes=24 * 1024 * 1024)
    first, last = (*prepared, start), (tile, y_a, y_b)

    def in_vmem(shapes):
        return jax.tree.map(lambda _: vmem, shapes)

    if tx_count == 2:
        made = pl.pallas_call(
            functools.partial(window_part, True, False, tx_count, ty_count),
            out_shape=state,
            in_specs=[vmem] * 8,
            out_specs=in_vmem(state),
            scratch_shapes=scratch,
            compiler_params=params,
            name="early",
        )(*first, *last)
        operands = (*first, *arrived)
        electric, partial, *_ = pl.pallas_call(
            functools.partial(window_part, False, True, tx_count, ty_count),
            out_shape=(*results, state),
            in_specs=[vmem] * len(operands) + [in_vmem(state)],
            out_specs=(vmem, vmem, in_vmem(state)),
            scratch_shapes=scratch,
            input_output_aliases={len(operands) + i: 2 + i for i in range(len(jax.tree.leaves(state)))},
            compiler_params=params,
            name="late",
        )(*operands, made)
    else:
        electric, partial = pl.pallas_call(
            functools.partial(window_part, True, True, tx_count, ty_count),
            out_shape=results,
            in_specs=[vmem] * (8 + len(arrived)),
            out_specs=(vmem, vmem),
            scratch_shapes=[jax.tree.map(lambda v: pltpu.VMEM(v.shape, jnp.float32), state), *scratch],
            compiler_params=params,
            name="window",
        )(*first, *last, *arrived)
    final = pl.pallas_call(
        emit_kernel,
        out_shape=f32(1, 2, 3, ROWS, LINES * NZ),
        in_specs=[vmem],
        out_specs=vmem,
        compiler_params=pltpu.CompilerParams(vmem_limit_bytes=8 * 1024 * 1024),
        name="emit",
    )(electric)

    if lax.axis_size("wave") == 4:
        one, two, three = [
            lax.ppermute(partial, "wave", [(i, i ^ k) for i in range(4)]) for k in (1, 2, 3)
        ]
        gradient = (partial + one) + (two + three)
    else:
        gradient = lax.psum(partial, "wave")
    return gradient, final


def solution(mesh):
    placed = (
        P("wave", None, None, "tx", "ty"),
        P("wave", None, None, None),
        P("wave", None, None),
        P("tx", "ty"),
        P("tx", "ty"),
        P(),
        P(),
        P(),
    )
    return jax.shard_map(
        functools.partial(on_device, mesh.shape["tx"], mesh.shape["ty"]),
        mesh=mesh,
        in_specs=placed,
        out_specs=(P("tx", "ty"), P("wave", None, None, "tx", "ty")),
        check_vma=False,
    )
```

```python
import functools

import jax
import jax.numpy as jnp
from jax import lax
from jax.experimental import pallas as pl
from jax.experimental.pallas import tpu as pltpu
from jax.sharding import PartitionSpec as P

NZ = 64
STEPS = 5
NMAT = 3
LANES = 2 * NZ
ROWS = 16
LINES = 8
CHUNKS = LINES // 2
PAD = 8
EXT_LINES = LINES + 2 * STEPS
FIELDS = 13

time_step = 0.5
contrast = 2.0

BEHIND_LINES = (4, 4, 4, 5, 4, 5, 2, 2, 2, 3, 3, 3, 4)
AHEAD_LINES = (4, 3, 4, 4, 4, 4, 2, 1, 2, 3, 2, 3, 4)
BEHIND_ROWS = (4, 4, 4, 4, 5, 5, 2, 2, 2, 3, 3, 3, 4)
AHEAD_ROWS = (3, 4, 4, 4, 4, 4, 1, 2, 2, 2, 3, 3, 4)
BEHIND_BOTH = (3, 3, 3, 4, 4, 4, 1, 1, 1, 2, 2, 2, 3)
AHEAD_BOTH = (3, 3, 3, 3, 3, 3, 1, 1, 1, 2, 2, 2, 3)
AHEAD_ROW_BEHIND_LINE = (3, 4, 3, 4, 3, 4, 1, 2, 1, 2, 3, 2, 4)
BEHIND_ROW_AHEAD_LINE = (4, 3, 3, 3, 4, 4, 2, 1, 1, 3, 2, 2, 4)
BORDER = 5


def line_entries(depth):
    return [(f, k) for f in range(FIELDS) for k in range(depth[f])]


def row_entries(entries):
    start, out = 0, []
    for f, k, depth in entries:
        out.append((f, k, depth, start))
        start += depth
    return out, start


def corner_entries(depth):
    return row_entries([(f, k, depth[f] - k) for f in range(FIELDS) for k in range(depth[f])])


Y_ENTRIES = {False: line_entries(BEHIND_LINES), True: line_entries(AHEAD_LINES)}
Y_SIZE = max(len(Y_ENTRIES[False]) + 1, len(Y_ENTRIES[True]) + 3)
X_ENTRIES = {
    ahead: row_entries([(f, line, depth[f]) for f in range(FIELDS) for line in range(LINES)])
    for ahead, depth in ((False, BEHIND_ROWS), (True, AHEAD_ROWS))
}
SAME_ENTRIES = {False: corner_entries(BEHIND_BOTH), True: corner_entries(AHEAD_BOTH)}
MIXED_ENTRIES = {False: corner_entries(BEHIND_ROW_AHEAD_LINE), True: corner_entries(AHEAD_ROW_BEHIND_LINE)}


def round_up(n):
    return (n + 7) // 8 * 8


X_SIZE = round_up(max(X_ENTRIES[False][1] + 2 * BORDER, X_ENTRIES[True][1] + 2 * BORDER + 2 * LINES))
SAME_SIZE = round_up(max(SAME_ENTRIES[False][1], SAME_ENTRIES[True][1] + 16))
MIXED_SIZE = round_up(max(MIXED_ENTRIES[ahead][1] + 2 * BORDER for ahead in (False, True)))


def low_lanes(shape):
    return lax.broadcasted_iota(jnp.int32, shape, len(shape) - 1) < NZ


def half_turn(v):
    return pltpu.roll(v, NZ, v.ndim - 1)


def choose(material, column):
    values = [column(m) for m in range(NMAT)]
    return jnp.where(material < 0.5, values[0], jnp.where(material < 1.5, values[1], values[2]))


def pole(table):
    out = []
    for m in range(NMAT):
        d, w, g = table[m, 1], table[m, 2], table[m, 3]
        denom = 1.0 + 0.25 * g
        drive = w * w * time_step / denom
        out.append(((1.0 - 0.25 * g) / denom, drive * 0.5, drive * d * 2.0))
    return [lambda m, i=i: out[m][i] for i in range(3)]


def is_lower_in_a():
    return lax.rem(lax.axis_index("ty"), 2) == 0


def pack_kernel(
    table_hbm,
    box_hbm,
    fields_hbm,
    material_hbm,
    density_hbm,
    tile,
    start,
    y_a,
    y_b,
    table,
    box,
    fields,
    material,
    density,
    sems,
):
    copies = [
        pltpu.make_async_copy(src, dst, sems.at[CHUNKS + i])
        for i, (src, dst) in enumerate(
            [(table_hbm, table), (box_hbm, box), (material_hbm, material), (density_hbm, density)]
        )
    ]
    chunks = [
        pltpu.make_async_copy(fields_hbm.at[0, :, :, pl.ds(8 * b, 8), :], fields.at[b], sems.at[b])
        for b in range(ROWS // 8)
    ]
    for copy in copies + chunks:
        copy.start()
    for copy in copies:
        copy.wait()
    decay, drive, coupled = pole(table)
    block = (8, LANES)
    low = low_lanes(block)
    lane = lax.broadcasted_iota(jnp.int32, block, 1)
    depth_id = jnp.where(low, lane, lane - NZ)
    last_z = (jnp.concatenate([depth_id, depth_id], axis=0) == NZ - 1)
    in_z = (depth_id >= box[4]) & (depth_id < box[5])
    first_line = lax.axis_index("ty") * LINES

    def split(one, two):
        return jnp.where(low, one, half_turn(two)), jnp.where(low, half_turn(one), two)

    for b in range(ROWS // 8):
        rows = slice(8 * b, 8 * b + 8)
        row = lax.broadcasted_iota(jnp.int32, block, 0) + (lax.axis_index("tx") * ROWS + 8 * b)
        design_rows = ((row >= box[0]) & (row < box[1]) & in_z).astype(jnp.float32)
        chunks[b].wait()
        for k in range(CHUNKS):
            at = slice(k * LANES, (k + 1) * LANES)
            pairs = [split(fields[b, 0, f, :, at], fields[b, 1, f, :, at]) for f in range(12)]
            mat, dens = material[rows, at].astype(jnp.float32), density[rows, at]
            turned = half_turn(mat)
            mats = (jnp.where(low, mat, turned), jnp.where(low, turned, mat))
            turned = half_turn(dens)
            denses = (jnp.where(low, dens, turned), jnp.where(low, turned, dens))
            for half in range(2):
                line = 2 * k + half
                mat, dens = mats[half], denses[half]
                where = first_line + line
                design = design_rows * ((where >= box[2]) & (where < box[3])).astype(jnp.float32)
                permittivity = choose(mat, lambda m: table[m, 0]) + design * dens * contrast
                reach = time_step * 0.5 / permittivity
                dec, dri, cou = [choose(mat, column) for column in (decay, drive, coupled)]
                for c in range(3):
                    e, p, j = pairs[c][half], 4.0 * pairs[6 + c][half], 2.0 * pairs[9 + c][half]
                    j = dec * j + cou * e - dri * p
                    p = p + j
                    start[c, line, rows, :] = e
                    tile[c, line, rows, :] = e - reach * j
                    tile[3 + c, line, rows, :] = 2.0 * pairs[3 + c][half]
                    tile[6 + c, line, rows, :] = p
                    tile[9 + c, line, rows, :] = dec * j - dri * p
                tile[12, line, rows, :] = jnp.where(low, mat, dens)

    edge = jnp.zeros((1, LANES), jnp.float32)

    def ahead_row(v):
        return jnp.concatenate([v[1:], edge], axis=0)

    def ahead_depth(v):
        return jnp.where(last_z, 0.0, pltpu.roll(v, LANES - 1, 1))

    for line in range(LINES):
        ex, ey, ez = [start[c, line] for c in range(3)]
        if line + 1 < LINES:
            ex_next, ez_next = start[0, line + 1], start[2, line + 1]
        else:
            ex_next = ez_next = jnp.zeros((ROWS, LANES), jnp.float32)
        tile[3, line] = tile[3, line] - ((ez_next - ez) - (ahead_depth(ey) - ey))
        tile[4, line] = tile[4, line] - ((ahead_depth(ex) - ex) - (ahead_row(ez) - ez))
        tile[5, line] = tile[5, line] - ((ahead_row(ey) - ey) - (ex_next - ex))

    lower = is_lower_in_a()
    for message, is_lower in ((y_a, lower), (y_b, jnp.logical_not(lower))):
        for ahead in (False, True):

            @pl.when(is_lower != ahead)
            def _(message=message, ahead=ahead):
                def line_of(k):
                    return k if ahead else LINES - 1 - k

                entries = Y_ENTRIES[ahead]
                for i, (f, k) in enumerate(entries):
                    message[i] = tile[f, line_of(k)]
                last = len(entries)
                for k in range(4 if ahead else 5):
                    message[last, k : k + 1, :] = start[1, line_of(k), 0:1, :]
                    message[last, 5 + k : 6 + k, :] = start[2, line_of(k), 0:1, :]
                if ahead:
                    message[last + 1] = start[0, 0]
                    message[last + 2] = start[2, 0]


def edge_kernel(tile, start, *messages):
    odd = lax.rem(lax.axis_index("tx"), 2)
    for kind in range(len(messages) // 3):
        along, same, mixed = messages[3 * kind : 3 * kind + 3]
        for ahead in (False, True):

            @pl.when((odd == kind) != ahead)
            def _(ahead=ahead, along=along, same=same, mixed=mixed):
                def rows(depth):
                    return slice(0, depth) if ahead else slice(ROWS - depth, ROWS)

                def pack(message, entries, line_of):
                    for f, k, depth, at in entries[0]:
                        message[at : at + depth, :] = tile[f, line_of(k), rows(depth), :]
                    return entries[1]

                def pack_first_line(message, at, depth):
                    for c in (0, 2):
                        message[at : at + depth, :] = start[c, 0, rows(depth), :]
                        at += depth
                    return at

                def pack_first_row(message, at, lines):
                    for c in (1, 2):
                        for line in lines:
                            message[at : at + 1, :] = start[c, line, 0:1, :]
                            at += 1

                at = pack(along, X_ENTRIES[ahead], lambda k: k)
                at = pack_first_line(along, at, BORDER)
                if ahead:
                    pack_first_row(along, at, range(LINES))
                at = pack(same, SAME_ENTRIES[ahead], lambda k: k if ahead else LINES - 1 - k)
                if ahead:
                    at = pack_first_line(same, at, 4)
                    pack_first_row(same, at, range(4))
                at = pack(mixed, MIXED_ENTRIES[ahead], lambda k: LINES - 1 - k if ahead else k)
                if ahead:
                    pack_first_row(mixed, at, [LINES - 1 - k for k in range(BORDER)])
                else:
                    pack_first_line(mixed, at, BORDER)


def prepare_kernel(
    tx_count,
    ty_count,
    waveforms_hbm,
    table_hbm,
    plane_hbm,
    box_hbm,
    profiles,
    sources,
    source_rows,
    design,
    poles,
    waveforms,
    table,
    plane,
    box,
    sems,
):
    copies = [
        pltpu.make_async_copy(src, dst, sems.at[i])
        for i, (src, dst) in enumerate(
            [(waveforms_hbm, waveforms), (table_hbm, table), (plane_hbm, plane), (box_hbm, box)]
        )
    ]
    for copy in copies:
        copy.start()
    for copy in copies:
        copy.wait()
    tx, ty = lax.axis_index("tx"), lax.axis_index("ty")
    shape = source_rows.shape
    low = low_lanes(shape)
    lane = lax.broadcasted_iota(jnp.int32, shape, 1)
    depth_id = jnp.where(low, lane, lane - NZ)
    row = window_rows(tx_count, shape)
    source_rows[...] = (row == jnp.where(low, plane[0], plane[1])).astype(jnp.float32)
    in_z = (depth_id >= box[4]) & (depth_id < box[5])
    design_rows = ((row >= box[0]) & (row < box[1]) & in_z).astype(jnp.float32) * contrast
    for line in range(1, EXT_LINES - 1):
        where = ty * LINES - STEPS + line
        design[line] = design_rows * ((where >= box[2]) & (where < box[3])).astype(jnp.float32)
    for i, column in enumerate((lambda m: table[m, 0], *pole(table))):
        for m in range(NMAT):
            at = NMAT * i + m
            poles[at : at + 1, :] = jnp.full((1, LANES), column(m), jnp.float32)
    low_row = low[:1]
    weights = [2.0 * jnp.where(low_row, waveforms[0, n], waveforms[1, n]) for n in range(STEPS)]
    for i in range(EXT_LINES // 2 - 1):
        chunk = jnp.clip(ty * CHUNKS + i - STEPS // 2, 0, ty_count * CHUNKS - 1)
        for c in range(3):
            both = profiles[c, :, pl.ds(pl.multiple_of(chunk * LANES, LANES), LANES)]
            one, two = both[0:1], both[1:2]
            first = jnp.where(low_row, one, half_turn(two))
            second = jnp.where(low_row, half_turn(one), two)
            for n in range(STEPS):
                sources[n, c, 2 * i + 1 : 2 * i + 2, :] = weights[n] * first
                sources[n, c, 2 * i + 2 : 2 * i + 3, :] = weights[n] * second


def window_rows(tx_count, shape):
    tx = lax.axis_index("tx")
    at = lax.broadcasted_iota(jnp.int32, shape, 0)
    if tx_count == 2:
        return at + tx * ROWS - jnp.where(at >= ROWS, tx * (ROWS + PAD), 0)
    return at + tx * ROWS - PAD


def window_part(early, late, tx_count, ty_count, *refs):
    *most, one, two = refs
    window_kernel(early, late, tx_count, ty_count, *most, (one, two))


def window_kernel(early, late, tx_count, ty_count, *refs):
    kinds = 1 if tx_count == 2 else 2
    refs = list(refs)
    sources, source_rows, design, poles, start = [refs.pop(0) for _ in range(5)]
    tile, y_a, y_b = [refs.pop(0) for _ in range(3)] if early else (None,) * 3
    messages = [refs.pop(0) for _ in range(3 * kinds)] if late else []
    if late and not early:
        refs.pop(0)
    electric_out, gradient_out = [refs.pop(0) for _ in range(2)] if late else (None, None)
    (E, H, Pol, J, C, coef, first_row), (Pol_next, J_next) = refs if len(refs) == 2 else (refs[:-1], refs[-1])
    H = [None] + list(H)
    Pol, J = (Pol, Pol_next), (J, J_next)
    wide = tx_count != 2
    ext_rows = E[0].shape[2]
    tx, ty = lax.axis_index("tx"), lax.axis_index("ty")
    odd_x = lax.rem(tx, 2)
    tile_row = PAD if wide else 0
    lines_base = ty * LINES - STEPS
    rows_all, lines_all = tx_count * ROWS, ty_count * LINES
    middle = slice(tile_row, tile_row + ROWS)

    def put(f, line, rows, value):
        if f < 12:
            (E[0], H[1], Pol[0], J[0])[f // 3][f % 3, line, rows, :] = value
        else:
            C[line, rows, :] = value

    def clear(lines, rows, count):
        for f in range(FIELDS):
            for line in lines:
                put(f, line, rows, jnp.zeros((count, LANES), jnp.float32))

    every_row = slice(0 if early else ROWS, ext_rows if late else ROWS)
    row_count = every_row.stop - every_row.start
    behind_lines, ahead_lines = range(STEPS), range(STEPS + LINES, EXT_LINES)
    no_behind, no_ahead = ty == 0, ty + 1 == ty_count
    if wide:

        @pl.when(tx == 0)
        def _():
            clear(range(EXT_LINES), slice(0, PAD), PAD)

        @pl.when(tx + 1 == tx_count)
        def _():
            clear(range(EXT_LINES), slice(PAD + ROWS, ext_rows), PAD)

    @pl.when(no_behind)
    def _():
        clear(behind_lines, every_row, row_count)

    @pl.when(no_ahead)
    def _():
        clear(ahead_lines, every_row, row_count)

    if early:
        for f in range(FIELDS):
            for line in range(LINES):
                put(f, STEPS + line, middle, tile[f, line])
    if late and not wide:
        H[1][1:3, :, ROWS:ext_rows, :] = jnp.zeros((2, EXT_LINES, PAD, LANES), jnp.float32)

    def near(ahead, k):
        return STEPS + LINES + k if ahead else STEPS - 1 - k

    def correct_line(line, rows, ex, ez):
        H[1][0, line, rows, :] = H[1][0, line, rows, :] - ez
        H[1][2, line, rows, :] = H[1][2, line, rows, :] + ex

    def correct_row(line, row, ey, ez):
        at = slice(row, row + 1)
        H[1][1, line, at, :] = H[1][1, line, at, :] + ez
        H[1][2, line, at, :] = H[1][2, line, at, :] - ey

    lower = is_lower_in_a()
    for message, is_lower in ((y_a, lower), (y_b, jnp.logical_not(lower))) if early else ():
        for ahead in (False, True):

            @pl.when(jnp.logical_and(is_lower == ahead, jnp.logical_not(no_ahead if ahead else no_behind)))
            def _(message=message, ahead=ahead):
                entries = Y_ENTRIES[ahead]
                for i, (f, k) in enumerate(entries):
                    put(f, near(ahead, k), middle, message[i])
                last = len(entries)
                for k in range(4 if ahead else 5):
                    first_row[0, near(ahead, k) : near(ahead, k) + 1, :] = message[last, k : k + 1, :]
                    first_row[1, near(ahead, k) : near(ahead, k) + 1, :] = message[last, 5 + k : 6 + k, :]
                if ahead:
                    correct_line(STEPS + LINES - 1, middle, message[last + 1], message[last + 2])
                else:
                    correct_line(STEPS - 1, middle, start[0, 0], start[2, 0])

    for kind in range(kinds if late else 0):
        along, same, mixed = messages[3 * kind : 3 * kind + 3]
        for ahead in (False, True):
            in_x = tx + 1 < tx_count if ahead else tx > 0
            halo = tile_row + ROWS if ahead else (PAD if wide else ext_rows)
            last_row = halo - 1

            @pl.when(jnp.logical_and((odd_x == kind) == ahead, in_x))
            def _(ahead=ahead, along=along, same=same, mixed=mixed, halo=halo, last_row=last_row):
                def rows(depth):
                    return slice(halo, halo + depth) if ahead else slice(halo - depth, halo)

                def unpack(message, entries, line_of):
                    for f, k, depth, at in entries[0]:
                        put(f, line_of(k), rows(depth), message[at : at + depth, :])
                    return entries[1]

                def first_line(message, at, depth, line):
                    ex, ez = message[at : at + depth, :], message[at + depth : at + 2 * depth, :]
                    correct_line(line, rows(depth), ex, ez)
                    return at + 2 * depth

                def rows_ahead(message, at, lines):
                    for i, line in enumerate(lines):
                        one, two = at + i, at + len(lines) + i
                        correct_row(line, last_row, message[one : one + 1, :], message[two : two + 1, :])

                def rows_own(lines):
                    for line in lines:
                        correct_row(
                            line,
                            last_row,
                            first_row[0, line : line + 1, :],
                            first_row[1, line : line + 1, :],
                        )

                along_end = unpack(along, X_ENTRIES[ahead], lambda k: STEPS + k)
                if ahead:
                    rows_ahead(along, along_end + 2 * BORDER, range(STEPS, STEPS + LINES))
                else:
                    for line in range(LINES):
                        correct_row(STEPS + line, last_row, start[1, line, 0:1, :], start[2, line, 0:1, :])

                @pl.when(jnp.logical_not(no_behind))
                def _():
                    message, entries = (mixed, MIXED_ENTRIES[True]) if ahead else (same, SAME_ENTRIES[False])
                    at = unpack(message, entries, lambda k: near(False, k))
                    first_line(along, along_end, BORDER, STEPS - 1)
                    if ahead:
                        rows_ahead(message, at, [near(False, k) for k in range(BORDER)])
                    else:
                        rows_own(behind_lines)

                @pl.when(jnp.logical_not(no_ahead))
                def _():
                    message, entries = (same, SAME_ENTRIES[True]) if ahead else (mixed, MIXED_ENTRIES[False])
                    at = unpack(message, entries, lambda k: near(True, k))
                    at = first_line(message, at, 4 if ahead else BORDER, STEPS + LINES - 1)
                    if ahead:
                        rows_ahead(message, at, [near(True, k) for k in range(4)])
                    else:
                        rows_own([near(True, k) for k in range(4)])

    shape = (row_count, LANES)
    low = low_lanes(shape)
    row = window_rows(tx_count, (ext_rows, LANES))
    row_mask = ((row >= 0) & (row < rows_all)).astype(jnp.float32)

    def line_inside(line):
        where = lines_base + line
        return ((where >= 0) & (where < lines_all)).astype(jnp.float32)

    def is_own(line):
        return STEPS <= line < STEPS + LINES

    for line in range(1, EXT_LINES - 1):
        mixed = C[line, every_row, :]
        turned = half_turn(mixed)
        mat = jnp.where(low, mixed, turned)
        dens = jnp.where(low, turned, mixed)
        eps, *others = [
            choose(mat, lambda m, i=i: poles[NMAT * i + m : NMAT * i + m + 1, :]) for i in range(4)
        ]
        reach = time_step * 0.5 / (eps + design[line, every_row, :] * dens)
        if wide:
            reach = reach * row_mask
        if not is_own(line):
            reach = reach * line_inside(line)
        coef[0, line, every_row, :] = reach
        for i, value in enumerate(others):
            coef[1 + i, line, every_row, :] = value

    count = ext_rows // 8
    block = (8, LANES)
    lane = lax.broadcasted_iota(jnp.int32, block, 1)
    depth_id = jnp.where(low_lanes(block), lane, lane - NZ)
    first_z, last_z = depth_id == 0, depth_id == NZ - 1
    sub = lax.broadcasted_iota(jnp.int32, block, 0)
    first_sub, last_sub = sub == 0, sub == 7
    sent = sub + tx * (7 - 2 * sub) < STEPS
    own = range(tile_row // 8, (tile_row + ROWS) // 8)
    def make_steps(made):
        def rows_of(b):
            return slice(8 * b, 8 * b + 8)

        def blocks(ref, c, line):
            return {b: ref[c, line, rows_of(b), :] for b in made}

        def turned_blocks(ref, c, line, v, shift, step):
            turned = {}
            for b in sorted({*made, *((b + step) % count for b in made)}):
                if b in made:
                    turned[b] = pltpu.roll(v[b], shift, 0)
                elif late or b in own:
                    turned[b] = pltpu.roll(ref[c, line, rows_of(b), :], shift, 0)
                else:
                    turned[b] = jnp.zeros(block, jnp.float32)
            return turned

        def ahead_row(ref, c, line, v):
            turned = turned_blocks(ref, c, line, v, 7, 1)
            return {b: jnp.where(last_sub, turned[(b + 1) % count], turned[b]) for b in made}

        def behind_row(ref, c, line, v):
            turned = turned_blocks(ref, c, line, v, 1, -1)
            return {b: jnp.where(first_sub, turned[(b - 1) % count], turned[b]) for b in made}

        def ahead_depth(v):
            return jnp.where(last_z, 0.0, pltpu.roll(v, LANES - 1, 1))

        def behind_depth(v):
            return jnp.where(first_z, 0.0, pltpu.roll(v, 1, 1))

        def settle(ref, c, line, b, value):
            if not wide and b not in own:
                value = jnp.where(sent, value, 0.0)
            ref[c, line, rows_of(b), :] = value

        def magnetic_line(n, line):
            ex, ey, ez = [blocks(E[n], c, line) for c in range(3)]
            ex_next, ez_next = blocks(E[n], 0, line + 1), blocks(E[n], 2, line + 1)
            hx, hy, hz = [blocks(H[n], c, line) for c in range(3)]
            ey_ahead, ez_ahead = ahead_row(E[n], 1, line, ey), ahead_row(E[n], 2, line, ez)
            for b in made:
                curls = (
                    (ez_next[b] - ez[b]) - (ahead_depth(ey[b]) - ey[b]),
                    (ahead_depth(ex[b]) - ex[b]) - (ez_ahead[b] - ez[b]),
                    (ey_ahead[b] - ey[b]) - (ex_next[b] - ex[b]),
                )
                if line < STEPS:
                    curls = [curl * line_inside(line) for curl in curls]
                if wide:
                    curls = [curl * row_mask[8 * b : 8 * b + 8] for curl in curls]
                for c, h in enumerate((hx, hy, hz)):
                    settle(H[n + 1], c, line, b, h[b] - curls[c])

        def electric_line(n, line):
            field = H[n + 1]
            hx, hy, hz = [blocks(field, c, line) for c in range(3)]
            hx_last, hz_last = blocks(field, 0, line - 1), blocks(field, 2, line - 1)
            hy_behind, hz_behind = behind_row(field, 1, line, hy), behind_row(field, 2, line, hz)
            for b in [b for b in made if n + 1 < STEPS or b in own]:
                rows = rows_of(b)
                curls = (
                    (hz[b] - hz_last[b]) - (hy[b] - behind_depth(hy[b])),
                    (hx[b] - behind_depth(hx[b])) - (hz[b] - hz_behind[b]),
                    (hy[b] - hy_behind[b]) - (hx[b] - hx_last[b]),
                )
                reach = coef[0, line, rows, :]
                for c in range(3):
                    e = E[n][c, line, rows, :]
                    curl = curls[c]
                    if n > 0:
                        held = 0 if n == 1 else 1
                        p, j = Pol[held][c, line, rows, :], J[held][c, line, rows, :]
                        if n == 1:
                            j = j + coef[3, line, rows, :] * e
                        else:
                            j = coef[1, line, rows, :] * j + coef[3, line, rows, :] * e - coef[2, line, rows, :] * p
                        if n < STEPS - 1:
                            J[1][c, line, rows, :] = j
                            Pol[1][c, line, rows, :] = p + j
                        curl = curl - j
                    drawn = source_rows[rows, :] * sources[n, c, line : line + 1, :]
                    settle(E[n + 1], c, line, b, e + reach * (curl - drawn))

        for n in range(STEPS):
            for line in range(n, EXT_LINES - 1 - n) if n > 0 else ():
                magnetic_line(n, line)
            for line in range(n + 1, EXT_LINES - 1 - n):
                electric_line(n, line)

    def make_gradient():
        low_tile = low_lanes((ROWS, LANES))

        def turned(line):
            return [[half_turn(E[n][c, line, middle, :]) for n in (5, 4, 3)] for c in range(3)]

        totals, following = [], turned(STEPS)
        for own_line in range(LINES):
            line, (x, y, z) = STEPS + own_line, following
            if own_line + 1 < LINES:
                following = turned(line + 1)
            terms = []
            for c, (five, four, three) in enumerate((x, y, z)):
                one, two = E[1][c, line, middle, :], E[2][c, line, middle, :]
                zero_low = jnp.where(low_tile, start[c, own_line], 0.0)
                three_low = jnp.where(low_tile, E[3][c, line, middle, :], 0.0)
                terms.append(five * (one - zero_low) + four * (two - one) + three * (three_low - two))
                electric_out[c, own_line] = E[STEPS][c, line, middle, :]
            totals.append((terms[0] + terms[1] + terms[2]) * design[line, middle, :])
        folded = [total + half_turn(total) for total in totals]
        for k in range(CHUNKS):
            gradient_out[:, k * LANES : (k + 1) * LANES] = jnp.where(low_tile, folded[2 * k], folded[2 * k + 1])

    if early:
        make_steps(list(range(count) if late else own))
    else:
        for side in range(2):

            @pl.when(tx == side)
            def _(side=side):
                make_steps([2, 1 - side])
                make_gradient()
        return
    if late:
        make_gradient()


def emit_kernel(electric, out):
    low = low_lanes((ROWS, LANES))
    for k in range(CHUNKS):
        at = slice(k * LANES, (k + 1) * LANES)
        for c in range(3):
            one, two = electric[c, 2 * k], electric[c, 2 * k + 1]
            out[0, 0, c, :, at] = jnp.where(low, one, half_turn(two))
            out[0, 1, c, :, at] = jnp.where(low, half_turn(one), two)


def pair_of(index, kind, count):
    other = index + 1 if index % 2 == kind else index - 1
    return other if 0 <= other < count else None


def f32(*shape):
    return jax.ShapeDtypeStruct(shape, jnp.float32)


def in_hbm(value):
    return pltpu.with_memory_space_constraint(value, pltpu.HBM)


def on_device(
    tx_count,
    ty_count,
    initial_fields,
    source_profiles,
    source_waveforms,
    material_map,
    design_density,
    material_table,
    plane_indices,
    design_box,
):
    hbm = pl.BlockSpec(memory_space=pltpu.HBM)
    vmem = pl.BlockSpec(memory_space=pltpu.VMEM)
    kinds = (0,) if tx_count == 2 else (0, 1)

    waves = lax.axis_size("wave")

    def swap(value, partner):
        def index(w, x, y):
            return (w * tx_count + x) * ty_count + y

        pairs = []
        for w in range(waves):
            for x in range(tx_count):
                for y in range(ty_count):
                    ox, oy = partner(w, x, y)
                    if ox is not None and oy is not None and 0 <= oy < ty_count:
                        pairs.append((index(w, x, y), index(w, ox, oy)))
                    elif waves % 2 == 0:
                        pairs.append((index(w, x, y), index(w ^ 1, x, y)))
        return lax.ppermute(value, ("wave", "tx", "ty"), pairs)

    def along_y(b):
        return lambda w, x, y: (x, pair_of(y, b, ty_count))

    def along_x(kind):
        return lambda w, x, y: (pair_of(x, kind, tx_count), y)

    def corner(kind, mixed):
        return lambda w, x, y: (pair_of(x, kind, tx_count), y + (1 if (x % 2 == kind) != mixed else -1))

    tile, start, y_a, y_b = pl.pallas_call(
        pack_kernel,
        out_shape=(
            f32(FIELDS, LINES, ROWS, LANES),
            f32(3, LINES, ROWS, LANES),
            f32(Y_SIZE, ROWS, LANES),
            f32(Y_SIZE, ROWS, LANES),
        ),
        in_specs=[hbm] * 5,
        out_specs=(vmem,) * 4,
        scratch_shapes=[
            pltpu.SMEM((NMAT, 4), jnp.float32),
            pltpu.SMEM((6,), jnp.int32),
            pltpu.VMEM((ROWS // 8, 2, 12, 8, LINES * NZ), jnp.float32),
            pltpu.VMEM((ROWS, LINES * NZ), jnp.int32),
            pltpu.VMEM((ROWS, LINES * NZ), jnp.float32),
            pltpu.SemaphoreType.DMA((CHUNKS + 4,)),
        ],
        compiler_params=pltpu.CompilerParams(vmem_limit_bytes=32 * 1024 * 1024),
        name="pack",
    )(*[in_hbm(v) for v in (material_table, design_box, initial_fields, material_map, design_density)])
    y_a, y_b = swap(y_a, along_y(0)), swap(y_b, along_y(1))

    sizes = (X_SIZE, SAME_SIZE, MIXED_SIZE) * len(kinds)
    messages = pl.pallas_call(
        edge_kernel,
        out_shape=[f32(size, LANES) for size in sizes],
        in_specs=[vmem, vmem],
        out_specs=[vmem] * len(sizes),
        compiler_params=pltpu.CompilerParams(vmem_limit_bytes=32 * 1024 * 1024),
        name="edges",
    )(tile, start)
    arrived = []
    for i, message in enumerate(messages):
        kind = i // 3
        arrived.append(swap(message, along_x(kind) if i % 3 == 0 else corner(kind, i % 3 == 2)))

    ext = (EXT_LINES, ROWS + (PAD if tx_count == 2 else 2 * PAD), LANES)
    prepared = pl.pallas_call(
        functools.partial(prepare_kernel, tx_count, ty_count),
        out_shape=(f32(STEPS, 3, EXT_LINES + 6, LANES), f32(*ext[1:]), f32(*ext), f32(16, LANES)),
        in_specs=[hbm] * 4 + [vmem],
        out_specs=(vmem,) * 4,
        scratch_shapes=[
            pltpu.SMEM((2, STEPS), jnp.float32),
            pltpu.SMEM((NMAT, 4), jnp.float32),
            pltpu.SMEM((2,), jnp.int32),
            pltpu.SMEM((6,), jnp.int32),
            pltpu.SemaphoreType.DMA((4,)),
        ],
        compiler_params=pltpu.CompilerParams(vmem_limit_bytes=16 * 1024 * 1024),
        name="prepare",
    )(
        *[in_hbm(v) for v in (source_waveforms[0], material_table, plane_indices, design_box)],
        source_profiles[0].transpose(1, 0, 2),
    )
    fields = f32(3, *ext)
    state = ([fields] * (STEPS + 1), [fields] * STEPS, fields, fields, f32(*ext), f32(4, *ext), f32(2, EXT_LINES + 6, LANES))
    scratch = [pltpu.VMEM(fields.shape, jnp.float32)] * 2
    results = (f32(3, LINES, ROWS, LANES), f32(ROWS, LINES * NZ))
    params = pltpu.CompilerParams(vmem_limit_bytes=24 * 1024 * 1024)
    first, last = (*prepared, start), (tile, y_a, y_b)

    def in_vmem(shapes):
        return jax.tree.map(lambda _: vmem, shapes)

    if tx_count == 2:
        made = pl.pallas_call(
            functools.partial(window_part, True, False, tx_count, ty_count),
            out_shape=state,
            in_specs=[vmem] * 8,
            out_specs=in_vmem(state),
            scratch_shapes=scratch,
            compiler_params=params,
            name="early",
        )(*first, *last)
        operands = (*first, *arrived)
        electric, partial, *_ = pl.pallas_call(
            functools.partial(window_part, False, True, tx_count, ty_count),
            out_shape=(*results, state),
            in_specs=[vmem] * len(operands) + [in_vmem(state)],
            out_specs=(vmem, vmem, in_vmem(state)),
            scratch_shapes=scratch,
            input_output_aliases={len(operands) + i: 2 + i for i in range(len(jax.tree.leaves(state)))},
            compiler_params=params,
            name="late",
        )(*operands, made)
    else:
        electric, partial = pl.pallas_call(
            functools.partial(window_part, True, True, tx_count, ty_count),
            out_shape=results,
            in_specs=[vmem] * (8 + len(arrived)),
            out_specs=(vmem, vmem),
            scratch_shapes=[jax.tree.map(lambda v: pltpu.VMEM(v.shape, jnp.float32), state), *scratch],
            compiler_params=params,
            name="window",
        )(*first, *last, *arrived)
    final = pl.pallas_call(
        emit_kernel,
        out_shape=f32(1, 2, 3, ROWS, LINES * NZ),
        in_specs=[vmem],
        out_specs=vmem,
        compiler_params=pltpu.CompilerParams(vmem_limit_bytes=8 * 1024 * 1024),
        name="emit",
    )(electric)

    if lax.axis_size("wave") == 4:
        one, two, three = [
            lax.ppermute(partial, "wave", [(i, i ^ k) for i in range(4)]) for k in (1, 2, 3)
        ]
        gradient = (partial + one) + (two + three)
    else:
        gradient = lax.psum(partial, "wave")
    return gradient, final


def solution(mesh):
    placed = (
        P("wave", None, None, "tx", "ty"),
        P("wave", None, None, None),
        P("wave", None, None),
        P("tx", "ty"),
        P("tx", "ty"),
        P(),
        P(),
        P(),
    )
    return jax.shard_map(
        functools.partial(on_device, mesh.shape["tx"], mesh.shape["ty"]),
        mesh=mesh,
        in_specs=placed,
        out_specs=(P("tx", "ty"), P("wave", None, None, "tx", "ty")),
        check_vma=False,
    )
```

```python
import functools

import jax
import jax.numpy as jnp
from jax import lax
from jax.experimental import pallas as pl
from jax.experimental.pallas import tpu as pltpu
from jax.sharding import PartitionSpec as P

NZ = 64
STEPS = 5
NMAT = 3
LANES = 2 * NZ
ROWS = 16
LINES = 8
CHUNKS = LINES // 2
PAD = 8
EXT_LINES = LINES + 2 * STEPS
FIELDS = 13

time_step = 0.5
contrast = 2.0

BEHIND_LINES = (4, 4, 4, 5, 4, 5, 2, 2, 2, 3, 3, 3, 4)
AHEAD_LINES = (4, 3, 4, 4, 4, 4, 2, 1, 2, 3, 2, 3, 4)
BEHIND_ROWS = (4, 4, 4, 4, 5, 5, 2, 2, 2, 3, 3, 3, 4)
AHEAD_ROWS = (3, 4, 4, 4, 4, 4, 1, 2, 2, 2, 3, 3, 4)
BEHIND_BOTH = (3, 3, 3, 4, 4, 4, 1, 1, 1, 2, 2, 2, 3)
AHEAD_BOTH = (3, 3, 3, 3, 3, 3, 1, 1, 1, 2, 2, 2, 3)
AHEAD_ROW_BEHIND_LINE = (3, 4, 3, 4, 3, 4, 1, 2, 1, 2, 3, 2, 4)
BEHIND_ROW_AHEAD_LINE = (4, 3, 3, 3, 4, 4, 2, 1, 1, 3, 2, 2, 4)
BORDER = 5


def line_entries(depth):
    return [(f, k) for f in range(FIELDS) for k in range(depth[f])]


def row_entries(entries):
    start, out = 0, []
    for f, k, depth in entries:
        out.append((f, k, depth, start))
        start += depth
    return out, start


def corner_entries(depth):
    return row_entries([(f, k, depth[f] - k) for f in range(FIELDS) for k in range(depth[f])])


Y_ENTRIES = {False: line_entries(BEHIND_LINES), True: line_entries(AHEAD_LINES)}
Y_SIZE = max(len(Y_ENTRIES[False]) + 1, len(Y_ENTRIES[True]) + 3)
X_ENTRIES = {
    ahead: row_entries([(f, line, depth[f]) for f in range(FIELDS) for line in range(LINES)])
    for ahead, depth in ((False, BEHIND_ROWS), (True, AHEAD_ROWS))
}
SAME_ENTRIES = {False: corner_entries(BEHIND_BOTH), True: corner_entries(AHEAD_BOTH)}
MIXED_ENTRIES = {False: corner_entries(BEHIND_ROW_AHEAD_LINE), True: corner_entries(AHEAD_ROW_BEHIND_LINE)}


def round_up(n):
    return (n + 7) // 8 * 8


X_SIZE = round_up(max(X_ENTRIES[False][1] + 2 * BORDER, X_ENTRIES[True][1] + 2 * BORDER + 2 * LINES))
SAME_SIZE = round_up(max(SAME_ENTRIES[False][1], SAME_ENTRIES[True][1] + 16))
MIXED_SIZE = round_up(max(MIXED_ENTRIES[ahead][1] + 2 * BORDER for ahead in (False, True)))


def low_lanes(shape):
    return lax.broadcasted_iota(jnp.int32, shape, len(shape) - 1) < NZ


def half_turn(v):
    return pltpu.roll(v, NZ, v.ndim - 1)


def choose(material, column):
    values = [column(m) for m in range(NMAT)]
    return jnp.where(material < 0.5, values[0], jnp.where(material < 1.5, values[1], values[2]))


def pole(table):
    out = []
    for m in range(NMAT):
        d, w, g = table[m, 1], table[m, 2], table[m, 3]
        denom = 1.0 + 0.25 * g
        drive = w * w * time_step / denom
        out.append(((1.0 - 0.25 * g) / denom, drive * 0.5, drive * d * 2.0))
    return [lambda m, i=i: out[m][i] for i in range(3)]


def is_lower_in_a():
    return lax.rem(lax.axis_index("ty"), 2) == 0


def pack_kernel(
    table_hbm,
    box_hbm,
    fields_hbm,
    material_hbm,
    density_hbm,
    tile,
    start,
    y_a,
    y_b,
    table,
    box,
    fields,
    material,
    density,
    sems,
):
    copies = [
        pltpu.make_async_copy(src, dst, sems.at[CHUNKS + i])
        for i, (src, dst) in enumerate(
            [(table_hbm, table), (box_hbm, box), (material_hbm, material), (density_hbm, density)]
        )
    ]
    chunks = [
        pltpu.make_async_copy(fields_hbm.at[0, :, :, pl.ds(8 * b, 8), :], fields.at[b], sems.at[b])
        for b in range(ROWS // 8)
    ]
    for copy in copies + chunks:
        copy.start()
    for copy in copies:
        copy.wait()
    decay, drive, coupled = pole(table)
    block = (8, LANES)
    low = low_lanes(block)
    lane = lax.broadcasted_iota(jnp.int32, block, 1)
    depth_id = jnp.where(low, lane, lane - NZ)
    last_z = (jnp.concatenate([depth_id, depth_id], axis=0) == NZ - 1)
    in_z = (depth_id >= box[4]) & (depth_id < box[5])
    first_line = lax.axis_index("ty") * LINES

    def split(one, two):
        return jnp.where(low, one, half_turn(two)), jnp.where(low, half_turn(one), two)

    for b in range(ROWS // 8):
        rows = slice(8 * b, 8 * b + 8)
        row = lax.broadcasted_iota(jnp.int32, block, 0) + (lax.axis_index("tx") * ROWS + 8 * b)
        design_rows = ((row >= box[0]) & (row < box[1]) & in_z).astype(jnp.float32)
        chunks[b].wait()
        for k in range(CHUNKS):
            at = slice(k * LANES, (k + 1) * LANES)
            pairs = [split(fields[b, 0, f, :, at], fields[b, 1, f, :, at]) for f in range(12)]
            mat, dens = material[rows, at].astype(jnp.float32), density[rows, at]
            turned = half_turn(mat)
            mats = (jnp.where(low, mat, turned), jnp.where(low, turned, mat))
            turned = half_turn(dens)
            denses = (jnp.where(low, dens, turned), jnp.where(low, turned, dens))
            for half in range(2):
                line = 2 * k + half
                mat, dens = mats[half], denses[half]
                where = first_line + line
                design = design_rows * ((where >= box[2]) & (where < box[3])).astype(jnp.float32)
                permittivity = choose(mat, lambda m: table[m, 0]) + design * dens * contrast
                reach = time_step * 0.5 / permittivity
                dec, dri, cou = [choose(mat, column) for column in (decay, drive, coupled)]
                for c in range(3):
                    e, p, j = pairs[c][half], 4.0 * pairs[6 + c][half], 2.0 * pairs[9 + c][half]
                    j = dec * j + cou * e - dri * p
                    p = p + j
                    start[c, line, rows, :] = e
                    tile[c, line, rows, :] = e - reach * j
                    tile[3 + c, line, rows, :] = 2.0 * pairs[3 + c][half]
                    tile[6 + c, line, rows, :] = p
                    tile[9 + c, line, rows, :] = dec * j - dri * p
                tile[12, line, rows, :] = jnp.where(low, mat, dens)

    edge = jnp.zeros((1, LANES), jnp.float32)

    def ahead_row(v):
        return jnp.concatenate([v[1:], edge], axis=0)

    def ahead_depth(v):
        return jnp.where(last_z, 0.0, pltpu.roll(v, LANES - 1, 1))

    for line in range(LINES):
        ex, ey, ez = [start[c, line] for c in range(3)]
        if line + 1 < LINES:
            ex_next, ez_next = start[0, line + 1], start[2, line + 1]
        else:
            ex_next = ez_next = jnp.zeros((ROWS, LANES), jnp.float32)
        tile[3, line] = tile[3, line] - ((ez_next - ez) - (ahead_depth(ey) - ey))
        tile[4, line] = tile[4, line] - ((ahead_depth(ex) - ex) - (ahead_row(ez) - ez))
        tile[5, line] = tile[5, line] - ((ahead_row(ey) - ey) - (ex_next - ex))

    lower = is_lower_in_a()
    for message, is_lower in ((y_a, lower), (y_b, jnp.logical_not(lower))):
        for ahead in (False, True):

            @pl.when(is_lower != ahead)
            def _(message=message, ahead=ahead):
                def line_of(k):
                    return k if ahead else LINES - 1 - k

                entries = Y_ENTRIES[ahead]
                for i, (f, k) in enumerate(entries):
                    message[i] = tile[f, line_of(k)]
                last = len(entries)
                for k in range(4 if ahead else 5):
                    message[last, k : k + 1, :] = start[1, line_of(k), 0:1, :]
                    message[last, 5 + k : 6 + k, :] = start[2, line_of(k), 0:1, :]
                if ahead:
                    message[last + 1] = start[0, 0]
                    message[last + 2] = start[2, 0]


def edge_kernel(tile, start, *messages):
    odd = lax.rem(lax.axis_index("tx"), 2)
    for kind in range(len(messages) // 3):
        along, same, mixed = messages[3 * kind : 3 * kind + 3]
        for ahead in (False, True):

            @pl.when((odd == kind) != ahead)
            def _(ahead=ahead, along=along, same=same, mixed=mixed):
                def rows(depth):
                    return slice(0, depth) if ahead else slice(ROWS - depth, ROWS)

                def pack(message, entries, line_of):
                    for f, k, depth, at in entries[0]:
                        message[at : at + depth, :] = tile[f, line_of(k), rows(depth), :]
                    return entries[1]

                def pack_first_line(message, at, depth):
                    for c in (0, 2):
                        message[at : at + depth, :] = start[c, 0, rows(depth), :]
                        at += depth
                    return at

                def pack_first_row(message, at, lines):
                    for c in (1, 2):
                        for line in lines:
                            message[at : at + 1, :] = start[c, line, 0:1, :]
                            at += 1

                at = pack(along, X_ENTRIES[ahead], lambda k: k)
                at = pack_first_line(along, at, BORDER)
                if ahead:
                    pack_first_row(along, at, range(LINES))
                at = pack(same, SAME_ENTRIES[ahead], lambda k: k if ahead else LINES - 1 - k)
                if ahead:
                    at = pack_first_line(same, at, 4)
                    pack_first_row(same, at, range(4))
                at = pack(mixed, MIXED_ENTRIES[ahead], lambda k: LINES - 1 - k if ahead else k)
                if ahead:
                    pack_first_row(mixed, at, [LINES - 1 - k for k in range(BORDER)])
                else:
                    pack_first_line(mixed, at, BORDER)


def prepare_kernel(
    tx_count,
    ty_count,
    waveforms_hbm,
    table_hbm,
    plane_hbm,
    box_hbm,
    profiles,
    sources,
    source_rows,
    design,
    poles,
    waveforms,
    table,
    plane,
    box,
    sems,
):
    copies = [
        pltpu.make_async_copy(src, dst, sems.at[i])
        for i, (src, dst) in enumerate(
            [(waveforms_hbm, waveforms), (table_hbm, table), (plane_hbm, plane), (box_hbm, box)]
        )
    ]
    for copy in copies:
        copy.start()
    for copy in copies:
        copy.wait()
    tx, ty = lax.axis_index("tx"), lax.axis_index("ty")
    shape = source_rows.shape
    low = low_lanes(shape)
    lane = lax.broadcasted_iota(jnp.int32, shape, 1)
    depth_id = jnp.where(low, lane, lane - NZ)
    row = window_rows(tx_count, shape)
    source_rows[...] = (row == jnp.where(low, plane[0], plane[1])).astype(jnp.float32)
    in_z = (depth_id >= box[4]) & (depth_id < box[5])
    design_rows = ((row >= box[0]) & (row < box[1]) & in_z).astype(jnp.float32) * contrast
    for line in range(1, EXT_LINES - 1):
        where = ty * LINES - STEPS + line
        design[line] = design_rows * ((where >= box[2]) & (where < box[3])).astype(jnp.float32)
    for i, column in enumerate((lambda m: table[m, 0], *pole(table))):
        for m in range(NMAT):
            at = NMAT * i + m
            poles[at : at + 1, :] = jnp.full((1, LANES), column(m), jnp.float32)
    low_row = low[:1]
    weights = [2.0 * jnp.where(low_row, waveforms[0, n], waveforms[1, n]) for n in range(STEPS)]
    for i in range(EXT_LINES // 2 - 1):
        chunk = jnp.clip(ty * CHUNKS + i - STEPS // 2, 0, ty_count * CHUNKS - 1)
        for c in range(3):
            both = profiles[c, :, pl.ds(pl.multiple_of(chunk * LANES, LANES), LANES)]
            one, two = both[0:1], both[1:2]
            first = jnp.where(low_row, one, half_turn(two))
            second = jnp.where(low_row, half_turn(one), two)
            for n in range(STEPS):
                sources[n, c, 2 * i + 1 : 2 * i + 2, :] = weights[n] * first
                sources[n, c, 2 * i + 2 : 2 * i + 3, :] = weights[n] * second


def window_rows(tx_count, shape):
    tx = lax.axis_index("tx")
    at = lax.broadcasted_iota(jnp.int32, shape, 0)
    if tx_count == 2:
        return at + tx * ROWS - jnp.where(at >= ROWS, tx * (ROWS + PAD), 0)
    return at + tx * ROWS - PAD


def window_part(early, late, tx_count, ty_count, *refs):
    *most, one, two = refs
    window_kernel(early, late, tx_count, ty_count, *most, (one, two))


def window_kernel(early, late, tx_count, ty_count, *refs):
    kinds = 1 if tx_count == 2 else 2
    refs = list(refs)
    sources, source_rows, design, poles, start = [refs.pop(0) for _ in range(5)]
    tile, y_a, y_b = [refs.pop(0) for _ in range(3)] if early else (None,) * 3
    messages = [refs.pop(0) for _ in range(3 * kinds)] if late else []
    if late and not early:
        refs.pop(0)
    electric_out, gradient_out = [refs.pop(0) for _ in range(2)] if late else (None, None)
    (E, H, Pol, J, C, coef, first_row), (Pol_next, J_next) = refs if len(refs) == 2 else (refs[:-1], refs[-1])
    H = [None] + list(H)
    Pol, J = (Pol, Pol_next), (J, J_next)
    wide = tx_count != 2
    ext_rows = E[0].shape[2]
    tx, ty = lax.axis_index("tx"), lax.axis_index("ty")
    odd_x = lax.rem(tx, 2)
    tile_row = PAD if wide else 0
    lines_base = ty * LINES - STEPS
    rows_all, lines_all = tx_count * ROWS, ty_count * LINES
    middle = slice(tile_row, tile_row + ROWS)

    def put(f, line, rows, value):
        if f < 12:
            (E[0], H[1], Pol[0], J[0])[f // 3][f % 3, line, rows, :] = value
        else:
            C[line, rows, :] = value

    def clear(lines, rows, count):
        for f in range(FIELDS):
            for line in lines:
                put(f, line, rows, jnp.zeros((count, LANES), jnp.float32))

    every_row = slice(0 if early else ROWS, ext_rows if late else ROWS)
    row_count = every_row.stop - every_row.start
    behind_lines, ahead_lines = range(STEPS), range(STEPS + LINES, EXT_LINES)
    no_behind, no_ahead = ty == 0, ty + 1 == ty_count
    if wide:

        @pl.when(tx == 0)
        def _():
            clear(range(EXT_LINES), slice(0, PAD), PAD)

        @pl.when(tx + 1 == tx_count)
        def _():
            clear(range(EXT_LINES), slice(PAD + ROWS, ext_rows), PAD)

    @pl.when(no_behind)
    def _():
        clear(behind_lines, every_row, row_count)

    @pl.when(no_ahead)
    def _():
        clear(ahead_lines, every_row, row_count)

    if early:
        for f in range(FIELDS):
            for line in range(LINES):
                put(f, STEPS + line, middle, tile[f, line])
    if late and not wide:
        H[1][1:3, :, ROWS:ext_rows, :] = jnp.zeros((2, EXT_LINES, PAD, LANES), jnp.float32)

    def near(ahead, k):
        return STEPS + LINES + k if ahead else STEPS - 1 - k

    def correct_line(line, rows, ex, ez):
        H[1][0, line, rows, :] = H[1][0, line, rows, :] - ez
        H[1][2, line, rows, :] = H[1][2, line, rows, :] + ex

    def correct_row(line, row, ey, ez):
        at = slice(row, row + 1)
        H[1][1, line, at, :] = H[1][1, line, at, :] + ez
        H[1][2, line, at, :] = H[1][2, line, at, :] - ey

    lower = is_lower_in_a()
    for message, is_lower in ((y_a, lower), (y_b, jnp.logical_not(lower))) if early else ():
        for ahead in (False, True):

            @pl.when(jnp.logical_and(is_lower == ahead, jnp.logical_not(no_ahead if ahead else no_behind)))
            def _(message=message, ahead=ahead):
                entries = Y_ENTRIES[ahead]
                for i, (f, k) in enumerate(entries):
                    put(f, near(ahead, k), middle, message[i])
                last = len(entries)
                for k in range(4 if ahead else 5):
                    first_row[0, near(ahead, k) : near(ahead, k) + 1, :] = message[last, k : k + 1, :]
                    first_row[1, near(ahead, k) : near(ahead, k) + 1, :] = message[last, 5 + k : 6 + k, :]
                if ahead:
                    correct_line(STEPS + LINES - 1, middle, message[last + 1], message[last + 2])
                else:
                    correct_line(STEPS - 1, middle, start[0, 0], start[2, 0])

    for kind in range(kinds if late else 0):
        along, same, mixed = messages[3 * kind : 3 * kind + 3]
        for ahead in (False, True):
            in_x = tx + 1 < tx_count if ahead else tx > 0
            halo = tile_row + ROWS if ahead else (PAD if wide else ext_rows)
            last_row = halo - 1

            @pl.when(jnp.logical_and((odd_x == kind) == ahead, in_x))
            def _(ahead=ahead, along=along, same=same, mixed=mixed, halo=halo, last_row=last_row):
                def rows(depth):
                    return slice(halo, halo + depth) if ahead else slice(halo - depth, halo)

                def unpack(message, entries, line_of):
                    for f, k, depth, at in entries[0]:
                        put(f, line_of(k), rows(depth), message[at : at + depth, :])
                    return entries[1]

                def first_line(message, at, depth, line):
                    ex, ez = message[at : at + depth, :], message[at + depth : at + 2 * depth, :]
                    correct_line(line, rows(depth), ex, ez)
                    return at + 2 * depth

                def rows_ahead(message, at, lines):
                    for i, line in enumerate(lines):
                        one, two = at + i, at + len(lines) + i
                        correct_row(line, last_row, message[one : one + 1, :], message[two : two + 1, :])

                def rows_own(lines):
                    for line in lines:
                        correct_row(
                            line,
                            last_row,
                            first_row[0, line : line + 1, :],
                            first_row[1, line : line + 1, :],
                        )

                along_end = unpack(along, X_ENTRIES[ahead], lambda k: STEPS + k)
                if ahead:
                    rows_ahead(along, along_end + 2 * BORDER, range(STEPS, STEPS + LINES))
                else:
                    for line in range(LINES):
                        correct_row(STEPS + line, last_row, start[1, line, 0:1, :], start[2, line, 0:1, :])

                @pl.when(jnp.logical_not(no_behind))
                def _():
                    message, entries = (mixed, MIXED_ENTRIES[True]) if ahead else (same, SAME_ENTRIES[False])
                    at = unpack(message, entries, lambda k: near(False, k))
                    first_line(along, along_end, BORDER, STEPS - 1)
                    if ahead:
                        rows_ahead(message, at, [near(False, k) for k in range(BORDER)])
                    else:
                        rows_own(behind_lines)

                @pl.when(jnp.logical_not(no_ahead))
                def _():
                    message, entries = (same, SAME_ENTRIES[True]) if ahead else (mixed, MIXED_ENTRIES[False])
                    at = unpack(message, entries, lambda k: near(True, k))
                    at = first_line(message, at, 4 if ahead else BORDER, STEPS + LINES - 1)
                    if ahead:
                        rows_ahead(message, at, [near(True, k) for k in range(4)])
                    else:
                        rows_own([near(True, k) for k in range(4)])

    shape = (row_count, LANES)
    low = low_lanes(shape)
    row = window_rows(tx_count, (ext_rows, LANES))
    row_mask = ((row >= 0) & (row < rows_all)).astype(jnp.float32)

    def line_inside(line):
        where = lines_base + line
        return ((where >= 0) & (where < lines_all)).astype(jnp.float32)

    def is_own(line):
        return STEPS <= line < STEPS + LINES

    for line in range(1, EXT_LINES - 1):
        mixed = C[line, every_row, :]
        turned = half_turn(mixed)
        mat = jnp.where(low, mixed, turned)
        dens = jnp.where(low, turned, mixed)
        eps, *others = [
            choose(mat, lambda m, i=i: poles[NMAT * i + m : NMAT * i + m + 1, :]) for i in range(4)
        ]
        reach = time_step * 0.5 / (eps + design[line, every_row, :] * dens)
        if wide:
            reach = reach * row_mask
        if not is_own(line):
            reach = reach * line_inside(line)
        coef[0, line, every_row, :] = reach
        for i, value in enumerate(others):
            coef[1 + i, line, every_row, :] = value

    count = ext_rows // 8
    block = (8, LANES)
    lane = lax.broadcasted_iota(jnp.int32, block, 1)
    depth_id = jnp.where(low_lanes(block), lane, lane - NZ)
    first_z, last_z = depth_id == 0, depth_id == NZ - 1
    sub = lax.broadcasted_iota(jnp.int32, block, 0)
    first_sub, last_sub = sub == 0, sub == 7
    sent = sub + tx * (7 - 2 * sub) < STEPS
    own = range(tile_row // 8, (tile_row + ROWS) // 8)
    def make_steps(made, side=None):
        def rows_of(b):
            return slice(8 * b, 8 * b + 8)

        def blocks(ref, c, line):
            return {b: ref[c, line, rows_of(b), :] for b in made}

        def turned_blocks(ref, c, line, v, shift, step):
            turned = {}
            for b in sorted({*made, *((b + step) % count for b in made)}):
                if b in made:
                    turned[b] = pltpu.roll(v[b], shift, 0)
                elif late or b in own:
                    turned[b] = pltpu.roll(ref[c, line, rows_of(b), :], shift, 0)
                else:
                    turned[b] = jnp.zeros(block, jnp.float32)
            return turned

        def ahead_row(ref, c, line, v):
            turned = turned_blocks(ref, c, line, v, 7, 1)
            return {b: jnp.where(last_sub, turned[(b + 1) % count], turned[b]) for b in made}

        def behind_row(ref, c, line, v):
            turned = turned_blocks(ref, c, line, v, 1, -1)
            return {b: jnp.where(first_sub, turned[(b - 1) % count], turned[b]) for b in made}

        def ahead_depth(v):
            return jnp.where(last_z, 0.0, pltpu.roll(v, LANES - 1, 1))

        def behind_depth(v):
            return jnp.where(first_z, 0.0, pltpu.roll(v, 1, 1))

        def settle(ref, c, line, b, value):
            if not wide and b not in own:
                value = jnp.where(sent, value, 0.0)
            ref[c, line, rows_of(b), :] = value

        def magnetic_line(n, line):
            ex, ey, ez = [blocks(E[n], c, line) for c in range(3)]
            ex_next, ez_next = blocks(E[n], 0, line + 1), blocks(E[n], 2, line + 1)
            hx, hy, hz = [blocks(H[n], c, line) for c in range(3)]
            ey_ahead, ez_ahead = ahead_row(E[n], 1, line, ey), ahead_row(E[n], 2, line, ez)
            for b in made:
                if side is not None and b not in own and (line == n or side == 0 and line == EXT_LINES - 2 - n):
                    continue
                curls = (
                    (ez_next[b] - ez[b]) - (ahead_depth(ey[b]) - ey[b]),
                    (ahead_depth(ex[b]) - ex[b]) - (ez_ahead[b] - ez[b]),
                    (ey_ahead[b] - ey[b]) - (ex_next[b] - ex[b]),
                )
                if line < STEPS:
                    curls = [curl * line_inside(line) for curl in curls]
                if wide:
                    curls = [curl * row_mask[8 * b : 8 * b + 8] for curl in curls]
                for c, h in enumerate((hx, hy, hz)):
                    settle(H[n + 1], c, line, b, h[b] - curls[c])

        def electric_line(n, line):
            field = H[n + 1]
            hx, hy, hz = [blocks(field, c, line) for c in range(3)]
            hx_last, hz_last = blocks(field, 0, line - 1), blocks(field, 2, line - 1)
            hy_behind, hz_behind = behind_row(field, 1, line, hy), behind_row(field, 2, line, hz)
            for b in [b for b in made if n + 1 < STEPS or b in own]:
                if side is not None and b not in own and line == (EXT_LINES - 2 - n if side == 0 else n + 1):
                    continue
                rows = rows_of(b)
                curls = (
                    (hz[b] - hz_last[b]) - (hy[b] - behind_depth(hy[b])),
                    (hx[b] - behind_depth(hx[b])) - (hz[b] - hz_behind[b]),
                    (hy[b] - hy_behind[b]) - (hx[b] - hx_last[b]),
                )
                reach = coef[0, line, rows, :]
                for c in range(3):
                    e = E[n][c, line, rows, :]
                    curl = curls[c]
                    if n > 0:
                        held = 0 if n == 1 else 1
                        p, j = Pol[held][c, line, rows, :], J[held][c, line, rows, :]
                        if n == 1:
                            j = j + coef[3, line, rows, :] * e
                        else:
                            j = coef[1, line, rows, :] * j + coef[3, line, rows, :] * e - coef[2, line, rows, :] * p
                        if n < STEPS - 1:
                            J[1][c, line, rows, :] = j
                            Pol[1][c, line, rows, :] = p + j
                        curl = curl - j
                    drawn = source_rows[rows, :] * sources[n, c, line : line + 1, :]
                    settle(E[n + 1], c, line, b, e + reach * (curl - drawn))

        for n in range(STEPS):
            for line in range(n, EXT_LINES - 1 - n) if n > 0 else ():
                magnetic_line(n, line)
            for line in range(n + 1, EXT_LINES - 1 - n):
                electric_line(n, line)

    def make_gradient():
        low_tile = low_lanes((ROWS, LANES))

        def turned(line):
            return [[half_turn(E[n][c, line, middle, :]) for n in (5, 4, 3)] for c in range(3)]

        totals, following = [], turned(STEPS)
        for own_line in range(LINES):
            line, (x, y, z) = STEPS + own_line, following
            if own_line + 1 < LINES:
                following = turned(line + 1)
            terms = []
            for c, (five, four, three) in enumerate((x, y, z)):
                one, two = E[1][c, line, middle, :], E[2][c, line, middle, :]
                zero_low = jnp.where(low_tile, start[c, own_line], 0.0)
                three_low = jnp.where(low_tile, E[3][c, line, middle, :], 0.0)
                terms.append(five * (one - zero_low) + four * (two - one) + three * (three_low - two))
                electric_out[c, own_line] = E[STEPS][c, line, middle, :]
            totals.append((terms[0] + terms[1] + terms[2]) * design[line, middle, :])
        folded = [total + half_turn(total) for total in totals]
        for k in range(CHUNKS):
            gradient_out[:, k * LANES : (k + 1) * LANES] = jnp.where(low_tile, folded[2 * k], folded[2 * k + 1])

    if early:
        make_steps(list(range(count) if late else own))
    else:
        for side in range(2):

            @pl.when(tx == side)
            def _(side=side):
                make_steps([2, 1 - side], side)
                make_gradient()
        return
    if late:
        make_gradient()


def emit_kernel(electric, out):
    low = low_lanes((ROWS, LANES))
    for k in range(CHUNKS):
        at = slice(k * LANES, (k + 1) * LANES)
        for c in range(3):
            one, two = electric[c, 2 * k], electric[c, 2 * k + 1]
            out[0, 0, c, :, at] = jnp.where(low, one, half_turn(two))
            out[0, 1, c, :, at] = jnp.where(low, half_turn(one), two)


def pair_of(index, kind, count):
    other = index + 1 if index % 2 == kind else index - 1
    return other if 0 <= other < count else None


def f32(*shape):
    return jax.ShapeDtypeStruct(shape, jnp.float32)


def in_hbm(value):
    return pltpu.with_memory_space_constraint(value, pltpu.HBM)


def on_device(
    tx_count,
    ty_count,
    initial_fields,
    source_profiles,
    source_waveforms,
    material_map,
    design_density,
    material_table,
    plane_indices,
    design_box,
):
    hbm = pl.BlockSpec(memory_space=pltpu.HBM)
    vmem = pl.BlockSpec(memory_space=pltpu.VMEM)
    kinds = (0,) if tx_count == 2 else (0, 1)

    waves = lax.axis_size("wave")

    def swap(value, partner):
        def index(w, x, y):
            return (w * tx_count + x) * ty_count + y

        pairs = []
        for w in range(waves):
            for x in range(tx_count):
                for y in range(ty_count):
                    ox, oy = partner(w, x, y)
                    if ox is not None and oy is not None and 0 <= oy < ty_count:
                        pairs.append((index(w, x, y), index(w, ox, oy)))
                    elif waves % 2 == 0:
                        pairs.append((index(w, x, y), index(w ^ 1, x, y)))
        return lax.ppermute(value, ("wave", "tx", "ty"), pairs)

    def along_y(b):
        return lambda w, x, y: (x, pair_of(y, b, ty_count))

    def along_x(kind):
        return lambda w, x, y: (pair_of(x, kind, tx_count), y)

    def corner(kind, mixed):
        return lambda w, x, y: (pair_of(x, kind, tx_count), y + (1 if (x % 2 == kind) != mixed else -1))

    tile, start, y_a, y_b = pl.pallas_call(
        pack_kernel,
        out_shape=(
            f32(FIELDS, LINES, ROWS, LANES),
            f32(3, LINES, ROWS, LANES),
            f32(Y_SIZE, ROWS, LANES),
            f32(Y_SIZE, ROWS, LANES),
        ),
        in_specs=[hbm] * 5,
        out_specs=(vmem,) * 4,
        scratch_shapes=[
            pltpu.SMEM((NMAT, 4), jnp.float32),
            pltpu.SMEM((6,), jnp.int32),
            pltpu.VMEM((ROWS // 8, 2, 12, 8, LINES * NZ), jnp.float32),
            pltpu.VMEM((ROWS, LINES * NZ), jnp.int32),
            pltpu.VMEM((ROWS, LINES * NZ), jnp.float32),
            pltpu.SemaphoreType.DMA((CHUNKS + 4,)),
        ],
        compiler_params=pltpu.CompilerParams(vmem_limit_bytes=32 * 1024 * 1024),
        name="pack",
    )(*[in_hbm(v) for v in (material_table, design_box, initial_fields, material_map, design_density)])
    y_a, y_b = swap(y_a, along_y(0)), swap(y_b, along_y(1))

    sizes = (X_SIZE, SAME_SIZE, MIXED_SIZE) * len(kinds)
    messages = pl.pallas_call(
        edge_kernel,
        out_shape=[f32(size, LANES) for size in sizes],
        in_specs=[vmem, vmem],
        out_specs=[vmem] * len(sizes),
        compiler_params=pltpu.CompilerParams(vmem_limit_bytes=32 * 1024 * 1024),
        name="edges",
    )(tile, start)
    arrived = []
    for i, message in enumerate(messages):
        kind = i // 3
        arrived.append(swap(message, along_x(kind) if i % 3 == 0 else corner(kind, i % 3 == 2)))

    ext = (EXT_LINES, ROWS + (PAD if tx_count == 2 else 2 * PAD), LANES)
    prepared = pl.pallas_call(
        functools.partial(prepare_kernel, tx_count, ty_count),
        out_shape=(f32(STEPS, 3, EXT_LINES + 6, LANES), f32(*ext[1:]), f32(*ext), f32(16, LANES)),
        in_specs=[hbm] * 4 + [vmem],
        out_specs=(vmem,) * 4,
        scratch_shapes=[
            pltpu.SMEM((2, STEPS), jnp.float32),
            pltpu.SMEM((NMAT, 4), jnp.float32),
            pltpu.SMEM((2,), jnp.int32),
            pltpu.SMEM((6,), jnp.int32),
            pltpu.SemaphoreType.DMA((4,)),
        ],
        compiler_params=pltpu.CompilerParams(vmem_limit_bytes=16 * 1024 * 1024),
        name="prepare",
    )(
        *[in_hbm(v) for v in (source_waveforms[0], material_table, plane_indices, design_box)],
        source_profiles[0].transpose(1, 0, 2),
    )
    fields = f32(3, *ext)
    state = ([fields] * (STEPS + 1), [fields] * STEPS, fields, fields, f32(*ext), f32(4, *ext), f32(2, EXT_LINES + 6, LANES))
    scratch = [pltpu.VMEM(fields.shape, jnp.float32)] * 2
    results = (f32(3, LINES, ROWS, LANES), f32(ROWS, LINES * NZ))
    params = pltpu.CompilerParams(vmem_limit_bytes=24 * 1024 * 1024)
    first, last = (*prepared, start), (tile, y_a, y_b)

    def in_vmem(shapes):
        return jax.tree.map(lambda _: vmem, shapes)

    if tx_count == 2:
        made = pl.pallas_call(
            functools.partial(window_part, True, False, tx_count, ty_count),
            out_shape=state,
            in_specs=[vmem] * 8,
            out_specs=in_vmem(state),
            scratch_shapes=scratch,
            compiler_params=params,
            name="early",
        )(*first, *last)
        operands = (*first, *arrived)
        electric, partial, *_ = pl.pallas_call(
            functools.partial(window_part, False, True, tx_count, ty_count),
            out_shape=(*results, state),
            in_specs=[vmem] * len(operands) + [in_vmem(state)],
            out_specs=(vmem, vmem, in_vmem(state)),
            scratch_shapes=scratch,
            input_output_aliases={len(operands) + i: 2 + i for i in range(len(jax.tree.leaves(state)))},
            compiler_params=params,
            name="late",
        )(*operands, made)
    else:
        electric, partial = pl.pallas_call(
            functools.partial(window_part, True, True, tx_count, ty_count),
            out_shape=results,
            in_specs=[vmem] * (8 + len(arrived)),
            out_specs=(vmem, vmem),
            scratch_shapes=[jax.tree.map(lambda v: pltpu.VMEM(v.shape, jnp.float32), state), *scratch],
            compiler_params=params,
            name="window",
        )(*first, *last, *arrived)
    final = pl.pallas_call(
        emit_kernel,
        out_shape=f32(1, 2, 3, ROWS, LINES * NZ),
        in_specs=[vmem],
        out_specs=vmem,
        compiler_params=pltpu.CompilerParams(vmem_limit_bytes=8 * 1024 * 1024),
        name="emit",
    )(electric)

    if lax.axis_size("wave") == 4:
        one, two, three = [
            lax.ppermute(partial, "wave", [(i, i ^ k) for i in range(4)]) for k in (1, 2, 3)
        ]
        gradient = (partial + one) + (two + three)
    else:
        gradient = lax.psum(partial, "wave")
    return gradient, final


def solution(mesh):
    placed = (
        P("wave", None, None, "tx", "ty"),
        P("wave", None, None, None),
        P("wave", None, None),
        P("tx", "ty"),
        P("tx", "ty"),
        P(),
        P(),
        P(),
    )
    return jax.shard_map(
        functools.partial(on_device, mesh.shape["tx"], mesh.shape["ty"]),
        mesh=mesh,
        in_specs=placed,
        out_specs=(P("tx", "ty"), P("wave", None, None, "tx", "ty")),
        check_vma=False,
    )
```
